32 devices in a mesh: groups: 2 (over x), row: 16 (over z, y, core).
Axes of the slice: x: 2, y: 2, z: 4, core: 2. Of those that a mesh axis runs over, the one named last changes fastest.
Arguments:
- right_sides: float32 [16, 65536], P(None, ('groups', 'row')), parts along dimension 1, may hold values from -80 to 80
- nugget: float32 [65536], P(('groups', 'row')), parts along dimension 0, may hold values from 0.25 to 2
- left_factors: bfloat16 [1024, 16, 2048], P(('groups', 'row')), parts along dimension 0, may hold values from -0.125 to 0.125
- right_factors: bfloat16 [1024, 16, 2048], P(('groups', 'row')), parts along dimension 0, may hold values from -0.125 to 0.125
- tile_column: int32 [1024, 1], P(('groups', 'row')), parts along dimension 0, may hold values from 0 to 15; in each aligned block of 32 rows (0 to 31, 32 to 63, ...) at most 4 rows name the same one
- live_slots: int32 [32], P(('groups', 'row')), parts along dimension 0, may hold values from 16 to 32, as said below
Outputs:
- solution: float32 [16, 65536], P(None, ('groups', 'row')), parts along dimension 1
- residual: float32 [16, 65536], P(None, ('groups', 'row')), parts along dimension 1
The draws below stay inside these ranges and needn't reach their ends.
There are 2 independent parts, one for each index of `groups`. The reference program is written for one: setup_inputs(seed, part) draws one part's arguments, and reference() takes and returns one part's arrays. A program takes and returns all parts, laid end to end along the dimension named above; each array names one. Nothing has to cross between parts.
Inputs may be any that keep to these rules, and one draw needn't show every extreme that they name: `tile_column`: among the 32 slots of one tile row at most 4 name the same tile column, a bound that some block reaches. `live_slots`: every tile row uses at least half of its 32 slots, and some tile row uses all of them.
All inputs are finite; a program needn't handle non-finite values.
Results may differ from the reference program's by a relative error of at most 0.0063.
Values may be sent and summed in bfloat16 or wider, within the bound.
No kernel may reach another device: no remote copies, remote signals or barrier semaphores. Data moves between devices by JAX's collectives and lax.ppermute only.
A program may use at most 64 MiB of HBM per device.

```python
import math
import jax
import jax.numpy as jnp
import numpy as np
from jax import lax

B = 2048
RB = 16
NRHS = 16
SLOTS = 32
ITERS = 2
NB = 16
LOCS = 32768
TILES = 512
CAP = 4


def draw_right_sides(key, part):
    key = jax.random.fold_in(key, 11)
    normal_key, scale_key = jax.random.split(key, 2)
    locations = B * NB
    position = jnp.arange(locations, dtype=jnp.float32) / locations
    rising = 1.0 + 2.0 * position
    spread = jnp.exp(jnp.log(10.0) * jax.random.uniform(scale_key, (locations,), jnp.float32)) / 3.0
    base_draw = jnp.clip(jax.random.normal(normal_key, (NRHS, locations), jnp.float32), -4.0, 4.0)
    return base_draw * (rising * spread)[None, :]


def draw_live_slots(key, part):
    key = jax.random.fold_in(key, 23)
    count_key, busy_key = jax.random.split(key, 2)
    counts = jax.random.randint(count_key, (NB,), SLOTS // 2, SLOTS + 1)
    busiest = jax.random.randint(busy_key, (), 0, NB)
    return jnp.where(jnp.arange(NB) == busiest, SLOTS, counts).astype(jnp.int32)


def block_scale(own_key, dims, pieces, low, top_value):
    loudness, own = 1.0, jax.random.fold_in(own_key, 6)
    for dim, shards_of in pieces:
        steps = jnp.exp(jax.random.uniform(jax.random.fold_in(own, dim), (shards_of,), jnp.float32, low / len(pieces), top_value / len(pieces)))
        loudness = loudness * jnp.repeat(steps, dims[dim] // shards_of).reshape([-1 if axis == dim else 1 for axis in range(len(dims))])
    return loudness


def deal_out(rng, own, number, rows, count, top, reach, skew):
    order = jax.random.permutation(rng, count)
    packed, common = load_shares(count, rows * top, reach, skew, True), load_shares(count, rows * top, reach, skew, False)
    places = jnp.arange(count)

    def named(tallies, offset_by):
        used = int((tallies > 0).sum())
        fixed = max(1, used // 4)
        moved = fixed + (places - fixed + offset_by * (used - fixed)) % max(1, count - fixed)
        return jnp.zeros((count,), jnp.int32).at[order[jnp.where(places < fixed, places, moved)]].set(jnp.asarray(tallies, jnp.int32))

    tallies = jnp.where(number % 4 == 0, named(packed, number // 4), named(common, number - number // 4 - 1))
    mixed = jax.random.permutation(jax.random.fold_in(own, 3), count)
    source_of, receiver = mixed[0:count // 2 * 2:2], mixed[1:count // 2 * 2:2]
    margin = jnp.minimum(tallies[source_of] - 1, reach - tallies[receiver]) // 2
    margin = jnp.where((source_of == order[0]) | (receiver == order[0]) | (tallies[receiver] == 0), 0, jnp.maximum(margin, 0))
    moved = jax.random.randint(jax.random.fold_in(own, 4), (count // 2,), 0, 1 << 20) % (margin + 1)
    tallies = tallies.at[source_of].add(-moved).at[receiver].add(moved)
    labels = jnp.searchsorted(jnp.cumsum(tallies), jnp.arange(rows * top), side="right").astype(jnp.int32)
    table = labels.reshape(top, rows).T
    table = table[jax.random.permutation(jax.random.fold_in(own, 1), rows)]
    offset_by = jax.random.randint(jax.random.fold_in(own, 2), (rows, 1), 0, top)
    return jnp.take_along_axis(table, (jnp.arange(top)[None, :] + offset_by) % top, axis=1)


def load_shares(count, total, bound, lean, full):
    weights = [(1 << 20) // math.isqrt(standing ** lean) + 1 for standing in range(1, count + 1)]
    largest = bound if full else min(bound, max(-(-total // count), total * weights[0] // sum(weights)))
    least = 1 if total - largest >= count - 1 else 0
    given, surplus = [largest] + [least] * (count - 1), total - largest - least * (count - 1)
    while surplus > 0:
        free = [i for i in range(1, count) if given[i] < largest] or [i for i in range(1, count) if given[i] < bound]
        mass, remaining = sum([weights[i] for i in free]), surplus
        for i in free:
            extra = min(bound - given[i], max(1, remaining * weights[i] // mass), surplus)
            given[i] = given[i] + extra
            surplus = surplus - extra
    return np.array(given)


def normal_values(key, extent, scale, bound, cuts=(), held_as=jnp.bfloat16):
    entries = scale * jax.random.normal(key, extent, jnp.float32)
    if cuts:
        entries = entries * block_scale(key, extent, cuts, -0.22, 0.18)
    return jnp.clip(entries, -bound, bound).astype(held_as)


def setup_inputs(seed: int = 0, part: int = 0) -> dict:
    seeds = jax.random.split(jax.random.key(seed), 7)
    own_keys = jax.random.split(jax.random.fold_in(seeds[6], part), 7)
    right_sides = draw_right_sides(jax.random.fold_in(jax.random.fold_in(seeds[6], part), 71), part)
    nugget = jnp.clip(jnp.exp(math.log(2.0) - 2.0794415 * jax.random.uniform(own_keys[1], (LOCS,), jnp.float32) ** block_scale(own_keys[1], (LOCS,), ((0, 16),), -0.2, 0.2)), 0.25, 2.0)
    left_factors = normal_values(own_keys[2], (TILES, RB, B), B ** -0.5, 0.125, ((0, 16),))
    right_factors = normal_values(own_keys[3], (TILES, RB, B), B ** -0.5, 0.125, ((0, 16),))
    tile_column_keys = jax.random.split(jax.random.fold_in(own_keys[4], 1), TILES // SLOTS)
    tile_column_turns = jax.random.permutation(jax.random.fold_in(own_keys[4], 3), TILES // SLOTS)
    tile_column = jax.vmap(lambda own, number: deal_out(jax.random.fold_in(own_keys[4], 2), own, number, SLOTS, NB, 1, CAP, 1))(tile_column_keys, tile_column_turns).reshape((TILES, 1))
    live_slots = draw_live_slots(jax.random.fold_in(jax.random.fold_in(seeds[6], part), 71), part)
    return dict(right_sides=right_sides, nugget=nugget, left_factors=left_factors, right_factors=right_factors, tile_column=tile_column, live_slots=live_slots)


def gram_solve(matrix, target):
    factor = jnp.linalg.cholesky(matrix)
    return jax.scipy.linalg.cho_solve((factor, True), target)

def pair_gram(former, latter):
    return jnp.dot(former, latter.T, precision=lax.Precision.HIGHEST)

def low_rank(direction_low, left_factors, right_factors, tile_column, live_slots):
    exact = lax.Precision.HIGHEST
    panels = direction_low.astype(jnp.float32).reshape(NRHS, NB, B)
    columns = tile_column[:, 0].astype(jnp.int32)
    slot_index = jnp.arange(SLOTS, dtype=jnp.int32)

    def device_term(spread, device):
        offset = (device * SLOTS).astype(jnp.int32)
        left_block = lax.dynamic_slice_in_dim(left_factors, offset, SLOTS, 0).astype(jnp.float32)
        right_block = lax.dynamic_slice_in_dim(right_factors, offset, SLOTS, 0).astype(jnp.float32)
        column_block = lax.dynamic_slice_in_dim(columns, offset, SLOTS, 0)
        own_panel = lax.dynamic_index_in_dim(panels, device, 1, keepdims=False)
        far_panels = jnp.take(panels, column_block, axis=1)
        projection = jnp.einsum('krb,nb->krn', left_block, own_panel, precision=exact)
        projection = projection + jnp.einsum('krb,nkb->krn', right_block, far_panels, precision=exact)
        live_mask = (slot_index < live_slots[device]).astype(jnp.float32)
        rounded = lax.optimization_barrier((projection * live_mask[:, None, None]).astype(jnp.bfloat16))
        projection_low = rounded.astype(jnp.float32)
        moved = jnp.einsum('krb,krn->nkb', right_block, projection_low, precision=exact)
        spread = spread.at[:, column_block].add(moved)
        own_term = jnp.einsum('krb,krn->nb', left_block, projection_low, precision=exact)
        spread = spread.at[:, device].add(own_term)
        return (spread, None)
    spread, unused = lax.scan(device_term, jnp.zeros((NRHS, NB, B), jnp.float32), jnp.arange(NB, dtype=jnp.int32))
    return spread.reshape(NRHS, NB * B)

def reference(right_sides, nugget, left_factors, right_factors, tile_column, live_slots):
    exact = lax.Precision.HIGHEST
    solution = jnp.zeros_like(right_sides)
    residual = right_sides
    direction = right_sides
    res_gram = pair_gram(residual, residual)
    for iteration in range(ITERS):
        direction_low = direction.astype(jnp.bfloat16)
        applied = nugget[None, :] * direction + low_rank(direction_low, left_factors, right_factors, tile_column, live_slots)
        curvature = pair_gram(direction, applied)
        step_size = gram_solve(curvature, res_gram)
        solution = solution + jnp.dot(step_size.T, direction, precision=exact)
        residual = residual - jnp.dot(step_size.T, applied, precision=exact)
        if iteration + 1 < ITERS:
            next_gram = pair_gram(residual, residual)
            update_mix = gram_solve(res_gram, next_gram)
            direction = residual + jnp.dot(update_mix.T, direction, precision=exact)
            res_gram = next_gram
    return (solution, residual)
```

```python
import functools

import jax
import jax.numpy as jnp
from jax import lax
from jax.experimental import pallas as pl
from jax.experimental.pallas import tpu as pltpu
from jax.sharding import PartitionSpec as P

ITERS = 2
LANES = 128
F32 = jnp.float32
BF16 = jnp.bfloat16
EXACT = lax.Precision.HIGHEST
NN = (((1,), (0,)), ((), ()))
NT = (((1,), (1,)), ((), ()))


def lane_group(shape, rhs):
    return lax.broadcasted_iota(jnp.int32, shape, len(shape) - 1) // rhs


def encode(small, rhs):
    group = lane_group(small.shape, rhs)
    high = small.astype(BF16).astype(F32)
    rest = small - high
    middle = rest.astype(BF16).astype(F32)
    low = rest - middle
    picked = jnp.where(group == 0, high, jnp.where(group == 1, middle, jnp.where(group == 2, low, 0.0)))
    return picked.astype(BF16)


def fold(wide, rhs):
    shift = LANES // 2
    while shift >= rhs:
        wide = wide + pltpu.roll(wide, shift, 1)
        shift //= 2
    return wide


def repeat_rows(block, rhs):
    return jnp.concatenate([block] * (LANES // rhs), axis=0)


def right_divide(top, bottom, rhs):
    both = jnp.concatenate([top, bottom], axis=0)
    lane = lax.broadcasted_iota(jnp.int32, both.shape, 1) % rhs
    for k in range(rhs):
        row = both[k : k + 1, :]
        column = both[:, k : k + 1]
        scaled = column * (1.0 / both[k : k + 1, k : k + 1])
        both = jnp.where(lane == k, scaled, both - scaled * row)
    return both[rhs:, :]


def left_multiply(square, block, rhs):
    return lax.dot_general(square[:, :rhs], block, NN, precision=EXACT, preferred_element_type=F32)


def flat(ref, chunks):
    return jnp.concatenate([ref[c] for c in range(chunks)], axis=1)


def open_kernel(rhs, chunks, right_ref, message_ref):
    block = right_ref[...]
    for c in range(chunks):
        message_ref[c] = block[:, c * LANES : (c + 1) * LANES].astype(BF16)
    gram = lax.dot_general(block, repeat_rows(block, rhs), NT, precision=EXACT, preferred_element_type=F32)
    message_ref[chunks] = encode(gram, rhs)


def gathered_gram(held_ref, other_ref, chunks, rhs):
    half = held_ref.shape[0]
    total = held_ref[0, chunks].astype(F32)
    for i in range(1, half):
        total = total + held_ref[i, chunks].astype(F32)
    for i in range(half):
        total = total + other_ref[i, chunks].astype(F32)
    return fold(total, rhs)


def projections(held_ref, other_ref, left_ref, right_ref, slot_ref, panel_ref, rhs, chunks):
    half = held_ref.shape[0]
    for i in range(half):
        for c in range(chunks):
            at = slice(c * LANES, (c + 1) * LANES)
            panel_ref[i * rhs : (i + 1) * rhs, at] = held_ref[i, c]
            panel_ref[(half + i) * rhs : (half + i + 1) * rhs, at] = other_ref[i, c]
    far = lax.dot_general(right_ref[...], panel_ref[...], NT, preferred_element_type=F32)
    own = repeat_rows(panel_ref[:rhs, :], rhs)
    near = lax.dot_general(left_ref[...], own, NT, preferred_element_type=F32)
    slot = slot_ref[...]
    group = lane_group(slot.shape, rhs)
    total = jnp.zeros(slot.shape, F32)
    per = LANES // rhs
    for j in range(2 * half // per):
        total = total + jnp.where(slot == group + j * per, far[:, j * LANES : (j + 1) * LANES], 0.0)
    return near + fold(total, rhs)


def spread_out(projected, left_ref, right_ref, slot_ref, send_ref, keep_ref, own_ref, rhs, chunks):
    slot = slot_ref[...]
    group = lane_group(slot.shape, rhs)
    per = LANES // rhs
    panels = 2 * keep_ref.shape[0] // chunks
    turned = [
        jnp.where(slot == group + j * per, projected, 0.0).T.astype(BF16) for j in range(panels // per)
    ]
    turned = jnp.concatenate(turned, axis=0)
    own_turned = projected.T[:rhs].astype(BF16)
    own_ref[...] = lax.dot_general(own_turned, left_ref[...], NN, preferred_element_type=F32)
    step = 2 * LANES
    for block in range(chunks // 2):
        at = slice(block * step, (block + 1) * step)
        moved = lax.dot_general(turned, right_ref[:, at], NN, preferred_element_type=F32)
        for i in range(panels):
            for b in range(2):
                piece = moved[i * rhs : (i + 1) * rhs, b * LANES : (b + 1) * LANES]
                c = 2 * block + b
                if i < panels // 2:
                    keep_ref[i * chunks + c] = piece
                else:
                    send_ref[(i - panels // 2) * chunks + c] = piece.astype(BF16)


def curvature_part(direction, nugget, projected, rhs):
    rounded = projected.astype(BF16).astype(F32)
    weighted = lax.dot_general(
        direction * nugget, repeat_rows(direction, rhs), NT, precision=EXACT, preferred_element_type=F32
    )
    first = lax.dot_general(projected.T[:rhs], rounded, NN, precision=EXACT, preferred_element_type=F32)
    second = lax.dot_general(rounded.T[:rhs], projected, NN, precision=EXACT, preferred_element_type=F32)
    return weighted + 0.5 * (first + second)


def first_kernel(
    rhs, chunks, direction_ref, nugget_ref, held_ref, other_ref, left_ref, right_ref, slot_ref,
    send_ref, keep_ref, own_ref, part_ref, gram_ref, projected_ref, panel_ref,
):
    gram_ref[...] = gathered_gram(held_ref, other_ref, chunks, rhs)
    projected = projections(held_ref, other_ref, left_ref, right_ref, slot_ref, panel_ref, rhs, chunks)
    projected = jnp.where(slot_ref[...] >= 0, projected, 0.0)
    projected_ref[...] = projected
    spread_out(projected, left_ref, right_ref, slot_ref, send_ref, keep_ref, own_ref, rhs, chunks)
    part = curvature_part(direction_ref[...], nugget_ref[...], projected, rhs)
    part_ref[...] = part
    send_ref[send_ref.shape[0] - 1] = encode(part, rhs)


def halve_kernel(rhs, keep_ref, part_ref, got_ref, *out):
    *sends, kept_ref, total_ref = out
    count = kept_ref.shape[0]
    total = part_ref[...] + fold(got_ref[got_ref.shape[0] - 1].astype(F32), rhs)
    total_ref[...] = total
    code = encode(total, rhs)
    kept_ref[...] = keep_ref[:count] + got_ref[:count].astype(F32)
    at = count
    for send in sends:
        size = send.shape[0] - 1
        send[:size] = (keep_ref[at : at + size] + got_ref[at : at + size].astype(F32)).astype(BF16)
        send[size] = code
        at += size


def gathered_product(keep_ref, own_ref, part_ref, got, direction, nugget, rhs, chunks):
    total = keep_ref[...]
    code = jnp.zeros(part_ref.shape, F32)
    for ref in got:
        total = total + ref[:chunks].astype(F32)
        code = code + ref[chunks].astype(F32)
    applied = nugget * direction + own_ref[...] + jnp.concatenate([total[c] for c in range(chunks)], axis=1)
    return applied, part_ref[...] + fold(code, rhs)


def middle_kernel(rhs, chunks, count, direction_ref, nugget_ref, own_ref, keep_ref, part_ref, gram_ref, *rest):
    got, (message_ref, residual_ref, solution_ref) = rest[:count], rest[count:]
    direction = direction_ref[...]
    applied, curvature = gathered_product(
        keep_ref, own_ref, part_ref, got, direction, nugget_ref[...], rhs, chunks
    )
    step = right_divide(curvature, gram_ref[...], rhs)
    residual = direction - left_multiply(step, applied, rhs)
    residual_ref[...] = residual
    solution_ref[...] = left_multiply(step, direction, rhs)
    for c in range(chunks):
        message_ref[c] = residual[:, c * LANES : (c + 1) * LANES].astype(BF16)
    gram = lax.dot_general(residual, repeat_rows(residual, rhs), NT, precision=EXACT, preferred_element_type=F32)
    message_ref[chunks] = encode(gram, rhs)


def second_kernel(
    rhs, chunks, right_side_ref, residual_ref, nugget_ref, gram_ref, before_ref, held_ref, other_ref,
    left_ref, right_ref, slot_ref,
    send_ref, keep_ref, own_ref, part_ref, next_gram_ref, direction_ref, panel_ref,
):
    next_gram = gathered_gram(held_ref, other_ref, chunks, rhs)
    next_gram_ref[...] = next_gram
    mix = right_divide(gram_ref[...], next_gram, rhs)
    direction = residual_ref[...] + left_multiply(mix, right_side_ref[...], rhs)
    direction_ref[...] = direction
    projected = projections(held_ref, other_ref, left_ref, right_ref, slot_ref, panel_ref, rhs, chunks)
    mixing = repeat_rows(jnp.where(lane_group(mix.shape, rhs) == 0, mix, 0.0), rhs)
    projected = projected + lax.dot_general(
        before_ref[...], mixing, NT, precision=EXACT, preferred_element_type=F32
    )
    projected = jnp.where(slot_ref[...] >= 0, projected, 0.0)
    spread_out(projected, left_ref, right_ref, slot_ref, send_ref, keep_ref, own_ref, rhs, chunks)
    part = curvature_part(direction, nugget_ref[...], projected, rhs)
    part_ref[...] = part
    send_ref[send_ref.shape[0] - 1] = encode(part, rhs)


def last_kernel(rhs, chunks, count, direction_ref, nugget_ref, own_ref, keep_ref, part_ref, gram_ref, *rest):
    got, (residual_ref, solution_ref, out_solution_ref, out_residual_ref) = rest[:count], rest[count:]
    direction = direction_ref[...]
    applied, curvature = gathered_product(
        keep_ref, own_ref, part_ref, got, direction, nugget_ref[...], rhs, chunks
    )
    step = right_divide(curvature, gram_ref[...], rhs)
    out_solution_ref[...] = solution_ref[...] + left_multiply(step, direction, rhs)
    out_residual_ref[...] = residual_ref[...] - left_multiply(step, applied, rhs)


def call(kernel, outs, *args, scratch=()):
    whole = pl.BlockSpec(memory_space=pltpu.VMEM)
    return pl.pallas_call(
        kernel,
        out_shape=[jax.ShapeDtypeStruct(shape, dtype) for shape, dtype in outs],
        in_specs=[whole] * len(args),
        out_specs=[whole] * len(outs),
        scratch_shapes=list(scratch),
        compiler_params=pltpu.CompilerParams(vmem_limit_bytes=40 * 1024 * 1024),
    )(*args)


def shards(right_sides, nugget, left_factors, right_factors, tile_column, live_slots):
    devices = lax.axis_size("row")
    bits = devices.bit_length() - 1
    low_bits = bits - 2
    slots, rank, width = left_factors.shape
    rhs = right_sides.shape[0]
    chunks = width // LANES
    half = devices // 2

    def swap(array, offset):
        return lax.ppermute(array, "row", [(i, i ^ offset) for i in range(devices)])

    place = tile_column[:, 0] ^ lax.axis_index("row")
    ordered = place >> low_bits
    for b in range(low_bits):
        ordered = ordered | (((place >> b) & 1) << (bits - 1 - b))
    ordered = jnp.where(jnp.arange(slots, dtype=jnp.int32) < live_slots[0], ordered, -1)
    slot = jnp.broadcast_to(ordered[:, None, None], (slots, rank, LANES)).reshape(slots * rank, LANES)

    left = left_factors.reshape(slots * rank, width)
    right = right_factors.reshape(slots * rank, width)
    nugget = nugget[None, :]

    def gather(message):
        held = jnp.stack([message] + [swap(message, k << low_bits) for k in range(1, 4)])
        for b in range(low_bits - 1, 0, -1):
            held = jnp.concatenate([held, swap(held, 1 << b)])
        return held, swap(held, 1)

    small = (rhs, LANES)
    panel = (rhs, width)
    message_shape = ((chunks + 1, rhs, LANES), BF16)

    def reduced(send, keep, part):
        got = swap(send, 1)
        count = half
        for b in range(1, low_bits):
            count //= 2
            outs = [
                ((count * chunks + 1, rhs, LANES), BF16), ((count * chunks, rhs, LANES), F32), (small, F32)
            ]
            send, keep, part = call(functools.partial(halve_kernel, rhs), outs, keep, part, got)
            got = swap(send, 1 << b)
        outs = [message_shape] * 3 + [((chunks, rhs, LANES), F32), (small, F32)]
        *sends, keep, part = call(functools.partial(halve_kernel, rhs), outs, keep, part, got)
        return keep, part, [swap(sends[k - 1], k << low_bits) for k in range(1, 4)]

    spread_outs = [
        ((half * chunks + 1, rhs, LANES), BF16),
        ((half * chunks, rhs, LANES), F32),
        (panel, F32),
        (small, F32),
        (small, F32),
    ]
    scratch = [pltpu.VMEM((devices * rhs, width), BF16)]

    (message,) = call(functools.partial(open_kernel, rhs, chunks), [message_shape], right_sides)
    held, other = gather(message)
    send, keep, own, part, gram, before = call(
        functools.partial(first_kernel, rhs, chunks),
        spread_outs + [((slots * rank, LANES), F32)],
        right_sides, nugget, held, other, left, right, slot,
        scratch=scratch,
    )
    keep, part, got = reduced(send, keep, part)
    message, residual, solution = call(
        functools.partial(middle_kernel, rhs, chunks, len(got)),
        [message_shape, (panel, F32), (panel, F32)],
        right_sides, nugget, own, keep, part, gram, *got,
    )
    held, other = gather(message)
    send, keep, own, part, next_gram, direction = call(
        functools.partial(second_kernel, rhs, chunks),
        spread_outs + [(panel, F32)],
        right_sides, residual, nugget, gram, before, held, other, left, right, slot,
        scratch=scratch,
    )
    keep, part, got = reduced(send, keep, part)
    return tuple(
        call(
            functools.partial(last_kernel, rhs, chunks, len(got)),
            [(panel, F32), (panel, F32)],
            direction, nugget, own, keep, part, next_gram, *got, residual, solution,
        )
    )


def solution(mesh):
    return jax.shard_map(
        shards,
        mesh=mesh,
        in_specs=(
            P(None, ("groups", "row")),
            P(("groups", "row")),
            P(("groups", "row"), None, None),
            P(("groups", "row"), None, None),
            P(("groups", "row"), None),
            P(("groups", "row")),
        ),
        out_specs=(P(None, ("groups", "row")), P(None, ("groups", "row"))),
        check_vma=False,
    )
```

```python
import functools

import jax
import jax.numpy as jnp
from jax import lax
from jax.experimental import pallas as pl
from jax.experimental.pallas import tpu as pltpu
from jax.sharding import PartitionSpec as P

LANES = 128
F32 = jnp.float32
BF16 = jnp.bfloat16
EXACT = lax.Precision.HIGHEST
NN = (((1,), (0,)), ((), ()))
NT = (((1,), (1,)), ((), ()))


def lanes_of(block):
    return lax.broadcasted_iota(jnp.int32, block.shape, len(block.shape) - 1)


def pair_of(first, second, rhs):
    parts = [first] if second is None else [first, second]
    rest = jnp.zeros((rhs, LANES - rhs * len(parts)), F32)
    return jnp.concatenate(parts + [rest], axis=1)


def encode(pair, rhs):
    high = pair.astype(BF16).astype(F32)
    rest = pair - high
    middle = rest.astype(BF16).astype(F32)
    low = rest - middle
    return (high + pltpu.roll(middle, 2 * rhs, 1) + pltpu.roll(low, 4 * rhs, 1)).astype(BF16)


def decode(code, rhs):
    total = code + pltpu.roll(code, LANES - 2 * rhs, 1) + pltpu.roll(code, LANES - 4 * rhs, 1)
    return jnp.where(lanes_of(total) < 2 * rhs, total, 0.0)


def second_of(pair, rhs):
    return pltpu.roll(pair, LANES - rhs, 1)


def right_divide(top, bottom, rhs):
    both = jnp.concatenate([top, bottom], axis=0)
    lane = lanes_of(both)
    both = jnp.where(lane < rhs, both, 0.0)
    one = lane[:1]
    for k in range(0, rhs, 2):
        col_0 = jnp.broadcast_to(both[:, k : k + 1], both.shape)
        col_1 = jnp.broadcast_to(both[:, k + 1 : k + 2], both.shape)
        a, b = col_0[k : k + 1], col_1[k : k + 1]
        c, d = col_0[k + 1 : k + 2], col_1[k + 1 : k + 2]
        inverse = 1.0 / (a * d - b * c)
        row_0 = jnp.where(one == k, -1.0, jnp.where(one == k + 1, 0.0, both[k : k + 1]))
        row_1 = jnp.where(one == k, 0.0, jnp.where(one == k + 1, -1.0, both[k + 1 : k + 2]))
        new_0 = (d * row_0 - b * row_1) * inverse
        new_1 = (a * row_1 - c * row_0) * inverse
        both = jnp.where((lane == k) | (lane == k + 1), 0.0, both) - col_0 * new_0 - col_1 * new_1
    return both[rhs:, :]


def left_multiply(square, block, rhs):
    return lax.dot_general(square[:, :rhs], block, NN, precision=EXACT, preferred_element_type=F32)


def gram(former, latter):
    return lax.dot_general(former, latter, NT, precision=EXACT, preferred_element_type=F32)


def rows_of(ref, chunks):
    panels, _, rhs, lanes = ref.shape
    return jnp.concatenate([ref[:, c].reshape(panels * rhs, lanes) for c in range(chunks)], axis=1)


def store_message(message_ref, block, rhs, at=0):
    for c in range(block.shape[1] // LANES):
        message_ref[at + c] = block[:, c * LANES : (c + 1) * LANES].astype(message_ref.dtype)


def far_terms(total, panels, right_ref, slot, bases, rhs, chunks):
    rows = jnp.concatenate([rows_of(ref, chunks) for ref in panels], axis=0)
    far = lax.dot_general(rows, right_ref[...], NT, preferred_element_type=F32)
    at = 0
    for base, ref in zip(bases, panels):
        for i in range(ref.shape[0]):
            total = total + jnp.where(slot == base + i, far[at : at + rhs], 0.0)
            at += rhs
    return total


def codes_of(panels_ref, chunks):
    count, held = panels_ref.shape[:2]
    code = jnp.zeros(panels_ref.shape[2:], F32)
    for i in range(count if held > chunks else 0):
        code = code + panels_ref[i, chunks].astype(F32)
    return code


def spread_terms(projected, right_ref, slot, base, out_ref, count, rhs, chunks, extra=None):
    masked = [jnp.where(slot == base + i, projected, 0.0).astype(BF16) for i in range(count)]
    masked = jnp.concatenate(masked, axis=0)
    step = 2 * LANES
    for block in range(chunks // 2):
        at = slice(block * step, (block + 1) * step)
        moved = lax.dot_general(masked, right_ref[:, at], NN, preferred_element_type=F32)
        for i in range(count):
            for b in range(2):
                piece = moved[i * rhs : (i + 1) * rhs, b * LANES : (b + 1) * LANES]
                if i == 0 and extra is not None:
                    place = block * step + b * LANES
                    piece = piece + extra[:, place : place + LANES]
                out_ref[i * chunks + 2 * block + b] = piece.astype(out_ref.dtype)


def open_kernel(rhs, right_side_hbm, message_ref, right_side_ref, sem):
    copy = pltpu.make_async_copy(right_side_hbm, right_side_ref, sem)
    copy.start()
    copy.wait()
    store_message(message_ref, right_side_ref[...], rhs)


def load_kernel(
    rhs, rank, place_of, own_ref, column_ref, live_ref, nugget_hbm, left_hbm, right_hbm,
    nugget_ref, left_ref, right_ref, slot_ref, near_ref, pair_ref, nugget_sem, left_sem, right_sem,
):
    nugget_copy = pltpu.make_async_copy(nugget_hbm, nugget_ref, nugget_sem)
    left_copy = pltpu.make_async_copy(left_hbm, left_ref, left_sem)
    right_copy = pltpu.make_async_copy(right_hbm, right_ref, right_sem)
    nugget_copy.start()
    left_copy.start()
    right_copy.start()
    me = lax.axis_index("row")
    slot_of = lax.broadcasted_iota(jnp.int32, (1, slot_ref.shape[1]), 1) // rank
    slot = jnp.full(slot_of.shape, -1, jnp.int32)
    for s in range(column_ref.shape[0]):
        place = jnp.where(s < live_ref[0], place_of(column_ref[s] ^ me), -1)
        slot = jnp.where(slot_of == s, place, slot)
    slot_ref[...] = jnp.broadcast_to(slot, slot_ref.shape)
    own = own_ref[...]
    nugget_copy.wait()
    pair_ref[...] = pair_of(gram(own * nugget_ref[...], own), gram(own, own), rhs)
    left_copy.wait()
    near_ref[...] = lax.dot_general(own.astype(BF16), left_ref[...], NT, preferred_element_type=F32)
    right_copy.wait()


def near_kernel(own_ref, left_ref, near_ref):
    near_ref[...] = lax.dot_general(own_ref[...].astype(BF16), left_ref[...], NT, preferred_element_type=F32)


def add_kernel(rhs, chunks, bases, first, right_ref, slot_ref, *rest):
    panels, (part_ref, code_ref, out_ref, code_out_ref) = rest[: len(bases)], rest[len(bases) :]
    slot = slot_ref[...]
    total, code = part_ref[...], code_ref[...]
    if first:
        total, code = jnp.where(slot >= 0, total, 0.0), jnp.zeros(code.shape, F32)
    total = far_terms(total, panels, right_ref, slot, bases, rhs, chunks)
    for ref in panels:
        code = code + codes_of(ref, chunks)
    out_ref[...] = total
    code_out_ref[...] = code


def symmetric_product(projected):
    rounded = projected.astype(BF16).astype(F32)
    first = gram(projected, rounded)
    return 0.5 * (first + first.T)


def first_kernel(
    rhs, chunks, base, panels_ref, right_ref, slot_ref, before_ref, pair_ref,
    send_ref, total_ref, projected_ref,
):
    slot = slot_ref[...]
    projected = far_terms(before_ref[...], [panels_ref], right_ref, slot, [base], rhs, chunks)
    projected_ref[...] = projected
    total = pair_ref[...] + pair_of(symmetric_product(projected), None, rhs)
    total_ref[...] = total
    count = send_ref.shape[0] // chunks
    spread_terms(projected, right_ref, slot, base, send_ref, count, rhs, chunks)
    send_ref[count * chunks] = encode(total, rhs)


def second_kernel(
    rhs, chunks, base, panels_ref, right_ref, slot_ref, before_ref, code_ref,
    right_side_ref, residual_ref, nugget_ref, gram_ref, earlier_ref,
    send_ref, total_ref, projected_ref, direction_ref, next_gram_ref,
):
    slot = slot_ref[...]
    next_gram = decode(code_ref[...] + codes_of(panels_ref, chunks), rhs)
    next_gram_ref[...] = next_gram
    mix = right_divide(gram_ref[...], next_gram, rhs)
    projected = far_terms(before_ref[...], [panels_ref], right_ref, slot, [base], rhs, chunks)
    projected = projected + left_multiply(mix, earlier_ref[...], rhs)
    projected_ref[...] = projected
    direction = residual_ref[...] + left_multiply(mix, right_side_ref[...], rhs)
    direction_ref[...] = direction
    total = pair_of(gram(direction * nugget_ref[...], direction) + symmetric_product(projected), None, rhs)
    total_ref[...] = total
    count = send_ref.shape[0] // chunks
    spread_terms(projected, right_ref, slot, base, send_ref, count, rhs, chunks)
    send_ref[count * chunks] = encode(total, rhs)


def spread_kernel(rhs, chunks, base, projected_ref, right_ref, slot_ref, out_ref):
    spread_terms(
        projected_ref[...], right_ref, slot_ref[...], base, out_ref, out_ref.shape[0] // chunks, rhs, chunks
    )


def spread_own_kernel(rhs, chunks, base, projected_ref, left_ref, right_ref, slot_ref, out_ref):
    projected = projected_ref[...]
    own = lax.dot_general(projected.astype(BF16), left_ref[...], NN, preferred_element_type=F32)
    spread_terms(
        projected, right_ref, slot_ref[...], base, out_ref, out_ref.shape[0] // chunks, rhs, chunks, own
    )


def join_kernel(keep_ref, got_ref, sum_ref):
    sum_ref[...] = keep_ref[...] + got_ref[...].astype(F32)


def split_kernel(rhs, keep_ref, pair_ref, got_ref, total_ref, *sends):
    total = pair_ref[...] + decode(got_ref[got_ref.shape[0] - 1].astype(F32), rhs)
    total_ref[...] = total
    end = keep_ref.shape[0]
    for i, send in enumerate(sends):
        size = send.shape[0] - (1 if i == 0 else 0)
        send[:size] = (keep_ref[end - size : end] + got_ref[end - size : end].astype(F32)).astype(BF16)
        end -= size
    sends[0][sends[0].shape[0] - 1] = encode(total, rhs)


def part_kernel(rhs, at, stay, keep_ref, pair_ref, got_ref, *out):
    chunks = got_ref.shape[0]
    total = pair_ref[...]
    out = list(out)
    if chunks % 2:
        chunks -= 1
        total = total + decode(got_ref[chunks].astype(F32), rhs)
        out.pop(0)[...] = total
    if stay:
        out.pop(0)[...] = keep_ref[at : at + stay] + got_ref[:stay].astype(F32)
    if chunks > stay:
        (send,) = out
        send[: chunks - stay] = (keep_ref[at + stay : at + chunks] + got_ref[stay:chunks].astype(F32)).astype(
            BF16
        )
        send[chunks - stay] = encode(total, rhs)


def message_kernel(rhs, panel_ref, pair_ref, message_ref):
    message_ref[: panel_ref.shape[0]] = panel_ref[...].astype(BF16)
    message_ref[panel_ref.shape[0]] = encode(pair_ref[...], rhs)


def code_kernel(rhs, pair_ref, code_ref):
    code_ref[...] = encode(pair_ref[...], rhs)


def pair_kernel(rhs, pair_ref, got_ref, total_ref):
    total_ref[...] = pair_ref[...] + decode(got_ref[...].astype(F32), rhs)


def gathered_product(keep_ref, pair_ref, got, direction, nugget, rhs, chunks):
    total = keep_ref[...]
    code = jnp.zeros(pair_ref.shape, F32)
    for ref in got:
        total = total + ref[:chunks].astype(F32)
        code = code + ref[chunks].astype(F32)
    applied = nugget * direction + jnp.concatenate([total[c] for c in range(chunks)], axis=1)
    return applied, pair_ref[...] + decode(code, rhs)


def middle_kernel(rhs, chunks, direction_ref, nugget_ref, keep_ref, pair_ref, *rest):
    got, (message_ref, residual_ref, solution_ref, gram_ref) = rest[:-4], rest[-4:]
    direction = direction_ref[...]
    applied, pair = gathered_product(keep_ref, pair_ref, got, direction, nugget_ref[...], rhs, chunks)
    first_gram = second_of(pair, rhs)
    gram_ref[...] = first_gram
    step = right_divide(pair, first_gram, rhs)
    residual = direction - left_multiply(step, applied, rhs)
    residual_ref[...] = residual
    store_message(message_ref, residual, rhs)
    message_ref[chunks] = encode(pair_of(gram(residual, residual), None, rhs), rhs)
    solution_ref[...] = left_multiply(step, direction, rhs)


def last_kernel(rhs, chunks, direction_ref, nugget_ref, keep_ref, pair_ref, gram_ref, *rest):
    got, (residual_ref, solution_ref, out_solution_ref, out_residual_ref) = rest[:-4], rest[-4:]
    direction = direction_ref[...]
    applied, pair = gathered_product(keep_ref, pair_ref, got, direction, nugget_ref[...], rhs, chunks)
    step = right_divide(pair, gram_ref[...], rhs)
    out_solution_ref[...] = solution_ref[...] + left_multiply(step, direction, rhs)
    out_residual_ref[...] = residual_ref[...] - left_multiply(step, applied, rhs)


def call(kernel, outs, *args, far=(), scalars=(), fixed=(), scratch=()):
    whole = pl.BlockSpec(memory_space=pltpu.VMEM)
    spaces = {i: pltpu.HBM for i in far} | {i: pltpu.SMEM for i in scalars}
    return pl.pallas_call(
        kernel,
        out_shape=[
            pltpu.VMEM(shape, dtype) if i in fixed else jax.ShapeDtypeStruct(shape, dtype)
            for i, (shape, dtype) in enumerate(outs)
        ],
        in_specs=[pl.BlockSpec(memory_space=spaces[i]) if i in spaces else whole for i in range(len(args))],
        out_specs=[whole] * len(outs),
        scratch_shapes=list(scratch),
        cost_estimate=pl.CostEstimate(flops=0, bytes_accessed=0, transcendentals=0),
        compiler_params=pltpu.CompilerParams(vmem_limit_bytes=32 * 1024 * 1024),
    )(*args)


def after(value, *others):
    return lax.optimization_barrier((value, *others))[0]


def shards(right_sides, nugget, left_factors, right_factors, tile_column, live_slots):
    devices = lax.axis_size("row")
    bits = devices.bit_length() - 1
    low_bits = bits - 2
    slots, rank, width = left_factors.shape
    rhs = right_sides.shape[0]
    chunks = width // LANES
    part = functools.partial

    def swap(array, offset):
        return lax.ppermute(array, "row", [(i, i ^ offset) for i in range(devices)])

    groups = []
    for k in range(4):
        group = [k << low_bits]
        for b in range(low_bits - 1, 1, -1):
            group = group + [o | (1 << b) for o in group]
        groups.append(group)
    m = len(groups[0])
    held_offsets = sum(groups, [])
    late_offsets = [o | 2 for o in held_offsets]
    offsets = held_offsets + [o | 1 for o in held_offsets] + late_offsets + [o | 1 for o in late_offsets]
    held, held_other, late, late_other = (4 * m * i for i in range(4))

    def place_of(offset):
        place = (offset >> low_bits) * m
        for b in range(low_bits - 1, 1, -1):
            place = place + (((offset >> b) & 1) << (low_bits - 1 - b))
        return place + (offset & 1) * held_other + ((offset >> 1) & 1) * late

    assert [place_of(o) for o in offsets] == list(range(devices))

    small = ((rhs, LANES), F32)
    panel = ((rhs, width), F32)
    row_block = ((rhs, slots * rank), F32)

    def plain(count):
        return ((count * chunks, rhs, LANES), BF16)

    def coded(count):
        return ((count * chunks + 1, rhs, LANES), BF16)

    def kept(count):
        return ((count * chunks, rhs, LANES), F32)

    def gather(message, early):
        mine = [message[None]] + [swap(message, k << low_bits)[None] for k in range(1, 4)]
        near, code, slot, right = early
        mine[1] = after(mine[1], near)
        for b in range(low_bits - 1, 1, -1):
            mine = [jnp.concatenate([g, swap(g, 1 << b)]) for g in mine]
        beside = [swap(jnp.concatenate(mine[i : i + 2]), 2) for i in (0, 2)]
        own_core = jnp.concatenate(mine)
        other_core = swap(own_core, 1)
        add = part(add_kernel, rhs, chunks)
        near, code = call(
            part(add, (held, held_other), True), [row_block, small],
            right, slot, own_core, other_core, near, code,
        )
        beside = after(jnp.concatenate(beside), near)
        other_beside = swap(beside, 1)
        near, code = call(part(add, (late,), False), [row_block, small], right, slot, beside, near, code)
        return other_beside, near, code

    def reduce(send, pair, projected, left, right, slot):
        got = swap(send, 1)
        (send,) = call(part(spread_kernel, rhs, chunks, held_other), [plain(4 * m)], projected, right, slot)
        (keep,) = call(
            part(spread_kernel, rhs, chunks, late), [kept(4 * m)], after(projected, send), right, slot
        )
        got_held = swap(send, 1)
        pair, send_c, send_b, send_a = call(
            part(split_kernel, rhs),
            [small, coded(m), plain(m), plain(2 * m)],
            keep, pair, got,
        )
        got_c, got_b, got_a = swap(send_c, 2), swap(send_b, 2), swap(send_a, 2)
        (keep,) = call(
            part(spread_own_kernel, rhs, chunks, held), [kept(4 * m)], after(projected, send_c), left, right, slot
        )
        (keep,) = call(join_kernel, [kept(4 * m)], keep, got_held)
        got_c = after(got_c, keep)
        size = m * chunks
        if m == 1:
            pair, send_c = call(
                part(part_kernel, rhs, 3 * size, 0), [small, coded(1)], keep, pair, got_c
            )
            last_c = swap(send_c, 3 << low_bits)
            (send_b,) = call(
                part(part_kernel, rhs, 2 * size, 0), [coded(1)], keep, pair, got_b
            )
            last_b = swap(send_b, 2 << low_bits)
            mine, send_a = call(
                part(part_kernel, rhs, 0, size), [kept(1), coded(1)], keep, pair, got_a
            )
            return mine, pair, [swap(send_a, 1 << low_bits), last_b, last_c]
        (pair,) = call(part(pair_kernel, rhs), [small], pair, got_c[-1])
        got = jnp.concatenate([got_a, got_b, got_c[:-1]])
        (keep,) = call(join_kernel, [kept(4 * m)], keep, got)
        four = [keep[i * size : (i + 1) * size] for i in range(4)]
        for b in range(2, low_bits):
            (code,) = call(part(code_kernel, rhs), [((rhs, LANES), BF16)], pair)
            (pair,) = call(part(pair_kernel, rhs), [small], pair, swap(code, 1 << b))
            half = four[0].shape[0] // 2
            four = [x[:half] + swap(x[half:].astype(BF16), 1 << b).astype(F32) for x in four]
        sends = [call(part(message_kernel, rhs), [coded(1)], x, pair)[0] for x in four[1:]]
        return four[0], pair, [swap(x, (k + 1) << low_bits) for k, x in enumerate(sends)]

    def in_hbm(array):
        return pltpu.with_memory_space_constraint(array, pltpu.HBM)

    semaphore = pltpu.SemaphoreType.DMA
    factor = ((slots * rank, width), BF16)
    message, right_sides = call(
        part(open_kernel, rhs), [plain(1), panel], in_hbm(right_sides), far=(0,), fixed=(1,), scratch=[semaphore]
    )
    nugget, left, right, slot, near, pair = call(
        part(load_kernel, rhs, rank, place_of),
        [((1, width), F32), factor, factor, ((rhs, slots * rank), jnp.int32), row_block, small],
        right_sides, tile_column[:, 0], live_slots, in_hbm(nugget[None, :]),
        in_hbm(left_factors.reshape(slots * rank, width)), in_hbm(right_factors.reshape(slots * rank, width)),
        far=(3, 4, 5), scalars=(1, 2), fixed=(0, 1, 2), scratch=[semaphore] * 3,
    )
    other, near, _ = gather(message, (near, pair, slot, right))
    send, pair, earlier = call(
        part(first_kernel, rhs, chunks, late_other),
        [coded(4 * m), small, row_block],
        other, right, slot, near, pair,
    )
    mine, pair, got = reduce(send, pair, earlier, left, right, slot)
    message, residual, solution, first_gram = call(
        part(middle_kernel, rhs, chunks),
        [coded(1), panel, panel, small],
        right_sides, nugget, mine, pair, *got,
    )
    (near,) = call(near_kernel, [row_block], residual, left)
    other, near, code = gather(message, (near, first_gram, slot, right))
    send, pair, projected, direction, next_gram = call(
        part(second_kernel, rhs, chunks, late_other),
        [coded(4 * m), small, row_block, panel, small],
        other, right, slot, near, code, right_sides, residual, nugget, first_gram, earlier,
    )
    mine, pair, got = reduce(send, pair, projected, left, right, slot)
    return tuple(
        call(
            part(last_kernel, rhs, chunks),
            [panel, panel],
            direction, nugget, mine, pair, next_gram, *got, residual, solution,
        )
    )


def solution(mesh):
    return jax.shard_map(
        shards,
        mesh=mesh,
        in_specs=(
            P(None, ("groups", "row")),
            P(("groups", "row")),
            P(("groups", "row"), None, None),
            P(("groups", "row"), None, None),
            P(("groups", "row"), None),
            P(("groups", "row")),
        ),
        out_specs=(P(None, ("groups", "row")), P(None, ("groups", "row"))),
        check_vma=False,
    )
```

```python
import functools

import jax
import jax.numpy as jnp
from jax import lax
from jax.experimental import pallas as pl
from jax.experimental.pallas import tpu as pltpu
from jax.sharding import PartitionSpec as P

LANES = 128
F32 = jnp.float32
BF16 = jnp.bfloat16
EXACT = lax.Precision.HIGHEST
NN = (((1,), (0,)), ((), ()))
NT = (((1,), (1,)), ((), ()))


def lanes_of(block):
    return lax.broadcasted_iota(jnp.int32, block.shape, len(block.shape) - 1)


def sums_of(parts, rhs):
    rest = jnp.zeros((rhs, LANES - rhs * len(parts)), F32)
    return jnp.concatenate(parts + [rest], axis=1)


def encode(pair, rhs):
    high = pair.astype(BF16).astype(F32)
    rest = pair - high
    middle = rest.astype(BF16).astype(F32)
    low = rest - middle
    return (high + pltpu.roll(middle, 2 * rhs, 1) + pltpu.roll(low, 4 * rhs, 1)).astype(BF16)


def decode(code, rhs):
    total = code + pltpu.roll(code, LANES - 2 * rhs, 1) + pltpu.roll(code, LANES - 4 * rhs, 1)
    return jnp.where(lanes_of(total) < 2 * rhs, total, 0.0)


def second_of(pair, rhs):
    return pltpu.roll(pair, LANES - rhs, 1)


def right_divide(top, bottom, rhs):
    both = jnp.concatenate([top, bottom], axis=0)
    lane = lanes_of(both)
    both = jnp.where(lane < rhs, both, 0.0)
    one = lane[:1]
    for k in range(0, rhs, 2):
        col_0 = jnp.broadcast_to(both[:, k : k + 1], both.shape)
        col_1 = jnp.broadcast_to(both[:, k + 1 : k + 2], both.shape)
        a, b = col_0[k : k + 1], col_1[k : k + 1]
        c, d = col_0[k + 1 : k + 2], col_1[k + 1 : k + 2]
        inverse = 1.0 / (a * d - b * c)
        row_0 = jnp.where(one == k, -1.0, jnp.where(one == k + 1, 0.0, both[k : k + 1]))
        row_1 = jnp.where(one == k, 0.0, jnp.where(one == k + 1, -1.0, both[k + 1 : k + 2]))
        new_0 = (d * row_0 - b * row_1) * inverse
        new_1 = (a * row_1 - c * row_0) * inverse
        both = jnp.where((lane == k) | (lane == k + 1), 0.0, both) - col_0 * new_0 - col_1 * new_1
    return both[rhs:, :]


def left_multiply(square, block, rhs):
    return lax.dot_general(square[:, :rhs], block, NN, precision=EXACT, preferred_element_type=F32)


def gram(former, latter):
    return lax.dot_general(former, latter, NT, precision=EXACT, preferred_element_type=F32)


def rows_of(ref, chunks):
    panels, _, rhs, lanes = ref.shape
    return jnp.concatenate([ref[:, c].reshape(panels * rhs, lanes) for c in range(chunks)], axis=1)


def store_message(message_ref, block, rhs, at=0):
    for c in range(block.shape[1] // LANES):
        message_ref[at + c] = block[:, c * LANES : (c + 1) * LANES].astype(message_ref.dtype)


def far_terms(total, panels, factors, places, bases, rhs, chunks):
    rows = jnp.concatenate([rows_of(ref, chunks) for ref in panels], axis=0)
    far = [lax.dot_general(rows, ref[...], NT, preferred_element_type=F32) for ref in factors]
    far = jnp.concatenate(far, axis=1)
    at = 0
    for base, ref in zip(bases, panels):
        for i in range(ref.shape[0]):
            total = total + jnp.where(places == base + i, far[at : at + rhs], 0.0)
            at += rhs
    return total


def codes_of(panels_ref, chunks):
    count, held = panels_ref.shape[:2]
    code = jnp.zeros(panels_ref.shape[2:], F32)
    for i in range(count if held > chunks else 0):
        code = code + panels_ref[i, chunks].astype(F32)
    return code


def spread_terms(projected, factors, places, wanted, store, rhs, chunks, extra=None):
    masked = [jnp.where(places == place, projected, 0.0).astype(BF16) for place in wanted]
    masked = jnp.concatenate(masked, axis=0)
    width = factors[0].shape[0]
    step = 2 * LANES
    for block in range(chunks // 2):
        at = slice(block * step, (block + 1) * step)
        moved = sum(
            lax.dot_general(
                masked[:, i * width : (i + 1) * width], ref[:, at], NN, preferred_element_type=F32
            )
            for i, ref in enumerate(factors)
        )
        for i in range(len(wanted)):
            for b in range(2):
                piece = moved[i * rhs : (i + 1) * rhs, b * LANES : (b + 1) * LANES]
                if i == 0 and extra is not None:
                    place = block * step + b * LANES
                    piece = piece + extra[:, place : place + LANES]
                store(i, 2 * block + b, piece)


def open_kernel(rhs, right_side_hbm, message_ref, right_side_ref, sem):
    copy = pltpu.make_async_copy(right_side_hbm, right_side_ref, sem)
    copy.start()
    copy.wait()
    store_message(message_ref, right_side_ref[...], rhs)


def load_kernel(
    rhs, rank, own_ref, column_hbm, live_ref, nugget_hbm, left_hbm,
    nugget_ref, left_ref, named_ref, near_ref, sums_ref,
    column_ref, column_sem, nugget_sem, left_sem,
):
    copies = [
        pltpu.make_async_copy(column_hbm, column_ref, column_sem),
        pltpu.make_async_copy(nugget_hbm, nugget_ref, nugget_sem),
        pltpu.make_async_copy(left_hbm, left_ref, left_sem),
    ]
    for copy in copies:
        copy.start()
    own = own_ref[...]
    for copy in copies[:2]:
        copy.wait()
    slot_of = lax.broadcasted_iota(jnp.int32, (1, named_ref.shape[1]), 1) // rank
    named = jnp.full(slot_of.shape, -1, jnp.int32)
    for s in range(column_ref.shape[0]):
        named = jnp.where(slot_of == s, jnp.where(s < live_ref[0], column_ref[s], -1), named)
    named_ref[...] = jnp.broadcast_to(named, named_ref.shape)
    sums_ref[...] = sums_of([gram(own * nugget_ref[...], own), gram(own, own)], rhs)
    copies[2].wait()
    near = lax.dot_general(own.astype(BF16), left_ref[...], NT, preferred_element_type=F32)
    near_ref[...] = jnp.where(named >= 0, near, 0.0)


def load_add_kernel(
    rhs, chunks, place_of, base, held_ref, near_ref, named_ref, other_named_ref, right_hbm, other_ref,
    part_ref, places_ref, right_ref, right_sem,
):
    copy = pltpu.make_async_copy(right_hbm, right_ref, right_sem)
    copy.start()
    named = jnp.concatenate([named_ref[...], other_named_ref[...]], axis=1)
    offset = named ^ lax.axis_index("row")
    places = jnp.where((named >= 0) & ((offset & 1) == 0), place_of(offset), -1)
    places = jnp.concatenate([places] * (rhs // places.shape[0]), axis=0)
    places_ref[...] = places
    near = near_ref[...]
    total = jnp.concatenate([near, jnp.zeros(near.shape, F32)], axis=1)
    copy.wait()
    part_ref[...] = far_terms(total, [held_ref], (right_ref, other_ref), places, [base], rhs, chunks)


def near_add_kernel(
    rhs, chunks, base, held_ref, own_ref, right_side_ref, nugget_ref, left_ref, named_ref, places_ref,
    right_ref, other_ref, part_ref, sums_ref,
):
    own = own_ref[...]
    near = lax.dot_general(own.astype(BF16), left_ref[...], NT, preferred_element_type=F32)
    near = jnp.where(named_ref[:1] >= 0, near, 0.0)
    total = jnp.concatenate([near, jnp.zeros(near.shape, F32)], axis=1)
    part_ref[...] = far_terms(total, [held_ref], (right_ref, other_ref), places_ref[...], [base], rhs, chunks)
    weighted = own * nugget_ref[...]
    code = codes_of(held_ref, chunks)
    none = jnp.zeros((rhs, rhs), F32)
    sums_ref[...] = decode(code, rhs) + sums_of([none, gram(weighted, own), gram(right_side_ref[...], weighted)], rhs)


def add_kernel(
    rhs, chunks, bases, beside_ref, late_ref, right_ref, other_ref, places_ref, part_ref, sums_ref, message_ref
):
    panels = (beside_ref, late_ref)
    total = far_terms(part_ref[...], panels, (right_ref, other_ref), places_ref[...], bases, rhs, chunks)
    width = total.shape[1]
    message_ref[:, :width] = total
    message_ref[:, width:] = sums_ref[...] + decode(codes_of(beside_ref, chunks) + codes_of(late_ref, chunks), rhs)


def both_cores(message_ref, got_ref):
    half = (message_ref.shape[1] - LANES) // 2
    own = message_ref[:, :half] + got_ref[:, half : 2 * half]
    other = message_ref[:, half : 2 * half] + got_ref[:, :half]
    sums = message_ref[:, 2 * half :] + got_ref[:, 2 * half :]
    return jnp.concatenate([own, other], axis=1), sums


def symmetric_product(projected):
    rounded = projected.astype(BF16).astype(F32)
    first = gram(projected, rounded)
    return 0.5 * (first + first.T)


def send_terms(send_ref, projected, factors, places, wanted, pair, rhs, chunks):
    def store(i, c, piece):
        send_ref[i * chunks + c] = piece.astype(BF16)

    spread_terms(projected, factors, places, wanted, store, rhs, chunks)
    send_ref[len(wanted) * chunks] = encode(pair, rhs)


def first_kernel(
    rhs, chunks, wanted, message_ref, got_ref, right_ref, other_ref, places_ref,
    send_ref, pair_ref, projected_ref, sums_ref,
):
    projected, sums = both_cores(message_ref, got_ref)
    projected_ref[...] = projected
    sums_ref[...] = sums
    pair = sums + sums_of([symmetric_product(projected)], rhs)
    pair_ref[...] = pair
    send_terms(send_ref, projected, (right_ref, other_ref), places_ref[...], wanted, pair, rhs, chunks)


def second_kernel(
    rhs, chunks, wanted, message_ref, got_ref, right_ref, other_ref, places_ref,
    gram_ref, weighted_ref, earlier_ref,
    send_ref, pair_ref, projected_ref, next_gram_ref, mix_ref,
):
    projected, sums = both_cores(message_ref, got_ref)
    next_gram_ref[...] = sums
    mix = right_divide(gram_ref[...], sums, rhs)
    projected = projected + left_multiply(mix, earlier_ref[...], rhs)
    projected_ref[...] = projected
    weighted = left_multiply(mix, jnp.concatenate([sums[:, 2 * rhs : 3 * rhs], weighted_ref[:, :rhs]], axis=1), rhs)
    mixed = weighted[:, :rhs]
    curvature = sums[:, rhs : 2 * rhs] + mixed + mixed.T + gram(weighted[:, rhs:], mix[:, :rhs])
    pair = sums_of([curvature + symmetric_product(projected)], rhs)
    pair_ref[...] = pair
    send_terms(send_ref, projected, (right_ref, other_ref), places_ref[...], wanted, pair, rhs, chunks)
    mix_ref[...] = mix


def spread_kernel(
    rhs, chunks, wanted, projected_ref, left_ref, right_ref, other_ref, places_ref, keep_ref, beside_ref
):
    projected = projected_ref[...]
    kept = keep_ref.shape[0] // chunks

    def store(i, c, piece):
        if i < kept:
            keep_ref[i * chunks + c] = piece
        else:
            beside_ref[(i - kept) * chunks + c] = piece.astype(BF16)

    own = projected[:, : projected.shape[1] // 2].astype(BF16)
    own = lax.dot_general(own, left_ref[...], NN, preferred_element_type=F32)
    spread_terms(projected, (right_ref, other_ref), places_ref[...], wanted, store, rhs, chunks, own)


def direction_kernel(rhs, mix_ref, right_side_ref, residual_ref, direction_ref):
    direction_ref[...] = residual_ref[...] + left_multiply(mix_ref[...], right_side_ref[...], rhs)


def join_kernel(keep_ref, got_ref, sum_ref):
    sum_ref[...] = keep_ref[...] + got_ref[...].astype(F32)


def part_kernel(rhs, keep_ref, pair_ref, got_ref, total_ref, *sends):
    size = sends[0].shape[0] - 1
    total = pair_ref[...] + decode(got_ref[got_ref.shape[0] - 1].astype(F32), rhs)
    total_ref[...] = total
    code = encode(total, rhs)
    for i, send in enumerate(sends):
        at = i * size
        send[:size] = (keep_ref[at + size : at + 2 * size] + got_ref[at : at + size].astype(F32)).astype(BF16)
        send[size] = code


def message_kernel(rhs, panel_ref, pair_ref, message_ref):
    message_ref[: panel_ref.shape[0]] = panel_ref[...].astype(BF16)
    message_ref[panel_ref.shape[0]] = encode(pair_ref[...], rhs)


def code_kernel(rhs, pair_ref, code_ref):
    code_ref[...] = encode(pair_ref[...], rhs)


def pair_kernel(rhs, pair_ref, got_ref, total_ref):
    total_ref[...] = pair_ref[...] + decode(got_ref[...].astype(F32), rhs)


def gathered_product(keep_ref, plain_ref, pair_ref, got, direction, nugget, rhs, chunks):
    total = keep_ref[:chunks]
    total = total + plain_ref[...].astype(F32)
    code = jnp.zeros(pair_ref.shape, F32)
    for ref in got:
        total = total + ref[:chunks].astype(F32)
        code = code + ref[chunks].astype(F32)
    applied = nugget * direction + jnp.concatenate([total[c] for c in range(chunks)], axis=1)
    return applied, pair_ref[...] + decode(code, rhs)


def middle_kernel(rhs, chunks, direction_ref, nugget_ref, keep_ref, plain_ref, pair_ref, *rest):
    got, (message_ref, residual_ref, solution_ref, gram_ref) = rest[:-4], rest[-4:]
    direction = direction_ref[...]
    applied, pair = gathered_product(keep_ref, plain_ref, pair_ref, got, direction, nugget_ref[...], rhs, chunks)
    first_gram = second_of(pair, rhs)
    gram_ref[...] = first_gram
    step = right_divide(pair, first_gram, rhs)
    residual = direction - left_multiply(step, applied, rhs)
    residual_ref[...] = residual
    store_message(message_ref, residual, rhs)
    message_ref[chunks] = encode(sums_of([gram(residual, residual)], rhs), rhs)
    solution_ref[...] = left_multiply(step, direction, rhs)


def last_kernel(rhs, chunks, direction_ref, nugget_ref, keep_ref, plain_ref, pair_ref, gram_ref, *rest):
    got, (residual_ref, solution_ref, out_solution_ref, out_residual_ref) = rest[:-4], rest[-4:]
    direction = direction_ref[...]
    applied, pair = gathered_product(keep_ref, plain_ref, pair_ref, got, direction, nugget_ref[...], rhs, chunks)
    step = right_divide(pair, gram_ref[...], rhs)
    out_solution_ref[...] = solution_ref[...] + left_multiply(step, direction, rhs)
    out_residual_ref[...] = residual_ref[...] - left_multiply(step, applied, rhs)


def call(kernel, outs, *args, far=(), scalars=(), fixed=(), scratch=()):
    whole = pl.BlockSpec(memory_space=pltpu.VMEM)
    spaces = {i: pltpu.HBM for i in far} | {i: pltpu.SMEM for i in scalars}
    return pl.pallas_call(
        kernel,
        out_shape=[
            pltpu.VMEM(shape, dtype) if i in fixed else jax.ShapeDtypeStruct(shape, dtype)
            for i, (shape, dtype) in enumerate(outs)
        ],
        in_specs=[pl.BlockSpec(memory_space=spaces[i]) if i in spaces else whole for i in range(len(args))],
        out_specs=[whole] * len(outs),
        scratch_shapes=list(scratch),
        cost_estimate=pl.CostEstimate(flops=0, bytes_accessed=0, transcendentals=0),
        compiler_params=pltpu.CompilerParams(vmem_limit_bytes=32 * 1024 * 1024),
    )(*args)


def after(value, *others):
    return lax.optimization_barrier((value, *others))[0]


def shards(right_sides, nugget, left_factors, right_factors, tile_column, live_slots):
    devices = lax.axis_size("row")
    bits = devices.bit_length() - 1
    low_bits = bits - 2
    slots, rank, width = left_factors.shape
    rhs = right_sides.shape[0]
    chunks = width // LANES
    part = functools.partial

    def swap(array, offset):
        return lax.ppermute(array, "row", [(i, i ^ offset) for i in range(devices)])

    order = (0, 3, 2, 1)
    groups = []
    for k in order:
        group = [k << low_bits]
        for b in range(low_bits - 1, 1, -1):
            group = group + [o | (1 << b) for o in group]
        groups.append(group)
    m = len(groups[0])
    held_offsets = sum(groups, [])
    offsets = held_offsets + [o | 2 for o in held_offsets]
    held, late = 0, 4 * m

    def place_of(offset):
        place = ((4 - (offset >> low_bits)) & 3) * m
        for b in range(low_bits - 1, 1, -1):
            place = place + (((offset >> b) & 1) << (low_bits - 1 - b))
        return place + ((offset >> 1) & 1) * late

    assert [place_of(o) for o in offsets] == list(range(devices // 2))
    stay, go = tuple(range(late + m)), tuple(range(late + m, 2 * late))

    small = ((rhs, LANES), F32)
    panel = ((rhs, width), F32)
    row_block = ((rhs, slots * rank), F32)
    two_rows = ((rhs, 2 * slots * rank), F32)
    core_message = ((rhs, 2 * slots * rank + LANES), F32)
    factor = ((slots * rank, width), BF16)
    semaphore = pltpu.SemaphoreType.DMA

    def plain(count):
        return ((count * chunks, rhs, LANES), BF16)

    def coded(count):
        return ((count * chunks + 1, rhs, LANES), BF16)

    def kept(count):
        return ((count * chunks, rhs, LANES), F32)

    def gather(message, first_terms, *early):
        mine = [message[None]] + [swap(message, k << low_bits)[None] for k in order[1:]]
        for b in range(low_bits - 1, 1, -1):
            mine = [jnp.concatenate([g, swap(g, 1 << b)]) for g in mine]
        beside = swap(mine[0], 2)
        late_panels = swap(after(jnp.concatenate(mine[1:]), beside, *early), 2)
        terms, sums, factors, places = first_terms(jnp.concatenate(mine))
        late_panels = after(late_panels, terms)
        (message,) = call(
            part(add_kernel, rhs, chunks, (late, late + m)),
            [core_message],
            beside, late_panels, *factors, places, terms, sums,
        )
        return message, swap(message, 1), factors, places

    def reduce(send, pair, projected, left, factors, places, *early):
        got = swap(send, 2)
        keep, beside = call(
            part(spread_kernel, rhs, chunks, stay),
            [kept(4 * m), plain(m)],
            projected, left, *factors, places,
        )
        if m == 1:
            pair, *sends = call(
                part(part_kernel, rhs), [small] + [coded(1)] * 3, keep, pair, after(got, keep, *early)
            )
            got = [swap(x, k << low_bits) for x, k in zip(sends, order[1:])]
            return keep, swap(beside, 2), pair, got
        (pair,) = call(part(pair_kernel, rhs), [small], pair, got[-1])
        (keep,) = call(join_kernel, [kept(4 * m)], keep, jnp.concatenate([swap(beside, 2), got[:-1]]))
        size = m * chunks
        four = [keep[i * size : (i + 1) * size] for i in range(4)]
        for b in range(2, low_bits):
            (code,) = call(part(code_kernel, rhs), [((rhs, LANES), BF16)], pair)
            (pair,) = call(part(pair_kernel, rhs), [small], pair, swap(code, 1 << b))
            half = four[0].shape[0] // 2
            four = [x[:half] + swap(x[half:].astype(BF16), 1 << b).astype(F32) for x in four]
        sends = [call(part(message_kernel, rhs), [coded(1)], x, pair)[0] for x in four[1:]]
        nothing = jnp.zeros(*plain(1))
        return four[0], nothing, pair, [swap(x, k << low_bits) for x, k in zip(sends, order[1:])]

    def in_hbm(array):
        return pltpu.with_memory_space_constraint(array, pltpu.HBM)

    message, right_sides = call(
        part(open_kernel, rhs), [plain(1), panel], in_hbm(right_sides), far=(0,), fixed=(1,), scratch=[semaphore]
    )
    right = right_factors.reshape(slots * rank, width)
    other = swap(right, 1)
    named_shape = ((8, slots * rank), jnp.int32)
    nugget, left, named, near, sums = call(
        part(load_kernel, rhs, rank),
        [((1, width), F32), factor, named_shape, row_block, small],
        right_sides, in_hbm(tile_column.reshape(slots)), live_slots, in_hbm(nugget[None, :]),
        in_hbm(left_factors.reshape(slots * rank, width)),
        far=(1, 3, 4), scalars=(2,), fixed=(0, 1), scratch=[pltpu.SMEM((slots,), jnp.int32)] + [semaphore] * 3,
    )
    other_named = swap(named, 1)

    def loading(mine):
        terms, places, here = call(
            part(load_add_kernel, rhs, chunks, place_of, held),
            [two_rows, ((rhs, 2 * slots * rank), jnp.int32), factor],
            mine, near, named, other_named, in_hbm(right), other,
            far=(4,), fixed=(2,), scratch=[semaphore],
        )
        return terms, sums, (here, other), places

    message, got, factors, places = gather(message, loading, near)
    send, pair, earlier, weighted = call(
        part(first_kernel, rhs, chunks, go),
        [coded(3 * m), small, two_rows, small],
        message, got, *factors, places,
    )
    mine, beside, pair, got = reduce(send, pair, earlier, left, factors, places)
    message, residual, solution, first_gram = call(
        part(middle_kernel, rhs, chunks),
        [coded(1), panel, panel, small],
        right_sides, nugget, mine, beside, pair, *got,
    )

    def loaded(mine):
        terms, sums = call(
            part(near_add_kernel, rhs, chunks, held),
            [two_rows, small],
            mine, residual, right_sides, nugget, left, named, places, *factors,
        )
        return terms, sums, factors, places

    message, got, _, _ = gather(message, loaded)
    send, pair, projected, next_gram, mix = call(
        part(second_kernel, rhs, chunks, go),
        [coded(3 * m), small, two_rows, small, small],
        message, got, *factors, places, first_gram, weighted, earlier,
    )
    (direction,) = call(part(direction_kernel, rhs), [panel], mix, right_sides, residual)
    mine, beside, pair, got = reduce(send, pair, projected, left, factors, places, direction)
    return tuple(
        call(
            part(last_kernel, rhs, chunks),
            [panel, panel],
            direction, nugget, mine, beside, pair, next_gram, *got, residual, solution,
        )
    )


def solution(mesh):
    return jax.shard_map(
        shards,
        mesh=mesh,
        in_specs=(
            P(None, ("groups", "row")),
            P(("groups", "row")),
            P(("groups", "row"), None, None),
            P(("groups", "row"), None, None),
            P(("groups", "row"), None),
            P(("groups", "row")),
        ),
        out_specs=(P(None, ("groups", "row")), P(None, ("groups", "row"))),
        check_vma=False,
    )
```

```python
import functools

import jax
import jax.numpy as jnp
from jax import lax
from jax.experimental import pallas as pl
from jax.experimental.pallas import tpu as pltpu
from jax.sharding import PartitionSpec as P

LANES = 128
F32 = jnp.float32
BF16 = jnp.bfloat16
EXACT = lax.Precision.HIGHEST
NN = (((1,), (0,)), ((), ()))
NT = (((1,), (1,)), ((), ()))


def lanes_of(block):
    return lax.broadcasted_iota(jnp.int32, block.shape, len(block.shape) - 1)


def sums_of(parts, rhs):
    rest = jnp.zeros((rhs, LANES - rhs * len(parts)), F32)
    return jnp.concatenate(parts + [rest], axis=1)


def encode(pair, rhs):
    high = pair.astype(BF16).astype(F32)
    rest = pair - high
    middle = rest.astype(BF16).astype(F32)
    low = rest - middle
    return (high + pltpu.roll(middle, 2 * rhs, 1) + pltpu.roll(low, 4 * rhs, 1)).astype(BF16)


def decode(code, rhs):
    total = code + pltpu.roll(code, LANES - 2 * rhs, 1) + pltpu.roll(code, LANES - 4 * rhs, 1)
    return jnp.where(lanes_of(total) < 2 * rhs, total, 0.0)


def second_of(pair, rhs):
    return pltpu.roll(pair, LANES - rhs, 1)


def right_divide(top, bottom, rhs):
    both = jnp.concatenate([top, bottom], axis=0)
    lane = lanes_of(both)
    both = jnp.where(lane < rhs, both, 0.0)
    one = lane[:1]
    for k in range(0, rhs, 4):
        cols = [jnp.broadcast_to(both[:, k + j : k + j + 1], both.shape) for j in range(4)]
        p = [[cols[j][k + i : k + i + 1] for j in range(4)] for i in range(4)]
        inside = (one >= k) & (one < k + 4)
        rows = [
            jnp.where(inside, jnp.where(one == k + i, -1.0, 0.0), both[k + i : k + i + 1]) for i in range(4)
        ]
        inverse = 1.0 / (p[0][0] * p[1][1] - p[0][1] * p[1][0])

        def upper(x, y):
            return (p[1][1] * x - p[0][1] * y) * inverse, (p[0][0] * y - p[1][0] * x) * inverse

        b_02, b_12 = upper(p[0][2], p[1][2])
        b_03, b_13 = upper(p[0][3], p[1][3])
        r_0, r_1 = upper(rows[0], rows[1])
        s_22 = p[2][2] - p[2][0] * b_02 - p[2][1] * b_12
        s_23 = p[2][3] - p[2][0] * b_03 - p[2][1] * b_13
        s_32 = p[3][2] - p[3][0] * b_02 - p[3][1] * b_12
        s_33 = p[3][3] - p[3][0] * b_03 - p[3][1] * b_13
        inverse_low = 1.0 / (s_22 * s_33 - s_23 * s_32)
        q_2 = rows[2] - p[2][0] * r_0 - p[2][1] * r_1
        q_3 = rows[3] - p[3][0] * r_0 - p[3][1] * r_1
        w_2 = (s_33 * q_2 - s_23 * q_3) * inverse_low
        w_3 = (s_22 * q_3 - s_32 * q_2) * inverse_low
        w_0 = r_0 - b_02 * w_2 - b_03 * w_3
        w_1 = r_1 - b_12 * w_2 - b_13 * w_3
        both = jnp.where((lane >= k) & (lane < k + 4), 0.0, both)
        both = both - cols[0] * w_0 - cols[1] * w_1 - cols[2] * w_2 - cols[3] * w_3
    return both[rhs:, :]


def left_multiply(square, block, rhs):
    return lax.dot_general(square[:, :rhs], block, NN, precision=EXACT, preferred_element_type=F32)


def gram(former, latter):
    return lax.dot_general(former, latter, NT, precision=EXACT, preferred_element_type=F32)


def rows_of(ref, chunks):
    panels, _, rhs, lanes = ref.shape
    return jnp.concatenate([ref[:, c].reshape(panels * rhs, lanes) for c in range(chunks)], axis=1)


def store_message(message_ref, block, rhs, at=0):
    for c in range(block.shape[1] // LANES):
        message_ref[at + c] = block[:, c * LANES : (c + 1) * LANES].astype(message_ref.dtype)


def far_terms(total, panels, turned_ref, places, bases, rhs, chunks):
    rows = jnp.concatenate([rows_of(ref, chunks) for ref in panels], axis=0)
    far = lax.dot_general(rows, turned_ref[...], NN, preferred_element_type=F32)
    at = 0
    for base, ref in zip(bases, panels):
        for i in range(ref.shape[0]):
            total = total + jnp.where(places == base + i, far[at : at + rhs], 0.0)
            at += rhs
    return total


def codes_of(panels_ref, chunks):
    count, held = panels_ref.shape[:2]
    code = jnp.zeros(panels_ref.shape[2:], F32)
    for i in range(count if held > chunks else 0):
        code = code + panels_ref[i, chunks].astype(F32)
    return code


def spread_terms(projected, factors, places, wanted, store, rhs, chunks, extra=None):
    masked = [jnp.where(places == place, projected, 0.0).astype(BF16) for place in wanted]
    masked = jnp.concatenate(masked, axis=0)
    width = factors[0].shape[0]
    step = 2 * LANES
    for block in range(chunks // 2):
        at = slice(block * step, (block + 1) * step)
        moved = sum(
            lax.dot_general(
                masked[:, i * width : (i + 1) * width], ref[:, at], NN, preferred_element_type=F32
            )
            for i, ref in enumerate(factors)
        )
        for i in range(len(wanted)):
            for b in range(2):
                piece = moved[i * rhs : (i + 1) * rhs, b * LANES : (b + 1) * LANES]
                if i == 0 and extra is not None:
                    place = block * step + b * LANES
                    piece = piece + extra[:, place : place + LANES]
                store(i, 2 * block + b, piece)


def open_kernel(rhs, right_side_hbm, message_ref, right_side_ref, sem):
    copy = pltpu.make_async_copy(right_side_hbm, right_side_ref, sem)
    copy.start()
    copy.wait()
    store_message(message_ref, right_side_ref[...], rhs)


def load_kernel(
    rhs, rank, own_ref, column_hbm, live_ref, nugget_hbm, left_hbm,
    nugget_ref, left_ref, named_ref, near_ref, sums_ref,
    column_ref, column_sem, nugget_sem, left_sem,
):
    copies = [
        pltpu.make_async_copy(column_hbm, column_ref, column_sem),
        pltpu.make_async_copy(nugget_hbm, nugget_ref, nugget_sem),
        pltpu.make_async_copy(left_hbm, left_ref, left_sem),
    ]
    for copy in copies:
        copy.start()
    own = own_ref[...]
    for copy in copies[:2]:
        copy.wait()
    slot_of = lax.broadcasted_iota(jnp.int32, (1, named_ref.shape[1]), 1) // rank
    named = jnp.full(slot_of.shape, -1, jnp.int32)
    for s in range(column_ref.shape[0]):
        named = jnp.where(slot_of == s, jnp.where(s < live_ref[0], column_ref[s], -1), named)
    named_ref[...] = jnp.broadcast_to(named, named_ref.shape)
    sums_ref[...] = sums_of([gram(own * nugget_ref[...], own), gram(own, own)], rhs)
    copies[2].wait()
    near = lax.dot_general(own.astype(BF16), left_ref[...], NT, preferred_element_type=F32)
    near_ref[...] = jnp.where(named >= 0, near, 0.0)


def load_add_kernel(
    rhs, chunks, place_of, base, held_ref, near_ref, named_ref, other_named_ref, right_hbm, other_ref,
    part_ref, places_ref, right_ref, turned_ref, right_sem,
):
    copy = pltpu.make_async_copy(right_hbm, right_ref, right_sem)
    copy.start()
    named = jnp.concatenate([named_ref[...], other_named_ref[...]], axis=1)
    offset = named ^ lax.axis_index("row")
    places = jnp.where((named >= 0) & ((offset & 1) == 0), place_of(offset), -1)
    places = jnp.concatenate([places] * (rhs // places.shape[0]), axis=0)
    places_ref[...] = places
    near = near_ref[...]
    total = jnp.concatenate([near, jnp.zeros(near.shape, F32)], axis=1)
    half = other_ref.shape[0]
    turned_ref[:, half:] = other_ref[...].T
    copy.wait()
    turned_ref[:, :half] = right_ref[...].T
    part_ref[...] = far_terms(total, [held_ref], turned_ref, places, [base], rhs, chunks)


def near_add_kernel(
    rhs, chunks, base, held_ref, own_ref, right_side_ref, nugget_ref, left_ref, named_ref, places_ref,
    turned_ref, part_ref, sums_ref,
):
    own = own_ref[...]
    near = lax.dot_general(own.astype(BF16), left_ref[...], NT, preferred_element_type=F32)
    near = jnp.where(named_ref[:1] >= 0, near, 0.0)
    total = jnp.concatenate([near, jnp.zeros(near.shape, F32)], axis=1)
    part_ref[...] = far_terms(total, [held_ref], turned_ref, places_ref[...], [base], rhs, chunks)
    weighted = own * nugget_ref[...]
    code = codes_of(held_ref, chunks)
    none = jnp.zeros((rhs, rhs), F32)
    sums_ref[...] = decode(code, rhs) + sums_of([none, gram(weighted, own), gram(right_side_ref[...], weighted)], rhs)


def add_kernel(
    rhs, chunks, bases, beside_ref, late_ref, turned_ref, places_ref, part_ref, sums_ref, message_ref
):
    panels = (beside_ref, late_ref)
    total = far_terms(part_ref[...], panels, turned_ref, places_ref[...], bases, rhs, chunks)
    width = total.shape[1]
    message_ref[:, :width] = total
    message_ref[:, width:] = sums_ref[...] + decode(codes_of(beside_ref, chunks) + codes_of(late_ref, chunks), rhs)


def both_cores(message_ref, got_ref):
    half = (message_ref.shape[1] - LANES) // 2
    own = message_ref[:, :half] + got_ref[:, half : 2 * half]
    other = message_ref[:, half : 2 * half] + got_ref[:, :half]
    sums = message_ref[:, 2 * half :] + got_ref[:, 2 * half :]
    return jnp.concatenate([own, other], axis=1), sums


def rounded_gram(projected):
    rounded = projected.astype(BF16)
    return lax.dot_general(rounded, rounded, NT, preferred_element_type=F32)


def send_terms(send_ref, projected, factors, places, wanted, pair, rhs, chunks):
    def store(i, c, piece):
        send_ref[i * chunks + c] = piece.astype(BF16)

    spread_terms(projected, factors, places, wanted, store, rhs, chunks)
    send_ref[len(wanted) * chunks] = encode(pair, rhs)


def first_kernel(
    rhs, chunks, wanted, message_ref, got_ref, right_ref, other_ref, places_ref,
    send_ref, pair_ref, projected_ref, sums_ref,
):
    projected, sums = both_cores(message_ref, got_ref)
    projected_ref[...] = projected
    sums_ref[...] = sums
    pair = sums + sums_of([rounded_gram(projected)], rhs)
    pair_ref[...] = pair
    send_terms(send_ref, projected, (right_ref, other_ref), places_ref[...], wanted, pair, rhs, chunks)


def second_kernel(
    rhs, chunks, wanted, message_ref, got_ref, right_ref, other_ref, places_ref,
    gram_ref, weighted_ref, earlier_ref,
    send_ref, pair_ref, projected_ref, next_gram_ref, mix_ref,
):
    projected, sums = both_cores(message_ref, got_ref)
    next_gram_ref[...] = sums
    mix = right_divide(gram_ref[...], sums, rhs)
    projected = projected + left_multiply(mix, earlier_ref[...], rhs)
    projected_ref[...] = projected
    weighted = left_multiply(mix, jnp.concatenate([sums[:, 2 * rhs : 3 * rhs], weighted_ref[:, :rhs]], axis=1), rhs)
    mixed = weighted[:, :rhs]
    curvature = sums[:, rhs : 2 * rhs] + mixed + mixed.T + gram(weighted[:, rhs:], mix[:, :rhs])
    pair = sums_of([curvature + rounded_gram(projected)], rhs)
    pair_ref[...] = pair
    send_terms(send_ref, projected, (right_ref, other_ref), places_ref[...], wanted, pair, rhs, chunks)
    mix_ref[...] = mix


def spread_kernel(
    rhs, chunks, wanted, projected_ref, left_ref, right_ref, other_ref, places_ref, keep_ref, beside_ref
):
    projected = projected_ref[...]
    kept = keep_ref.shape[0] // chunks

    def store(i, c, piece):
        if i < kept:
            keep_ref[i * chunks + c] = piece
        else:
            beside_ref[(i - kept) * chunks + c] = piece.astype(BF16)

    own = projected[:, : projected.shape[1] // 2].astype(BF16)
    own = lax.dot_general(own, left_ref[...], NN, preferred_element_type=F32)
    spread_terms(projected, (right_ref, other_ref), places_ref[...], wanted, store, rhs, chunks, own)


def solution_kernel(rhs, step_ref, right_side_ref, solution_ref):
    solution_ref[...] = left_multiply(step_ref[...], right_side_ref[...], rhs)


def direction_kernel(rhs, mix_ref, right_side_ref, residual_ref, direction_ref):
    direction_ref[...] = residual_ref[...] + left_multiply(mix_ref[...], right_side_ref[...], rhs)


def join_kernel(keep_ref, got_ref, sum_ref):
    sum_ref[...] = keep_ref[...] + got_ref[...].astype(F32)


def part_kernel(rhs, keep_ref, pair_ref, got_ref, total_ref, *sends):
    size = sends[0].shape[0] - 1
    total = pair_ref[...] + decode(got_ref[got_ref.shape[0] - 1].astype(F32), rhs)
    total_ref[...] = total
    code = encode(total, rhs)
    for i, send in enumerate(sends):
        at = i * size
        send[:size] = (keep_ref[at + size : at + 2 * size] + got_ref[at : at + size].astype(F32)).astype(BF16)
        send[size] = code


def message_kernel(rhs, panel_ref, pair_ref, message_ref):
    message_ref[: panel_ref.shape[0]] = panel_ref[...].astype(BF16)
    message_ref[panel_ref.shape[0]] = encode(pair_ref[...], rhs)


def code_kernel(rhs, pair_ref, code_ref):
    code_ref[...] = encode(pair_ref[...], rhs)


def pair_kernel(rhs, pair_ref, got_ref, total_ref):
    total_ref[...] = pair_ref[...] + decode(got_ref[...].astype(F32), rhs)


def gathered_product(keep_ref, plain_ref, pair_ref, got, direction, nugget, rhs, chunks):
    total = keep_ref[:chunks]
    total = total + plain_ref[...].astype(F32)
    code = jnp.zeros(pair_ref.shape, F32)
    for ref in got:
        total = total + ref[:chunks].astype(F32)
        code = code + ref[chunks].astype(F32)
    applied = nugget * direction + jnp.concatenate([total[c] for c in range(chunks)], axis=1)
    return applied, pair_ref[...] + decode(code, rhs)


def middle_kernel(rhs, chunks, direction_ref, nugget_ref, keep_ref, plain_ref, pair_ref, *rest):
    got, (message_ref, residual_ref, step_ref, gram_ref) = rest[:-4], rest[-4:]
    direction = direction_ref[...]
    applied, pair = gathered_product(keep_ref, plain_ref, pair_ref, got, direction, nugget_ref[...], rhs, chunks)
    first_gram = second_of(pair, rhs)
    gram_ref[...] = first_gram
    step = right_divide(pair, first_gram, rhs)
    residual = direction - left_multiply(step, applied, rhs)
    residual_ref[...] = residual
    store_message(message_ref, residual, rhs)
    message_ref[chunks] = encode(sums_of([gram(residual, residual)], rhs), rhs)
    step_ref[...] = step


def last_kernel(rhs, chunks, direction_ref, nugget_ref, keep_ref, plain_ref, pair_ref, gram_ref, *rest):
    got, (residual_ref, solution_ref, out_solution_ref, out_residual_ref) = rest[:-4], rest[-4:]
    direction = direction_ref[...]
    applied, pair = gathered_product(keep_ref, plain_ref, pair_ref, got, direction, nugget_ref[...], rhs, chunks)
    step = right_divide(pair, gram_ref[...], rhs)
    out_solution_ref[...] = solution_ref[...] + left_multiply(step, direction, rhs)
    out_residual_ref[...] = residual_ref[...] - left_multiply(step, applied, rhs)


def call(kernel, outs, *args, far=(), scalars=(), fixed=(), scratch=()):
    whole = pl.BlockSpec(memory_space=pltpu.VMEM)
    spaces = {i: pltpu.HBM for i in far} | {i: pltpu.SMEM for i in scalars}
    return pl.pallas_call(
        kernel,
        out_shape=[
            pltpu.VMEM(shape, dtype) if i in fixed else jax.ShapeDtypeStruct(shape, dtype)
            for i, (shape, dtype) in enumerate(outs)
        ],
        in_specs=[pl.BlockSpec(memory_space=spaces[i]) if i in spaces else whole for i in range(len(args))],
        out_specs=[whole] * len(outs),
        scratch_shapes=list(scratch),
        cost_estimate=pl.CostEstimate(flops=0, bytes_accessed=0, transcendentals=0),
        compiler_params=pltpu.CompilerParams(vmem_limit_bytes=32 * 1024 * 1024),
    )(*args)


def after(value, *others):
    return lax.optimization_barrier((value, *others))[0]


def shards(right_sides, nugget, left_factors, right_factors, tile_column, live_slots):
    devices = lax.axis_size("row")
    bits = devices.bit_length() - 1
    low_bits = bits - 2
    slots, rank, width = left_factors.shape
    rhs = right_sides.shape[0]
    chunks = width // LANES
    part = functools.partial

    def swap(array, offset):
        return lax.ppermute(array, "row", [(i, i ^ offset) for i in range(devices)])

    order = (0, 3, 2, 1)
    groups = []
    for k in order:
        group = [k << low_bits]
        for b in range(low_bits - 1, 1, -1):
            group = group + [o | (1 << b) for o in group]
        groups.append(group)
    m = len(groups[0])
    held_offsets = sum(groups, [])
    offsets = held_offsets + [o | 2 for o in held_offsets]
    held, late = 0, 4 * m

    def place_of(offset):
        place = ((4 - (offset >> low_bits)) & 3) * m
        for b in range(low_bits - 1, 1, -1):
            place = place + (((offset >> b) & 1) << (low_bits - 1 - b))
        return place + ((offset >> 1) & 1) * late

    assert [place_of(o) for o in offsets] == list(range(devices // 2))
    stay, go = tuple(range(late + m)), tuple(range(late + m, 2 * late))

    small = ((rhs, LANES), F32)
    panel = ((rhs, width), F32)
    row_block = ((rhs, slots * rank), F32)
    two_rows = ((rhs, 2 * slots * rank), F32)
    core_message = ((rhs, 2 * slots * rank + LANES), F32)
    factor = ((slots * rank, width), BF16)
    semaphore = pltpu.SemaphoreType.DMA

    def plain(count):
        return ((count * chunks, rhs, LANES), BF16)

    def coded(count):
        return ((count * chunks + 1, rhs, LANES), BF16)

    def kept(count):
        return ((count * chunks, rhs, LANES), F32)

    def gather(message, first_terms, *early):
        mine = [message[None]] + [swap(message, k << low_bits)[None] for k in order[1:]]
        for b in range(low_bits - 1, 1, -1):
            mine = [jnp.concatenate([g, swap(g, 1 << b)]) for g in mine]
        beside = swap(mine[0], 2)
        late_panels = swap(after(jnp.concatenate(mine[1:]), beside, *early), 2)
        terms, sums, turned, factors, places = first_terms(jnp.concatenate(mine))
        late_panels = after(late_panels, terms)
        (message,) = call(
            part(add_kernel, rhs, chunks, (late, late + m)),
            [core_message],
            beside, late_panels, turned, places, terms, sums,
        )
        return message, swap(message, 1), turned, factors, places

    def reduce(send, pair, projected, left, factors, places, *early):
        got = swap(send, 2)
        keep, beside = call(
            part(spread_kernel, rhs, chunks, stay),
            [kept(4 * m), plain(m)],
            projected, left, *factors, places,
        )
        if m == 1:
            pair, *sends = call(
                part(part_kernel, rhs), [small] + [coded(1)] * 3, keep, pair, after(got, keep, *early)
            )
            got = [swap(x, k << low_bits) for x, k in zip(sends, order[1:])]
            return keep, swap(beside, 2), pair, got
        (pair,) = call(part(pair_kernel, rhs), [small], pair, got[-1])
        (keep,) = call(join_kernel, [kept(4 * m)], keep, jnp.concatenate([swap(beside, 2), got[:-1]]))
        size = m * chunks
        four = [keep[i * size : (i + 1) * size] for i in range(4)]
        for b in range(2, low_bits):
            (code,) = call(part(code_kernel, rhs), [((rhs, LANES), BF16)], pair)
            (pair,) = call(part(pair_kernel, rhs), [small], pair, swap(code, 1 << b))
            half = four[0].shape[0] // 2
            four = [x[:half] + swap(x[half:].astype(BF16), 1 << b).astype(F32) for x in four]
        sends = [call(part(message_kernel, rhs), [coded(1)], x, pair)[0] for x in four[1:]]
        nothing = jnp.zeros(*plain(1))
        return four[0], nothing, pair, [swap(x, k << low_bits) for x, k in zip(sends, order[1:])]

    def in_hbm(array):
        return pltpu.with_memory_space_constraint(array, pltpu.HBM)

    message, right_sides = call(
        part(open_kernel, rhs), [plain(1), panel], in_hbm(right_sides), far=(0,), fixed=(1,), scratch=[semaphore]
    )
    right = right_factors.reshape(slots * rank, width)
    other = swap(after(right, message), 1)
    named_shape = ((8, slots * rank), jnp.int32)
    nugget, left, named, near, sums = call(
        part(load_kernel, rhs, rank),
        [((1, width), F32), factor, named_shape, row_block, small],
        right_sides, in_hbm(tile_column.reshape(slots)), live_slots, in_hbm(nugget[None, :]),
        in_hbm(left_factors.reshape(slots * rank, width)),
        far=(1, 3, 4), scalars=(2,), fixed=(0, 1), scratch=[pltpu.SMEM((slots,), jnp.int32)] + [semaphore] * 3,
    )
    other_named = swap(named, 1)

    def loading(mine):
        terms, places, here, turned = call(
            part(load_add_kernel, rhs, chunks, place_of, held),
            [two_rows, ((rhs, 2 * slots * rank), jnp.int32), factor, ((width, 2 * slots * rank), BF16)],
            mine, near, named, other_named, in_hbm(right), other,
            far=(4,), fixed=(2, 3), scratch=[semaphore],
        )
        return terms, sums, turned, (here, other), places

    message, got, turned, factors, places = gather(message, loading, near)
    send, pair, earlier, weighted = call(
        part(first_kernel, rhs, chunks, go),
        [coded(3 * m), small, two_rows, small],
        message, got, *factors, places,
    )
    mine, beside, pair, got = reduce(send, pair, earlier, left, factors, places)
    message, residual, step, first_gram = call(
        part(middle_kernel, rhs, chunks),
        [coded(1), panel, small, small],
        right_sides, nugget, mine, beside, pair, *got,
    )

    (solution,) = call(part(solution_kernel, rhs), [panel], step, right_sides)

    def loaded(mine):
        terms, sums = call(
            part(near_add_kernel, rhs, chunks, held),
            [two_rows, small],
            after(mine, solution), residual, right_sides, nugget, left, named, places, turned,
        )
        return terms, sums, turned, factors, places

    message, got, *_ = gather(message, loaded)
    send, pair, projected, next_gram, mix = call(
        part(second_kernel, rhs, chunks, go),
        [coded(3 * m), small, two_rows, small, small],
        message, got, *factors, places, first_gram, weighted, earlier,
    )
    (direction,) = call(part(direction_kernel, rhs), [panel], mix, right_sides, residual)
    mine, beside, pair, got = reduce(send, pair, projected, left, factors, places, direction)
    return tuple(
        call(
            part(last_kernel, rhs, chunks),
            [panel, panel],
            direction, nugget, mine, beside, pair, next_gram, *got, residual, solution,
        )
    )


def solution(mesh):
    return jax.shard_map(
        shards,
        mesh=mesh,
        in_specs=(
            P(None, ("groups", "row")),
            P(("groups", "row")),
            P(("groups", "row"), None, None),
            P(("groups", "row"), None, None),
            P(("groups", "row"), None),
            P(("groups", "row")),
        ),
        out_specs=(P(None, ("groups", "row")), P(None, ("groups", "row"))),
        check_vma=False,
    )
```

```python
import functools

import jax
import jax.numpy as jnp
from jax import lax
from jax.experimental import pallas as pl
from jax.experimental.pallas import tpu as pltpu
from jax.sharding import PartitionSpec as P

LANES = 128
F32 = jnp.float32
BF16 = jnp.bfloat16
EXACT = lax.Precision.HIGHEST
NN = (((1,), (0,)), ((), ()))
NT = (((1,), (1,)), ((), ()))


def lanes_of(block):
    return lax.broadcasted_iota(jnp.int32, block.shape, len(block.shape) - 1)


def sums_of(parts, rhs):
    rest = jnp.zeros((rhs, LANES - rhs * len(parts)), F32)
    return jnp.concatenate(parts + [rest], axis=1)


def encode(pair, rhs):
    high = pair.astype(BF16).astype(F32)
    rest = pair - high
    middle = rest.astype(BF16).astype(F32)
    low = rest - middle
    return (high + pltpu.roll(middle, 2 * rhs, 1) + pltpu.roll(low, 4 * rhs, 1)).astype(BF16)


def decode(code, rhs):
    total = code + pltpu.roll(code, LANES - 2 * rhs, 1) + pltpu.roll(code, LANES - 4 * rhs, 1)
    return jnp.where(lanes_of(total) < 2 * rhs, total, 0.0)


def second_of(pair, rhs):
    return pltpu.roll(pair, LANES - rhs, 1)


def right_divide(top, bottom, rhs):
    both = jnp.concatenate([top, bottom], axis=0)
    lane = lanes_of(both)
    both = jnp.where(lane < rhs, both, 0.0)
    one = lane[:1]
    for k in range(0, rhs, 4):
        cols = [jnp.broadcast_to(both[:, k + j : k + j + 1], both.shape) for j in range(4)]
        p = [[cols[j][k + i : k + i + 1] for j in range(4)] for i in range(4)]
        inside = (one >= k) & (one < k + 4)
        rows = [
            jnp.where(inside, jnp.where(one == k + i, -1.0, 0.0), both[k + i : k + i + 1]) for i in range(4)
        ]
        inverse = 1.0 / (p[0][0] * p[1][1] - p[0][1] * p[1][0])

        def upper(x, y):
            return (p[1][1] * x - p[0][1] * y) * inverse, (p[0][0] * y - p[1][0] * x) * inverse

        b_02, b_12 = upper(p[0][2], p[1][2])
        b_03, b_13 = upper(p[0][3], p[1][3])
        r_0, r_1 = upper(rows[0], rows[1])
        s_22 = p[2][2] - p[2][0] * b_02 - p[2][1] * b_12
        s_23 = p[2][3] - p[2][0] * b_03 - p[2][1] * b_13
        s_32 = p[3][2] - p[3][0] * b_02 - p[3][1] * b_12
        s_33 = p[3][3] - p[3][0] * b_03 - p[3][1] * b_13
        inverse_low = 1.0 / (s_22 * s_33 - s_23 * s_32)
        q_2 = rows[2] - p[2][0] * r_0 - p[2][1] * r_1
        q_3 = rows[3] - p[3][0] * r_0 - p[3][1] * r_1
        w_2 = (s_33 * q_2 - s_23 * q_3) * inverse_low
        w_3 = (s_22 * q_3 - s_32 * q_2) * inverse_low
        w_0 = r_0 - b_02 * w_2 - b_03 * w_3
        w_1 = r_1 - b_12 * w_2 - b_13 * w_3
        both = jnp.where((lane >= k) & (lane < k + 4), 0.0, both)
        both = both - cols[0] * w_0 - cols[1] * w_1 - cols[2] * w_2 - cols[3] * w_3
    return both[rhs:, :]


def left_multiply(square, block, rhs):
    return lax.dot_general(square[:, :rhs], block, NN, precision=EXACT, preferred_element_type=F32)


def gram(former, latter):
    return lax.dot_general(former, latter, NT, precision=EXACT, preferred_element_type=F32)


def rows_of(ref, chunks):
    panels, _, rhs, lanes = ref.shape
    return jnp.concatenate([ref[:, c].reshape(panels * rhs, lanes) for c in range(chunks)], axis=1)


def store_message(message_ref, block, rhs, at=0):
    for c in range(block.shape[1] // LANES):
        message_ref[at + c] = block[:, c * LANES : (c + 1) * LANES].astype(message_ref.dtype)


def far_terms(total, panels, turned_ref, places, bases, rhs, chunks):
    rows = jnp.concatenate([rows_of(ref, chunks) for ref in panels], axis=0)
    far = lax.dot_general(rows, turned_ref[...], NN, preferred_element_type=F32)
    at = 0
    for base, ref in zip(bases, panels):
        for i in range(ref.shape[0]):
            total = total + jnp.where(places == base + i, far[at : at + rhs], 0.0)
            at += rhs
    return total


def codes_of(panels_ref, chunks):
    count, held = panels_ref.shape[:2]
    code = jnp.zeros(panels_ref.shape[2:], F32)
    for i in range(count if held > chunks else 0):
        code = code + panels_ref[i, chunks].astype(F32)
    return code


def spread_terms(projected, factors, places, wanted, store, rhs, chunks, extra=None):
    masked = [jnp.where(places == place, projected, 0.0).astype(BF16) for place in wanted]
    masked = jnp.concatenate(masked, axis=0)
    width = factors[0].shape[0]
    step = 2 * LANES
    for block in range(chunks // 2):
        at = slice(block * step, (block + 1) * step)
        moved = sum(
            lax.dot_general(
                masked[:, i * width : (i + 1) * width], ref[:, at], NN, preferred_element_type=F32
            )
            for i, ref in enumerate(factors)
        )
        for i in range(len(wanted)):
            for b in range(2):
                piece = moved[i * rhs : (i + 1) * rhs, b * LANES : (b + 1) * LANES]
                if i == 0 and extra is not None:
                    place = block * step + b * LANES
                    piece = piece + extra[:, place : place + LANES]
                store(i, 2 * block + b, piece)


def open_kernel(rhs, right_side_hbm, message_ref, right_side_ref, sem):
    copy = pltpu.make_async_copy(right_side_hbm, right_side_ref, sem)
    copy.start()
    copy.wait()
    store_message(message_ref, right_side_ref[...], rhs)


def load_kernel(
    rhs, rank, own_ref, column_hbm, live_ref, nugget_hbm, left_hbm,
    nugget_ref, left_ref, named_ref, near_ref, sums_ref,
    column_ref, column_sem, nugget_sem, left_sem,
):
    copies = [
        pltpu.make_async_copy(column_hbm, column_ref, column_sem),
        pltpu.make_async_copy(nugget_hbm, nugget_ref, nugget_sem),
        pltpu.make_async_copy(left_hbm, left_ref, left_sem),
    ]
    for copy in copies:
        copy.start()
    own = own_ref[...]
    for copy in copies[:2]:
        copy.wait()
    slot_of = lax.broadcasted_iota(jnp.int32, (1, named_ref.shape[1]), 1) // rank
    named = jnp.full(slot_of.shape, -1, jnp.int32)
    for s in range(column_ref.shape[0]):
        named = jnp.where(slot_of == s, jnp.where(s < live_ref[0], column_ref[s], -1), named)
    named_ref[...] = jnp.broadcast_to(named, named_ref.shape)
    sums_ref[...] = sums_of([gram(own * nugget_ref[...], own), gram(own, own)], rhs)
    copies[2].wait()
    near = lax.dot_general(own.astype(BF16), left_ref[...], NT, preferred_element_type=F32)
    near_ref[...] = jnp.where(named >= 0, near, 0.0)


def load_add_kernel(
    rhs, chunks, place_of, base, held_ref, near_ref, named_ref, other_named_ref, right_hbm, other_ref,
    part_ref, places_ref, right_ref, turned_ref, right_sem,
):
    copy = pltpu.make_async_copy(right_hbm, right_ref, right_sem)
    copy.start()
    named = jnp.concatenate([named_ref[...], other_named_ref[...]], axis=1)
    offset = named ^ lax.axis_index("row")
    places = jnp.where((named >= 0) & ((offset & 1) == 0), place_of(offset), -1)
    places = jnp.concatenate([places] * (rhs // places.shape[0]), axis=0)
    places_ref[...] = places
    near = near_ref[...]
    total = jnp.concatenate([near, jnp.zeros(near.shape, F32)], axis=1)
    half = other_ref.shape[0]
    turned_ref[:, half:] = other_ref[...].T
    copy.wait()
    turned_ref[:, :half] = right_ref[...].T
    part_ref[...] = far_terms(total, [held_ref], turned_ref, places, [base], rhs, chunks)


def near_add_kernel(
    rhs, chunks, base, held_ref, own_ref, right_side_ref, nugget_ref, left_ref, named_ref, places_ref,
    turned_ref, part_ref, sums_ref,
):
    own = own_ref[...]
    near = lax.dot_general(own.astype(BF16), left_ref[...], NT, preferred_element_type=F32)
    near = jnp.where(named_ref[:1] >= 0, near, 0.0)
    total = jnp.concatenate([near, jnp.zeros(near.shape, F32)], axis=1)
    part_ref[...] = far_terms(total, [held_ref], turned_ref, places_ref[...], [base], rhs, chunks)
    weighted = own * nugget_ref[...]
    code = codes_of(held_ref, chunks)
    none = jnp.zeros((rhs, rhs), F32)
    sums_ref[...] = decode(code, rhs) + sums_of([none, gram(weighted, own), gram(right_side_ref[...], weighted)], rhs)


def add_kernel(
    rhs, chunks, bases, turned_ref, places_ref, part_ref, sums_ref, *rest
):
    *panels, message_ref = rest
    total = far_terms(part_ref[...], panels, turned_ref, places_ref[...], bases, rhs, chunks)
    width = total.shape[1]
    message_ref[:, :width] = total
    message_ref[:, width:] = sums_ref[...] + decode(sum(codes_of(ref, chunks) for ref in panels), rhs)


def both_cores(message_ref, got_ref):
    half = (message_ref.shape[1] - LANES) // 2
    own = message_ref[:, :half] + got_ref[:, half : 2 * half]
    other = message_ref[:, half : 2 * half] + got_ref[:, :half]
    sums = message_ref[:, 2 * half :] + got_ref[:, 2 * half :]
    return jnp.concatenate([own, other], axis=1), sums


def rounded_gram(projected):
    rounded = projected.astype(BF16)
    return lax.dot_general(rounded, rounded, NT, preferred_element_type=F32)


def send_terms(sends, projected, factors, places, wanted, pair, rhs, chunks):
    slots = [(send, i) for send in sends for i in range(send.shape[0] // chunks)]

    def store(i, c, piece):
        send, j = slots[i]
        send[j * chunks + c] = piece.astype(BF16)

    spread_terms(projected, factors, places, wanted, store, rhs, chunks)
    code = encode(pair, rhs)
    for send in sends:
        send[send.shape[0] - 1] = code


def first_kernel(
    rhs, chunks, wanted, message_ref, got_ref, right_ref, other_ref, places_ref,
    pair_ref, projected_ref, sums_ref, *sends,
):
    projected, sums = both_cores(message_ref, got_ref)
    projected_ref[...] = projected
    sums_ref[...] = sums
    pair = sums + sums_of([rounded_gram(projected)], rhs)
    pair_ref[...] = pair
    send_terms(sends, projected, (right_ref, other_ref), places_ref[...], wanted, pair, rhs, chunks)


def second_kernel(
    rhs, chunks, wanted, message_ref, got_ref, right_ref, other_ref, places_ref,
    gram_ref, weighted_ref, earlier_ref,
    pair_ref, projected_ref, next_gram_ref, mix_ref, *sends,
):
    projected, sums = both_cores(message_ref, got_ref)
    next_gram_ref[...] = sums
    mix = right_divide(gram_ref[...], sums, rhs)
    projected = projected + left_multiply(mix, earlier_ref[...], rhs)
    projected_ref[...] = projected
    weighted = left_multiply(mix, jnp.concatenate([sums[:, 2 * rhs : 3 * rhs], weighted_ref[:, :rhs]], axis=1), rhs)
    mixed = weighted[:, :rhs]
    curvature = sums[:, rhs : 2 * rhs] + mixed + mixed.T + gram(weighted[:, rhs:], mix[:, :rhs])
    pair = sums_of([curvature + rounded_gram(projected)], rhs)
    pair_ref[...] = pair
    send_terms(sends, projected, (right_ref, other_ref), places_ref[...], wanted, pair, rhs, chunks)
    mix_ref[...] = mix


def spread_kernel(
    rhs, chunks, wanted, projected_ref, left_ref, right_ref, other_ref, places_ref, pair_ref, keep_ref, *outs
):
    projected = projected_ref[...]
    slots = [(ref, i) for ref in (keep_ref, *outs) for i in range(ref.shape[0] // chunks)]

    def store(i, c, piece):
        ref, j = slots[i]
        ref[j * chunks + c] = piece.astype(ref.dtype)

    own = projected[:, : projected.shape[1] // 2].astype(BF16)
    own = lax.dot_general(own, left_ref[...], NN, preferred_element_type=F32)
    spread_terms(projected, (right_ref, other_ref), places_ref[...], wanted, store, rhs, chunks, own)
    for ref in outs:
        if ref.shape[0] % chunks:
            ref[ref.shape[0] - 1] = encode(pair_ref[...], rhs)


def solution_kernel(rhs, step_ref, right_side_ref, solution_ref):
    solution_ref[...] = left_multiply(step_ref[...], right_side_ref[...], rhs)


def direction_kernel(rhs, mix_ref, right_side_ref, residual_ref, direction_ref):
    direction_ref[...] = residual_ref[...] + left_multiply(mix_ref[...], right_side_ref[...], rhs)


def join_kernel(keep_ref, *rest):
    *got, sum_ref = rest
    total = keep_ref[...]
    for ref in got:
        total = total + ref[...].astype(F32)
    sum_ref[...] = total


def pass_kernel(keep_ref, got_ref, message_ref):
    size = keep_ref.shape[0]
    message_ref[:size] = (keep_ref[...] + got_ref[:size].astype(F32)).astype(BF16)
    message_ref[size] = got_ref[size]


def part_kernel(rhs, keep_ref, pair_ref, got_ref, total_ref, *sends):
    size = sends[0].shape[0] - 1
    total = pair_ref[...] + decode(got_ref[got_ref.shape[0] - 1].astype(F32), rhs)
    total_ref[...] = total
    code = encode(total, rhs)
    for i, send in enumerate(sends):
        at = i * size
        send[:size] = (keep_ref[at : at + size] + got_ref[at : at + size].astype(F32)).astype(BF16)
        send[size] = code


def join_coded_kernel(rhs, keep_ref, pair_ref, *rest):
    *got, sum_ref, total_ref = rest
    size = keep_ref.shape[0]
    total, code = keep_ref[...], jnp.zeros(pair_ref.shape, F32)
    for ref in got:
        total = total + ref[:size].astype(F32)
        code = code + ref[size].astype(F32)
    sum_ref[...] = total
    total_ref[...] = pair_ref[...] + decode(code, rhs)


def message_kernel(rhs, panel_ref, pair_ref, message_ref):
    message_ref[: panel_ref.shape[0]] = panel_ref[...].astype(BF16)
    message_ref[panel_ref.shape[0]] = encode(pair_ref[...], rhs)


def code_kernel(rhs, pair_ref, code_ref):
    code_ref[...] = encode(pair_ref[...], rhs)


def pair_kernel(rhs, pair_ref, got_ref, total_ref):
    total_ref[...] = pair_ref[...] + decode(got_ref[...].astype(F32), rhs)


def gathered_product(keep_ref, pair_ref, got, direction, nugget, rhs, chunks):
    total = keep_ref[...]
    code = jnp.zeros(pair_ref.shape, F32)
    for ref in got:
        total = total + ref[:chunks].astype(F32)
        code = code + ref[chunks].astype(F32)
    applied = nugget * direction + jnp.concatenate([total[c] for c in range(chunks)], axis=1)
    return applied, pair_ref[...] + decode(code, rhs)


def middle_kernel(
    rhs, chunks, direction_ref, nugget_ref, keep_ref, pair_ref, *rest
):
    *got, message_ref, residual_ref, step_ref, gram_ref = rest
    direction = direction_ref[...]
    applied, pair = gathered_product(keep_ref, pair_ref, got, direction, nugget_ref[...], rhs, chunks)
    first_gram = second_of(pair, rhs)
    gram_ref[...] = first_gram
    step = right_divide(pair, first_gram, rhs)
    residual = direction - left_multiply(step, applied, rhs)
    residual_ref[...] = residual
    store_message(message_ref, residual, rhs)
    message_ref[chunks] = encode(sums_of([gram(residual, residual)], rhs), rhs)
    step_ref[...] = step


def last_kernel(
    rhs, chunks, direction_ref, nugget_ref, keep_ref, pair_ref, gram_ref, residual_ref, solution_ref, *rest
):
    *got, out_solution_ref, out_residual_ref = rest
    direction = direction_ref[...]
    applied, pair = gathered_product(keep_ref, pair_ref, got, direction, nugget_ref[...], rhs, chunks)
    step = right_divide(pair, gram_ref[...], rhs)
    out_solution_ref[...] = solution_ref[...] + left_multiply(step, direction, rhs)
    out_residual_ref[...] = residual_ref[...] - left_multiply(step, applied, rhs)


def call(kernel, outs, *args, far=(), scalars=(), fixed=(), scratch=(), micros=0.0):
    whole = pl.BlockSpec(memory_space=pltpu.VMEM)
    spaces = {i: pltpu.HBM for i in far} | {i: pltpu.SMEM for i in scalars}
    return pl.pallas_call(
        kernel,
        out_shape=[
            pltpu.VMEM(shape, dtype) if i in fixed else jax.ShapeDtypeStruct(shape, dtype)
            for i, (shape, dtype) in enumerate(outs)
        ],
        in_specs=[pl.BlockSpec(memory_space=spaces[i]) if i in spaces else whole for i in range(len(args))],
        out_specs=[whole] * len(outs),
        scratch_shapes=list(scratch),
        cost_estimate=pl.CostEstimate(flops=int(micros * 1e9), bytes_accessed=0, transcendentals=0),
        compiler_params=pltpu.CompilerParams(vmem_limit_bytes=32 * 1024 * 1024),
    )(*args)


def after(value, *others):
    return lax.optimization_barrier((value, *others))[0]


def shards(right_sides, nugget, left_factors, right_factors, tile_column, live_slots):
    devices = lax.axis_size("row")
    bits = devices.bit_length() - 1
    low_bits = bits - 2
    slots, rank, width = left_factors.shape
    rhs = right_sides.shape[0]
    chunks = width // LANES
    part = functools.partial

    def swap(array, offset):
        return lax.ppermute(array, "row", [(i, i ^ offset) for i in range(devices)])

    order = (0, 3, 2, 1)
    groups = []
    for k in order:
        group = [k << low_bits]
        for b in range(low_bits - 1, 1, -1):
            group = group + [o | (1 << b) for o in group]
        groups.append(group)
    m = len(groups[0])
    held_offsets = sum(groups, [])
    offsets = held_offsets + [o | 2 for o in held_offsets]
    held, late = 0, 4 * m

    def place_of(offset):
        place = ((4 - (offset >> low_bits)) & 3) * m
        for b in range(low_bits - 1, 1, -1):
            place = place + (((offset >> b) & 1) << (low_bits - 1 - b))
        return place + ((offset >> 1) & 1) * late

    assert [place_of(o) for o in offsets] == list(range(devices // 2))
    stay, go = tuple(range(late + m)), tuple(range(late + m, 2 * late))

    small = ((rhs, LANES), F32)
    panel = ((rhs, width), F32)
    row_block = ((rhs, slots * rank), F32)
    two_rows = ((rhs, 2 * slots * rank), F32)
    core_message = ((rhs, 2 * slots * rank + LANES), F32)
    factor = ((slots * rank, width), BF16)
    semaphore = pltpu.SemaphoreType.DMA

    def plain(count):
        return ((count * chunks, rhs, LANES), BF16)

    def coded(count):
        return ((count * chunks + 1, rhs, LANES), BF16)

    def kept(count):
        return ((count * chunks, rhs, LANES), F32)

    late_sends = [coded(2), coded(1)] if m == 1 else [coded(m)] * 3

    def gather(message, first_terms, *early):
        if m == 1:
            far_3, far_2 = [swap(message, k << low_bits)[None] for k in order[1:3]]
            beside = swap(message[None], 2)
            far_1 = swap(message, order[3] << low_bits)[None]
            last = [
                swap(after(jnp.concatenate([far_3, far_2]), *early), 2),
                swap(beside, order[3] << low_bits),
            ]
            bases = (late, late + 1, late + 3)
            held_panels = jnp.concatenate([message[None], far_3, far_2, far_1])
        else:
            mine = [message[None]] + [swap(message, k << low_bits)[None] for k in order[1:]]
            for b in range(low_bits - 1, 1, -1):
                mine = [jnp.concatenate([g, swap(g, 1 << b)]) for g in mine]
            beside = swap(mine[0], 2)
            last = [swap(jnp.concatenate(mine[1:]), 2)]
            bases = (late, late + m)
            held_panels = jnp.concatenate(mine)
        terms, sums, turned, factors, places = first_terms(held_panels)
        last = [after(x, terms) for x in last]
        (message,) = call(
            part(add_kernel, rhs, chunks, bases), [core_message], turned, places, terms, sums, beside, *last
        )
        return message, swap(message, 1), turned, factors, places

    def reduce(sends, pair, projected, left, factors, places):
        spread = part(spread_kernel, rhs, chunks, stay)
        operands = (projected, left, *factors, places, pair)
        if m == 1:
            got_side = swap(sends[0], 2)
            got_far = swap(sends[1], order[3] << low_bits)
            mine, keep, send, beside = call(spread, [kept(1), kept(2), coded(1), kept(1)], *operands)
            got_1 = swap(send, order[3] << low_bits)
            (send,) = call(pass_kernel, [coded(1)], beside, got_far)
            got_beside = swap(send, 2)
            total, *sends = call(
                part(part_kernel, rhs), [small] + [coded(1)] * 2, keep, pair, after(got_side, send)
            )
            got = [swap(x, k << low_bits) for x, k in zip(sends, order[1:3])]
            mine, pair = call(
                part(join_coded_kernel, rhs), [kept(1), small], mine, total, got_1, got_beside, micros=5.0
            )
            return mine, pair, got
        got = [swap(x, k << low_bits) for x, k in zip(sends, order[1:])]
        keep, *sends, beside = call(spread, [kept(m)] + [plain(m)] * 3 + [kept(m)], *operands)
        got_here = [swap(x, k << low_bits) for x, k in zip(sends, order[1:])]
        turned, pair = call(part(join_coded_kernel, rhs), [kept(m), small], beside, pair, *got)
        (keep,) = call(join_kernel, [kept(m)], keep, *got_here)
        for b in range(2, low_bits):
            (code,) = call(part(code_kernel, rhs), [((rhs, LANES), BF16)], pair)
            (pair,) = call(part(pair_kernel, rhs), [small], pair, swap(code, 1 << b))
            half = keep.shape[0] // 2
            keep, turned = [
                x[:half] + swap(x[half:].astype(BF16), 1 << b).astype(F32) for x in (keep, turned)
            ]
        (turned,) = call(part(message_kernel, rhs), [coded(1)], turned, pair)
        return keep, pair, [swap(turned, 2)]

    def in_hbm(array):
        return pltpu.with_memory_space_constraint(array, pltpu.HBM)

    message, right_sides = call(
        part(open_kernel, rhs), [plain(1), panel], in_hbm(right_sides), far=(0,), fixed=(1,), scratch=[semaphore]
    )
    right = right_factors.reshape(slots * rank, width)
    other = swap(after(right, message), 1)
    named_shape = ((8, slots * rank), jnp.int32)
    nugget, left, named, near, sums = call(
        part(load_kernel, rhs, rank),
        [((1, width), F32), factor, named_shape, row_block, small],
        right_sides, in_hbm(tile_column.reshape(slots)), live_slots, in_hbm(nugget[None, :]),
        in_hbm(left_factors.reshape(slots * rank, width)),
        far=(1, 3, 4), scalars=(2,), fixed=(0, 1), scratch=[pltpu.SMEM((slots,), jnp.int32)] + [semaphore] * 3,
    )
    other_named = swap(named, 1)

    def loading(mine):
        terms, places, here, turned = call(
            part(load_add_kernel, rhs, chunks, place_of, held),
            [two_rows, ((rhs, 2 * slots * rank), jnp.int32), factor, ((width, 2 * slots * rank), BF16)],
            mine, near, named, other_named, in_hbm(right), other,
            far=(4,), fixed=(2, 3), scratch=[semaphore], micros=0.0,
        )
        return terms, sums, turned, (here, other), places

    message, got, turned, factors, places = gather(message, loading, near)
    pair, earlier, weighted, *sends = call(
        part(first_kernel, rhs, chunks, go),
        [small, two_rows, small] + late_sends,
        message, got, *factors, places,
    )
    mine, pair, got = reduce(sends, pair, earlier, left, factors, places)
    message, residual, step, first_gram = call(
        part(middle_kernel, rhs, chunks),
        [coded(1), panel, small, small],
        right_sides, nugget, mine, pair, *got,
    )

    (solution,) = call(part(solution_kernel, rhs), [panel], step, right_sides)

    def loaded(mine):
        terms, sums = call(
            part(near_add_kernel, rhs, chunks, held),
            [two_rows, small],
            after(mine, solution), residual, right_sides, nugget, left, named, places, turned,
            micros=0.0,
        )
        return terms, sums, turned, factors, places

    message, got, *_ = gather(message, loaded)
    pair, projected, next_gram, mix, *sends = call(
        part(second_kernel, rhs, chunks, go),
        [small, two_rows, small, small] + late_sends,
        message, got, *factors, places, first_gram, weighted, earlier,
    )
    (direction,) = call(part(direction_kernel, rhs), [panel], mix, right_sides, residual)
    projected = after(projected, direction)
    mine, pair, got = reduce(sends, pair, projected, left, factors, places)
    return tuple(
        call(
            part(last_kernel, rhs, chunks),
            [panel, panel],
            direction, nugget, mine, pair, next_gram, residual, solution, *got,
        )
    )


def solution(mesh):
    return jax.shard_map(
        shards,
        mesh=mesh,
        in_specs=(
            P(None, ("groups", "row")),
            P(("groups", "row")),
            P(("groups", "row"), None, None),
            P(("groups", "row"), None, None),
            P(("groups", "row"), None),
            P(("groups", "row")),
        ),
        out_specs=(P(None, ("groups", "row")), P(None, ("groups", "row"))),
        check_vma=False,
    )
```

```python
import functools

import jax
import jax.numpy as jnp
from jax import lax
from jax.experimental import pallas as pl
from jax.experimental.pallas import tpu as pltpu
from jax.sharding import PartitionSpec as P

LANES = 128
F32 = jnp.float32
BF16 = jnp.bfloat16
EXACT = lax.Precision.HIGHEST
NN = (((1,), (0,)), ((), ()))
NT = (((1,), (1,)), ((), ()))


def lanes_of(block):
    return lax.broadcasted_iota(jnp.int32, block.shape, len(block.shape) - 1)


def sums_of(parts, rhs):
    rest = jnp.zeros((rhs, LANES - rhs * len(parts)), F32)
    return jnp.concatenate(parts + [rest], axis=1)


def encode(pair, rhs):
    high = pair.astype(BF16).astype(F32)
    rest = pair - high
    middle = rest.astype(BF16).astype(F32)
    low = rest - middle
    return (high + pltpu.roll(middle, 2 * rhs, 1) + pltpu.roll(low, 4 * rhs, 1)).astype(BF16)


def decode(code, rhs):
    total = code + pltpu.roll(code, LANES - 2 * rhs, 1) + pltpu.roll(code, LANES - 4 * rhs, 1)
    return jnp.where(lanes_of(total) < 2 * rhs, total, 0.0)


def second_of(pair, rhs):
    return pltpu.roll(pair, LANES - rhs, 1)


def right_divide(top, bottom, rhs):
    both = jnp.concatenate([top, bottom], axis=0)
    lane = lanes_of(both)
    both = jnp.where(lane < rhs, both, 0.0)
    one = lane[:1]
    for k in range(0, rhs, 4):
        cols = [jnp.broadcast_to(both[:, k + j : k + j + 1], both.shape) for j in range(4)]
        p = [[cols[j][k + i : k + i + 1] for j in range(4)] for i in range(4)]
        inside = (one >= k) & (one < k + 4)
        rows = [
            jnp.where(inside, jnp.where(one == k + i, -1.0, 0.0), both[k + i : k + i + 1]) for i in range(4)
        ]
        inverse = 1.0 / (p[0][0] * p[1][1] - p[0][1] * p[1][0])

        def upper(x, y):
            return (p[1][1] * x - p[0][1] * y) * inverse, (p[0][0] * y - p[1][0] * x) * inverse

        b_02, b_12 = upper(p[0][2], p[1][2])
        b_03, b_13 = upper(p[0][3], p[1][3])
        r_0, r_1 = upper(rows[0], rows[1])
        s_22 = p[2][2] - p[2][0] * b_02 - p[2][1] * b_12
        s_23 = p[2][3] - p[2][0] * b_03 - p[2][1] * b_13
        s_32 = p[3][2] - p[3][0] * b_02 - p[3][1] * b_12
        s_33 = p[3][3] - p[3][0] * b_03 - p[3][1] * b_13
        inverse_low = 1.0 / (s_22 * s_33 - s_23 * s_32)
        q_2 = rows[2] - p[2][0] * r_0 - p[2][1] * r_1
        q_3 = rows[3] - p[3][0] * r_0 - p[3][1] * r_1
        w_2 = (s_33 * q_2 - s_23 * q_3) * inverse_low
        w_3 = (s_22 * q_3 - s_32 * q_2) * inverse_low
        w_0 = r_0 - b_02 * w_2 - b_03 * w_3
        w_1 = r_1 - b_12 * w_2 - b_13 * w_3
        both = jnp.where((lane >= k) & (lane < k + 4), 0.0, both)
        both = both - cols[0] * w_0 - cols[1] * w_1 - cols[2] * w_2 - cols[3] * w_3
    return both[rhs:, :]


def left_multiply(square, block, rhs):
    return lax.dot_general(square[:, :rhs], block, NN, precision=EXACT, preferred_element_type=F32)


def gram(former, latter):
    return lax.dot_general(former, latter, NT, precision=EXACT, preferred_element_type=F32)


def rows_of(ref, chunks):
    panels, _, rhs, lanes = ref.shape
    return jnp.concatenate([ref[:, c].reshape(panels * rhs, lanes) for c in range(chunks)], axis=1)


def store_message(message_ref, block, rhs, at=0):
    for c in range(block.shape[1] // LANES):
        message_ref[at + c] = block[:, c * LANES : (c + 1) * LANES].astype(message_ref.dtype)


def far_terms(total, panels, turned_ref, places, bases, rhs, chunks):
    rows = jnp.concatenate([rows_of(ref, chunks) for ref in panels], axis=0)
    far = lax.dot_general(rows, turned_ref[...], NN, preferred_element_type=F32)
    at = 0
    for base, ref in zip(bases, panels):
        for i in range(ref.shape[0]):
            total = total + jnp.where(places == base + i, far[at : at + rhs], 0.0)
            at += rhs
    return total


def codes_of(panels_ref, chunks):
    count, held = panels_ref.shape[:2]
    code = jnp.zeros(panels_ref.shape[2:], F32)
    for i in range(count if held > chunks else 0):
        code = code + panels_ref[i, chunks].astype(F32)
    return code


def spread_terms(projected, factors, places, wanted, store, rhs, chunks, extra=None):
    masked = [jnp.where(places == place, projected, 0.0).astype(BF16) for place in wanted]
    masked = jnp.concatenate(masked, axis=0)
    width = factors[0].shape[0]
    step = 2 * LANES
    for block in range(chunks // 2):
        at = slice(block * step, (block + 1) * step)
        moved = sum(
            lax.dot_general(
                masked[:, i * width : (i + 1) * width], ref[:, at], NN, preferred_element_type=F32
            )
            for i, ref in enumerate(factors)
        )
        for i in range(len(wanted)):
            for b in range(2):
                piece = moved[i * rhs : (i + 1) * rhs, b * LANES : (b + 1) * LANES]
                if i == 0 and extra is not None:
                    place = block * step + b * LANES
                    piece = piece + extra[:, place : place + LANES]
                store(i, 2 * block + b, piece)


def open_kernel(rhs, right_side_hbm, message_ref, right_side_ref, sem):
    copy = pltpu.make_async_copy(right_side_hbm, right_side_ref, sem)
    copy.start()
    copy.wait()
    store_message(message_ref, right_side_ref[...], rhs)


def load_kernel(
    rhs, rank, own_ref, column_hbm, live_ref, nugget_hbm, left_hbm,
    nugget_ref, left_ref, named_ref, near_ref, sums_ref,
    column_ref, column_sem, nugget_sem, left_sem,
):
    copies = [
        pltpu.make_async_copy(column_hbm, column_ref, column_sem),
        pltpu.make_async_copy(nugget_hbm, nugget_ref, nugget_sem),
        pltpu.make_async_copy(left_hbm, left_ref, left_sem),
    ]
    for copy in copies:
        copy.start()
    own = own_ref[...]
    for copy in copies[:2]:
        copy.wait()
    slot_of = lax.broadcasted_iota(jnp.int32, (1, named_ref.shape[1]), 1) // rank
    named = jnp.full(slot_of.shape, -1, jnp.int32)
    for s in range(column_ref.shape[0]):
        named = jnp.where(slot_of == s, jnp.where(s < live_ref[0], column_ref[s], -1), named)
    named_ref[...] = jnp.broadcast_to(named, named_ref.shape)
    sums_ref[...] = sums_of([gram(own * nugget_ref[...], own), gram(own, own)], rhs)
    copies[2].wait()
    near = lax.dot_general(own.astype(BF16), left_ref[...], NT, preferred_element_type=F32)
    near_ref[...] = jnp.where(named >= 0, near, 0.0)


def load_add_kernel(
    rhs, chunks, place_of, base, held_ref, near_ref, named_ref, other_named_ref, right_hbm, other_ref,
    part_ref, places_ref, right_ref, turned_ref, right_sem,
):
    copy = pltpu.make_async_copy(right_hbm, right_ref, right_sem)
    copy.start()
    named = jnp.concatenate([named_ref[...], other_named_ref[...]], axis=1)
    offset = named ^ lax.axis_index("row")
    places = jnp.where((named >= 0) & ((offset & 1) == 0), place_of(offset), -1)
    places = jnp.concatenate([places] * (rhs // places.shape[0]), axis=0)
    places_ref[...] = places
    near = near_ref[...]
    total = jnp.concatenate([near, jnp.zeros(near.shape, F32)], axis=1)
    half = other_ref.shape[0]
    turned_ref[:, half:] = other_ref[...].T
    copy.wait()
    turned_ref[:, :half] = right_ref[...].T
    part_ref[...] = far_terms(total, [held_ref], turned_ref, places, [base], rhs, chunks)


def near_add_kernel(
    rhs, chunks, base, held_ref, own_ref, right_side_ref, nugget_ref, left_ref, named_ref, places_ref,
    turned_ref, part_ref, sums_ref,
):
    own = own_ref[...]
    near = lax.dot_general(own.astype(BF16), left_ref[...], NT, preferred_element_type=F32)
    near = jnp.where(named_ref[:1] >= 0, near, 0.0)
    total = jnp.concatenate([near, jnp.zeros(near.shape, F32)], axis=1)
    part_ref[...] = far_terms(total, [held_ref], turned_ref, places_ref[...], [base], rhs, chunks)
    weighted = own * nugget_ref[...]
    code = codes_of(held_ref, chunks)
    none = jnp.zeros((rhs, rhs), F32)
    sums_ref[...] = decode(code, rhs) + sums_of([none, gram(weighted, own), gram(right_side_ref[...], weighted)], rhs)


def add_kernel(
    rhs, chunks, bases, turned_ref, places_ref, part_ref, sums_ref, *rest
):
    *panels, message_ref = rest
    total = far_terms(part_ref[...], panels, turned_ref, places_ref[...], bases, rhs, chunks)
    width = total.shape[1]
    message_ref[:, :width] = total
    message_ref[:, width:] = sums_ref[...] + decode(sum(codes_of(ref, chunks) for ref in panels), rhs)


def both_cores(message_ref, got_ref):
    half = (message_ref.shape[1] - LANES) // 2
    own = message_ref[:, :half] + got_ref[:, half : 2 * half]
    other = message_ref[:, half : 2 * half] + got_ref[:, :half]
    sums = message_ref[:, 2 * half :] + got_ref[:, 2 * half :]
    return jnp.concatenate([own, other], axis=1), sums


def rounded_gram(projected):
    rounded = projected.astype(BF16)
    return lax.dot_general(rounded, rounded, NT, preferred_element_type=F32)


def send_terms(sends, projected, factors, places, wanted, pair, rhs, chunks):
    slots = [(send, i) for send in sends for i in range(send.shape[0] // chunks)]

    def store(i, c, piece):
        send, j = slots[i]
        send[j * chunks + c] = piece.astype(BF16)

    spread_terms(projected, factors, places, wanted, store, rhs, chunks)
    code = encode(pair, rhs)
    for send in sends:
        send[send.shape[0] - 1] = code


def first_kernel(
    rhs, chunks, wanted, message_ref, got_ref, right_ref, other_ref, places_ref,
    pair_ref, projected_ref, sums_ref, *sends,
):
    projected, sums = both_cores(message_ref, got_ref)
    projected_ref[...] = projected
    sums_ref[...] = sums
    pair = sums + sums_of([rounded_gram(projected)], rhs)
    pair_ref[...] = pair
    send_terms(sends, projected, (right_ref, other_ref), places_ref[...], wanted, pair, rhs, chunks)


def second_kernel(
    rhs, chunks, wanted, message_ref, got_ref, right_ref, other_ref, places_ref,
    gram_ref, weighted_ref, earlier_ref,
    pair_ref, projected_ref, next_gram_ref, mix_ref, *sends,
):
    projected, sums = both_cores(message_ref, got_ref)
    next_gram_ref[...] = sums
    mix = right_divide(gram_ref[...], sums, rhs)
    projected = projected + left_multiply(mix, earlier_ref[...], rhs)
    projected_ref[...] = projected
    weighted = left_multiply(mix, jnp.concatenate([sums[:, 2 * rhs : 3 * rhs], weighted_ref[:, :rhs]], axis=1), rhs)
    mixed = weighted[:, :rhs]
    curvature = sums[:, rhs : 2 * rhs] + mixed + mixed.T + gram(weighted[:, rhs:], mix[:, :rhs])
    pair = sums_of([curvature + rounded_gram(projected)], rhs)
    pair_ref[...] = pair
    send_terms(sends, projected, (right_ref, other_ref), places_ref[...], wanted, pair, rhs, chunks)
    mix_ref[...] = mix


def spread_kernel(
    rhs, chunks, wanted, projected_ref, left_ref, right_ref, other_ref, places_ref, pair_ref, keep_ref, *outs
):
    projected = projected_ref[...]
    slots = [(ref, i) for ref in (keep_ref, *outs) for i in range(ref.shape[0] // chunks)]

    def store(i, c, piece):
        ref, j = slots[i]
        ref[j * chunks + c] = piece.astype(ref.dtype)

    own = projected[:, : projected.shape[1] // 2].astype(BF16)
    own = lax.dot_general(own, left_ref[...], NN, preferred_element_type=F32)
    spread_terms(projected, (right_ref, other_ref), places_ref[...], wanted, store, rhs, chunks, own)
    for ref in outs:
        if ref.shape[0] % chunks:
            ref[ref.shape[0] - 1] = encode(pair_ref[...], rhs)


def solution_kernel(rhs, step_ref, right_side_ref, solution_ref):
    solution_ref[...] = left_multiply(step_ref[...], right_side_ref[...], rhs)


def direction_kernel(rhs, mix_ref, right_side_ref, residual_ref, direction_ref):
    direction_ref[...] = residual_ref[...] + left_multiply(mix_ref[...], right_side_ref[...], rhs)


def join_kernel(keep_ref, *rest):
    *got, sum_ref = rest
    total = keep_ref[...]
    for ref in got:
        total = total + ref[...].astype(F32)
    sum_ref[...] = total


def pass_kernel(rhs, keep_ref, *rest):
    *got, message_ref = rest
    size = keep_ref.shape[0]
    message_ref[:size] = (keep_ref[...] + sum(ref[:size].astype(F32) for ref in got)).astype(BF16)
    message_ref[size] = encode(decode(sum(ref[size].astype(F32) for ref in got), rhs), rhs)


def part_kernel(rhs, keep_ref, pair_ref, got_ref, total_ref, *sends):
    size = sends[0].shape[0] - 1
    total = pair_ref[...] + decode(got_ref[got_ref.shape[0] - 1].astype(F32), rhs)
    total_ref[...] = total
    code = encode(total, rhs)
    for i, send in enumerate(sends):
        at = i * size
        send[:size] = (keep_ref[at : at + size] + got_ref[at : at + size].astype(F32)).astype(BF16)
        send[size] = code


def join_coded_kernel(rhs, keep_ref, pair_ref, *rest):
    *got, sum_ref, total_ref = rest
    size = keep_ref.shape[0]
    total, code = keep_ref[...], jnp.zeros(pair_ref.shape, F32)
    for ref in got:
        total = total + ref[:size].astype(F32)
        code = code + ref[size].astype(F32)
    sum_ref[...] = total
    total_ref[...] = pair_ref[...] + decode(code, rhs)


def message_kernel(rhs, panel_ref, pair_ref, message_ref):
    message_ref[: panel_ref.shape[0]] = panel_ref[...].astype(BF16)
    message_ref[panel_ref.shape[0]] = encode(pair_ref[...], rhs)


def code_kernel(rhs, pair_ref, code_ref):
    code_ref[...] = encode(pair_ref[...], rhs)


def pair_kernel(rhs, pair_ref, got_ref, total_ref):
    total_ref[...] = pair_ref[...] + decode(got_ref[...].astype(F32), rhs)


def gathered_product(keep_ref, pair_ref, got, direction, nugget, rhs, chunks):
    total = keep_ref[...]
    code = jnp.zeros(pair_ref.shape, F32)
    for ref in got:
        total = total + ref[:chunks].astype(F32)
        code = code + ref[chunks].astype(F32)
    applied = nugget * direction + jnp.concatenate([total[c] for c in range(chunks)], axis=1)
    return applied, pair_ref[...] + decode(code, rhs)


def middle_kernel(
    rhs, chunks, direction_ref, nugget_ref, keep_ref, pair_ref, *rest
):
    *got, message_ref, residual_ref, step_ref, gram_ref = rest
    direction = direction_ref[...]
    applied, pair = gathered_product(keep_ref, pair_ref, got, direction, nugget_ref[...], rhs, chunks)
    first_gram = second_of(pair, rhs)
    gram_ref[...] = first_gram
    step = right_divide(pair, first_gram, rhs)
    residual = direction - left_multiply(step, applied, rhs)
    residual_ref[...] = residual
    store_message(message_ref, residual, rhs)
    message_ref[chunks] = encode(sums_of([gram(residual, residual)], rhs), rhs)
    step_ref[...] = step


def last_kernel(
    rhs, chunks, direction_ref, nugget_ref, keep_ref, pair_ref, gram_ref, residual_ref, solution_ref, *rest
):
    *got, out_solution_ref, out_residual_ref = rest
    direction = direction_ref[...]
    applied, pair = gathered_product(keep_ref, pair_ref, got, direction, nugget_ref[...], rhs, chunks)
    step = right_divide(pair, gram_ref[...], rhs)
    out_solution_ref[...] = solution_ref[...] + left_multiply(step, direction, rhs)
    out_residual_ref[...] = residual_ref[...] - left_multiply(step, applied, rhs)


def call(kernel, outs, *args, far=(), scalars=(), fixed=(), scratch=(), micros=0.0):
    whole = pl.BlockSpec(memory_space=pltpu.VMEM)
    spaces = {i: pltpu.HBM for i in far} | {i: pltpu.SMEM for i in scalars}
    return pl.pallas_call(
        kernel,
        out_shape=[
            pltpu.VMEM(shape, dtype) if i in fixed else jax.ShapeDtypeStruct(shape, dtype)
            for i, (shape, dtype) in enumerate(outs)
        ],
        in_specs=[pl.BlockSpec(memory_space=spaces[i]) if i in spaces else whole for i in range(len(args))],
        out_specs=[whole] * len(outs),
        scratch_shapes=list(scratch),
        cost_estimate=pl.CostEstimate(flops=int(micros * 1e9), bytes_accessed=0, transcendentals=0),
        compiler_params=pltpu.CompilerParams(vmem_limit_bytes=32 * 1024 * 1024),
    )(*args)


def after(value, *others):
    return lax.optimization_barrier((value, *others))[0]


def shards(right_sides, nugget, left_factors, right_factors, tile_column, live_slots):
    devices = lax.axis_size("row")
    bits = devices.bit_length() - 1
    low_bits = bits - 2
    slots, rank, width = left_factors.shape
    rhs = right_sides.shape[0]
    chunks = width // LANES
    part = functools.partial

    def swap(array, offset):
        return lax.ppermute(array, "row", [(i, i ^ offset) for i in range(devices)])

    order = (0, 3, 2, 1)
    groups = []
    for k in order:
        group = [k << low_bits]
        for b in range(low_bits - 1, 1, -1):
            group = group + [o | (1 << b) for o in group]
        groups.append(group)
    m = len(groups[0])
    held_offsets = sum(groups, [])
    offsets = held_offsets + [o | 2 for o in held_offsets]
    held, late = 0, 4 * m

    def place_of(offset):
        place = ((4 - (offset >> low_bits)) & 3) * m
        for b in range(low_bits - 1, 1, -1):
            place = place + (((offset >> b) & 1) << (low_bits - 1 - b))
        return place + ((offset >> 1) & 1) * late

    assert [place_of(o) for o in offsets] == list(range(devices // 2))
    stay, go = tuple(range(late + m)), tuple(range(late + m, 2 * late))

    small = ((rhs, LANES), F32)
    panel = ((rhs, width), F32)
    row_block = ((rhs, slots * rank), F32)
    two_rows = ((rhs, 2 * slots * rank), F32)
    core_message = ((rhs, 2 * slots * rank + LANES), F32)
    factor = ((slots * rank, width), BF16)
    semaphore = pltpu.SemaphoreType.DMA

    def plain(count):
        return ((count * chunks, rhs, LANES), BF16)

    def coded(count):
        return ((count * chunks + 1, rhs, LANES), BF16)

    def kept(count):
        return ((count * chunks, rhs, LANES), F32)

    late_sends = [coded(m)] * 3

    def gather(message, first_terms, *early):
        if m == 1:
            far_3, far_2 = [swap(message, k << low_bits)[None] for k in order[1:3]]
            beside = swap(message[None], 2)
            far_1 = swap(message, order[3] << low_bits)[None]
            last = [
                swap(after(jnp.concatenate([far_3, far_2]), *early), 2),
                swap(beside, order[3] << low_bits),
            ]
            bases = (late, late + 1, late + 3)
            held_panels = jnp.concatenate([message[None], far_3, far_2, far_1])
        else:
            mine = [message[None]] + [swap(message, k << low_bits)[None] for k in order[1:]]
            for b in range(low_bits - 1, 1, -1):
                mine = [jnp.concatenate([g, swap(g, 1 << b)]) for g in mine]
            beside = swap(mine[0], 2)
            last = [swap(jnp.concatenate(mine[1:]), 2)]
            bases = (late, late + m)
            held_panels = jnp.concatenate(mine)
        terms, sums, turned, factors, places = first_terms(held_panels)
        last = [after(x, terms) for x in last]
        (message,) = call(
            part(add_kernel, rhs, chunks, bases), [core_message], turned, places, terms, sums, beside, *last
        )
        return message, swap(message, 1), turned, factors, places

    def reduce(sends, pair, projected, left, factors, places, *early):
        spread = part(spread_kernel, rhs, chunks, stay)
        operands = (projected, left, *factors, places, pair)
        if m == 1:
            got_side = swap(sends[0], 2)
            got_far = [swap(sends[i], order[i + 1] << low_bits) for i in (1, 2)]
            mine, keep, *sends, beside = call(spread, [kept(1)] * 2 + [coded(1)] * 2 + [kept(1)], *operands)
            got_here = [swap(sends[i - 1], order[i + 1] << low_bits) for i in (1, 2)]
            pair, send = call(part(part_kernel, rhs), [small, coded(1)], keep, pair, got_side)
            got_last = swap(send, order[1] << low_bits)
            (send,) = call(part(pass_kernel, rhs), [coded(1)], beside, *got_far)
            got_beside = swap(send, 2)
            join = part(join_coded_kernel, rhs)
            mine, pair = call(join, [kept(1), small], after(mine, *early), pair, *got_here, micros=0.3)
            mine, pair = call(join, [kept(1), small], mine, pair, got_last, micros=0.3)
            return mine, pair, [got_beside]
        got = [swap(x, k << low_bits) for x, k in zip(sends, order[1:])]
        keep, *sends, beside = call(spread, [kept(m)] + [plain(m)] * 3 + [kept(m)], *operands)
        got_here = [swap(x, k << low_bits) for x, k in zip(sends, order[1:])]
        turned, pair = call(part(join_coded_kernel, rhs), [kept(m), small], beside, pair, *got)
        (keep,) = call(join_kernel, [kept(m)], after(keep, *early), *got_here)
        for b in range(2, low_bits):
            (code,) = call(part(code_kernel, rhs), [((rhs, LANES), BF16)], pair)
            (pair,) = call(part(pair_kernel, rhs), [small], pair, swap(code, 1 << b))
            half = keep.shape[0] // 2
            keep, turned = [
                x[:half] + swap(x[half:].astype(BF16), 1 << b).astype(F32) for x in (keep, turned)
            ]
        (turned,) = call(part(message_kernel, rhs), [coded(1)], turned, pair)
        return keep, pair, [swap(turned, 2)]

    def in_hbm(array):
        return pltpu.with_memory_space_constraint(array, pltpu.HBM)

    message, right_sides = call(
        part(open_kernel, rhs), [plain(1), panel], in_hbm(right_sides), far=(0,), fixed=(1,), scratch=[semaphore]
    )
    right = right_factors.reshape(slots * rank, width)
    other = swap(after(right, message), 1)
    named_shape = ((8, slots * rank), jnp.int32)
    nugget, left, named, near, sums = call(
        part(load_kernel, rhs, rank),
        [((1, width), F32), factor, named_shape, row_block, small],
        right_sides, in_hbm(tile_column.reshape(slots)), live_slots, in_hbm(nugget[None, :]),
        in_hbm(left_factors.reshape(slots * rank, width)),
        far=(1, 3, 4), scalars=(2,), fixed=(0, 1), scratch=[pltpu.SMEM((slots,), jnp.int32)] + [semaphore] * 3,
    )
    other_named = swap(named, 1)

    def loading(mine):
        terms, places, here, turned = call(
            part(load_add_kernel, rhs, chunks, place_of, held),
            [two_rows, ((rhs, 2 * slots * rank), jnp.int32), factor, ((width, 2 * slots * rank), BF16)],
            mine, near, named, other_named, in_hbm(right), other,
            far=(4,), fixed=(2, 3), scratch=[semaphore], micros=0.0,
        )
        return terms, sums, turned, (here, other), places

    message, got, turned, factors, places = gather(message, loading, near)
    pair, earlier, weighted, *sends = call(
        part(first_kernel, rhs, chunks, go),
        [small, two_rows, small] + late_sends,
        message, got, *factors, places,
    )
    mine, pair, got = reduce(sends, pair, earlier, left, factors, places)
    message, residual, step, first_gram = call(
        part(middle_kernel, rhs, chunks),
        [coded(1), panel, small, small],
        right_sides, nugget, mine, pair, *got,
    )

    (solution,) = call(part(solution_kernel, rhs), [panel], step, right_sides)

    def loaded(mine):
        terms, sums = call(
            part(near_add_kernel, rhs, chunks, held),
            [two_rows, small],
            after(mine, solution), residual, right_sides, nugget, left, named, places, turned,
            micros=0.0,
        )
        return terms, sums, turned, factors, places

    message, got, *_ = gather(message, loaded)
    pair, projected, next_gram, mix, *sends = call(
        part(second_kernel, rhs, chunks, go),
        [small, two_rows, small, small] + late_sends,
        message, got, *factors, places, first_gram, weighted, earlier,
    )
    (direction,) = call(part(direction_kernel, rhs), [panel], mix, right_sides, residual)
    mine, pair, got = reduce(sends, pair, projected, left, factors, places, direction)
    return tuple(
        call(
            part(last_kernel, rhs, chunks),
            [panel, panel],
            direction, nugget, mine, pair, next_gram, residual, solution, *got,
        )
    )


def solution(mesh):
    return jax.shard_map(
        shards,
        mesh=mesh,
        in_specs=(
            P(None, ("groups", "row")),
            P(("groups", "row")),
            P(("groups", "row"), None, None),
            P(("groups", "row"), None, None),
            P(("groups", "row"), None),
            P(("groups", "row")),
        ),
        out_specs=(P(None, ("groups", "row")), P(None, ("groups", "row"))),
        check_vma=False,
    )
```

```python
import functools

import jax
import jax.numpy as jnp
from jax import lax
from jax.experimental import pallas as pl
from jax.experimental.pallas import tpu as pltpu
from jax.sharding import PartitionSpec as P

LANES = 128
F32 = jnp.float32
BF16 = jnp.bfloat16
EXACT = lax.Precision.HIGHEST
NN = (((1,), (0,)), ((), ()))
NT = (((1,), (1,)), ((), ()))


def lanes_of(block):
    return lax.broadcasted_iota(jnp.int32, block.shape, len(block.shape) - 1)


def sums_of(parts, rhs):
    rest = jnp.zeros((rhs, LANES - rhs * len(parts)), F32)
    return jnp.concatenate(parts + [rest], axis=1)


def encode(pair, rhs):
    high = pair.astype(BF16).astype(F32)
    rest = pair - high
    middle = rest.astype(BF16).astype(F32)
    low = rest - middle
    return (high + pltpu.roll(middle, 2 * rhs, 1) + pltpu.roll(low, 4 * rhs, 1)).astype(BF16)


def decode(code, rhs):
    total = code + pltpu.roll(code, LANES - 2 * rhs, 1) + pltpu.roll(code, LANES - 4 * rhs, 1)
    return jnp.where(lanes_of(total) < 2 * rhs, total, 0.0)


def second_of(pair, rhs):
    return pltpu.roll(pair, LANES - rhs, 1)


def right_divide(top, bottom, rhs):
    both = jnp.concatenate([top, bottom], axis=0)
    lane = lanes_of(both)
    both = jnp.where(lane < rhs, both, 0.0)
    one = lane[:1]
    for k in range(0, rhs, 4):
        cols = [jnp.broadcast_to(both[:, k + j : k + j + 1], both.shape) for j in range(4)]
        p = [[cols[j][k + i : k + i + 1] for j in range(4)] for i in range(4)]
        inside = (one >= k) & (one < k + 4)
        rows = [
            jnp.where(inside, jnp.where(one == k + i, -1.0, 0.0), both[k + i : k + i + 1]) for i in range(4)
        ]
        inverse = 1.0 / (p[0][0] * p[1][1] - p[0][1] * p[1][0])

        def upper(x, y):
            return (p[1][1] * x - p[0][1] * y) * inverse, (p[0][0] * y - p[1][0] * x) * inverse

        b_02, b_12 = upper(p[0][2], p[1][2])
        b_03, b_13 = upper(p[0][3], p[1][3])
        r_0, r_1 = upper(rows[0], rows[1])
        s_22 = p[2][2] - p[2][0] * b_02 - p[2][1] * b_12
        s_23 = p[2][3] - p[2][0] * b_03 - p[2][1] * b_13
        s_32 = p[3][2] - p[3][0] * b_02 - p[3][1] * b_12
        s_33 = p[3][3] - p[3][0] * b_03 - p[3][1] * b_13
        inverse_low = 1.0 / (s_22 * s_33 - s_23 * s_32)
        q_2 = rows[2] - p[2][0] * r_0 - p[2][1] * r_1
        q_3 = rows[3] - p[3][0] * r_0 - p[3][1] * r_1
        w_2 = (s_33 * q_2 - s_23 * q_3) * inverse_low
        w_3 = (s_22 * q_3 - s_32 * q_2) * inverse_low
        w_0 = r_0 - b_02 * w_2 - b_03 * w_3
        w_1 = r_1 - b_12 * w_2 - b_13 * w_3
        both = jnp.where((lane >= k) & (lane < k + 4), 0.0, both)
        both = both - cols[0] * w_0 - cols[1] * w_1 - cols[2] * w_2 - cols[3] * w_3
    return both[rhs:, :]


def left_multiply(square, block, rhs):
    return lax.dot_general(square[:, :rhs], block, NN, precision=EXACT, preferred_element_type=F32)


def gram(former, latter):
    return lax.dot_general(former, latter, NT, precision=EXACT, preferred_element_type=F32)


def rows_of(ref, chunks):
    panels, _, rhs, lanes = ref.shape
    return jnp.concatenate([ref[:, c].reshape(panels * rhs, lanes) for c in range(chunks)], axis=1)


def store_message(message_ref, block, rhs, at=0):
    for c in range(block.shape[1] // LANES):
        message_ref[at + c] = block[:, c * LANES : (c + 1) * LANES].astype(message_ref.dtype)


def far_terms(total, panels, turned_ref, places, bases, rhs, chunks):
    rows = jnp.concatenate([rows_of(ref, chunks) for ref in panels], axis=0)
    far = lax.dot_general(rows, turned_ref[...], NN, preferred_element_type=F32)
    at = 0
    for base, ref in zip(bases, panels):
        for i in range(ref.shape[0]):
            total = total + jnp.where(places == base + i, far[at : at + rhs], 0.0)
            at += rhs
    return total


def codes_of(panels_ref, chunks):
    count, held = panels_ref.shape[:2]
    code = jnp.zeros(panels_ref.shape[2:], F32)
    for i in range(count if held > chunks else 0):
        code = code + panels_ref[i, chunks].astype(F32)
    return code


def spread_terms(projected, factors, places, wanted, store, rhs, chunks):
    masked = [jnp.where(places == place, projected, 0.0).astype(BF16) for place in wanted]
    masked = jnp.concatenate(masked, axis=0)
    width = factors[0].shape[0]
    step = 2 * LANES
    for block in range(chunks // 2):
        at = slice(block * step, (block + 1) * step)
        moved = sum(
            lax.dot_general(
                masked[:, i * width : (i + 1) * width], ref[:, at], NN, preferred_element_type=F32
            )
            for i, ref in enumerate(factors)
        )
        for i in range(len(wanted)):
            for b in range(2):
                piece = moved[i * rhs : (i + 1) * rhs, b * LANES : (b + 1) * LANES]
                store(i, 2 * block + b, piece)


def open_kernel(rhs, right_side_hbm, message_ref, right_side_ref, sem):
    copy = pltpu.make_async_copy(right_side_hbm, right_side_ref, sem)
    copy.start()
    copy.wait()
    store_message(message_ref, right_side_ref[...], rhs)


def load_kernel(
    rhs, rank, own_ref, column_hbm, live_ref, nugget_hbm, left_hbm, right_hbm,
    nugget_ref, left_ref, right_ref, named_ref, near_ref, sums_ref,
    column_ref, column_sem, nugget_sem, left_sem, right_sem,
):
    copies = [
        pltpu.make_async_copy(column_hbm, column_ref, column_sem),
        pltpu.make_async_copy(nugget_hbm, nugget_ref, nugget_sem),
        pltpu.make_async_copy(left_hbm, left_ref, left_sem),
        pltpu.make_async_copy(right_hbm, right_ref, right_sem),
    ]
    for copy in copies:
        copy.start()
    own = own_ref[...]
    for copy in copies[:2]:
        copy.wait()
    slot_of = lax.broadcasted_iota(jnp.int32, (1, named_ref.shape[1]), 1) // rank
    named = jnp.full(slot_of.shape, -1, jnp.int32)
    for s in range(column_ref.shape[0]):
        named = jnp.where(slot_of == s, jnp.where(s < live_ref[0], column_ref[s], -1), named)
    named_ref[...] = jnp.broadcast_to(named, named_ref.shape)
    sums_ref[...] = sums_of([gram(own * nugget_ref[...], own), gram(own, own)], rhs)
    copies[2].wait()
    near = lax.dot_general(own.astype(BF16), left_ref[...], NT, preferred_element_type=F32)
    near_ref[...] = jnp.where(named >= 0, near, 0.0)
    copies[3].wait()


def load_add_kernel(
    rhs, chunks, place_of, base, held_ref, near_ref, named_ref, other_named_ref, right_ref, other_ref,
    part_ref, places_ref, turned_ref,
):
    named = jnp.concatenate([named_ref[...], other_named_ref[...]], axis=1)
    offset = named ^ lax.axis_index("row")
    places = jnp.where((named >= 0) & ((offset & 1) == 0), place_of(offset), -1)
    places = jnp.concatenate([places] * (rhs // places.shape[0]), axis=0)
    places_ref[...] = places
    near = near_ref[...]
    total = jnp.concatenate([near, jnp.zeros(near.shape, F32)], axis=1)
    half = other_ref.shape[0]
    turned_ref[:, half:] = other_ref[...].T
    turned_ref[:, :half] = right_ref[...].T
    part_ref[...] = far_terms(total, [held_ref], turned_ref, places, [base], rhs, chunks)


def near_add_kernel(
    rhs, chunks, base, held_ref, own_ref, right_side_ref, nugget_ref, left_ref, named_ref, places_ref,
    turned_ref, part_ref, sums_ref,
):
    own = own_ref[...]
    near = lax.dot_general(own.astype(BF16), left_ref[...], NT, preferred_element_type=F32)
    near = jnp.where(named_ref[:1] >= 0, near, 0.0)
    total = jnp.concatenate([near, jnp.zeros(near.shape, F32)], axis=1)
    part_ref[...] = far_terms(total, [held_ref], turned_ref, places_ref[...], [base], rhs, chunks)
    weighted = own * nugget_ref[...]
    code = codes_of(held_ref, chunks)
    none = jnp.zeros((rhs, rhs), F32)
    sums_ref[...] = decode(code, rhs) + sums_of([none, gram(weighted, own), gram(right_side_ref[...], weighted)], rhs)


def add_kernel(
    rhs, chunks, bases, turned_ref, places_ref, part_ref, sums_ref, *rest
):
    *panels, message_ref = rest
    total = far_terms(part_ref[...], panels, turned_ref, places_ref[...], bases, rhs, chunks)
    width = total.shape[1]
    message_ref[:, :width] = total
    message_ref[:, width:] = sums_ref[...] + decode(sum(codes_of(ref, chunks) for ref in panels), rhs)


def both_cores(message_ref, got_ref):
    half = (message_ref.shape[1] - LANES) // 2
    own = message_ref[:, :half] + got_ref[:, half : 2 * half]
    other = message_ref[:, half : 2 * half] + got_ref[:, :half]
    sums = message_ref[:, 2 * half :] + got_ref[:, 2 * half :]
    return jnp.concatenate([own, other], axis=1), sums


def rounded_gram(projected):
    rounded = projected.astype(BF16)
    return lax.dot_general(rounded, rounded, NT, preferred_element_type=F32)


def send_terms(outs, projected, factors, places, wanted, pair, rhs, chunks):
    slots = [(ref, i) for ref in outs for i in range(ref.shape[0] // chunks)]

    def store(i, c, piece):
        ref, j = slots[i]
        ref[j * chunks + c] = piece.astype(ref.dtype)

    spread_terms(projected, factors, places, wanted, store, rhs, chunks)
    code = encode(pair, rhs)
    for ref in outs:
        if ref.shape[0] % chunks:
            ref[ref.shape[0] - 1] = code


def first_kernel(
    rhs, chunks, wanted, message_ref, got_ref, right_ref, other_ref, places_ref,
    pair_ref, projected_ref, sums_ref, *sends,
):
    projected, sums = both_cores(message_ref, got_ref)
    projected_ref[...] = projected
    sums_ref[...] = sums
    pair = sums + sums_of([rounded_gram(projected)], rhs)
    pair_ref[...] = pair
    send_terms(sends, projected, (right_ref, other_ref), places_ref[...], wanted, pair, rhs, chunks)


def second_kernel(
    rhs, chunks, wanted, message_ref, got_ref, right_ref, other_ref, places_ref,
    gram_ref, weighted_ref, earlier_ref,
    pair_ref, projected_ref, next_gram_ref, mix_ref, *sends,
):
    projected, sums = both_cores(message_ref, got_ref)
    next_gram_ref[...] = sums
    mix = right_divide(gram_ref[...], sums, rhs)
    projected = projected + left_multiply(mix, earlier_ref[...], rhs)
    projected_ref[...] = projected
    weighted = left_multiply(mix, jnp.concatenate([sums[:, 2 * rhs : 3 * rhs], weighted_ref[:, :rhs]], axis=1), rhs)
    mixed = weighted[:, :rhs]
    curvature = sums[:, rhs : 2 * rhs] + mixed + mixed.T + gram(weighted[:, rhs:], mix[:, :rhs])
    pair = sums_of([curvature + rounded_gram(projected)], rhs)
    pair_ref[...] = pair
    send_terms(sends, projected, (right_ref, other_ref), places_ref[...], wanted, pair, rhs, chunks)
    mix_ref[...] = mix


def solution_kernel(rhs, step_ref, right_side_ref, solution_ref):
    solution_ref[...] = left_multiply(step_ref[...], right_side_ref[...], rhs)


def direction_kernel(rhs, mix_ref, right_side_ref, residual_ref, direction_ref):
    direction_ref[...] = residual_ref[...] + left_multiply(mix_ref[...], right_side_ref[...], rhs)


def join_kernel(keep_ref, *rest):
    *got, sum_ref = rest
    total = keep_ref[...]
    for ref in got:
        total = total + ref[...].astype(F32)
    sum_ref[...] = total


def pass_kernel(rhs, keep_ref, *rest):
    *got, message_ref = rest
    size = keep_ref.shape[0]
    message_ref[:size] = (keep_ref[...] + sum(ref[:size].astype(F32) for ref in got)).astype(BF16)
    message_ref[size] = encode(decode(sum(ref[size].astype(F32) for ref in got), rhs), rhs)


def part_kernel(rhs, keep_ref, pair_ref, got_ref, total_ref, *sends):
    size = sends[0].shape[0] - 1
    total = pair_ref[...] + decode(got_ref[got_ref.shape[0] - 1].astype(F32), rhs)
    total_ref[...] = total
    code = encode(total, rhs)
    for i, send in enumerate(sends):
        at = i * size
        send[:size] = (keep_ref[at : at + size] + got_ref[at : at + size].astype(F32)).astype(BF16)
        send[size] = code


def own_kernel(rhs, chunks, projected_ref, left_ref, keep_ref, *rest):
    *_, sum_ref, total_ref = rest
    join_coded_kernel(rhs, keep_ref, *rest)
    own = projected_ref[:, : left_ref.shape[0]].astype(BF16)
    own = lax.dot_general(own, left_ref[...], NN, preferred_element_type=F32)
    for c in range(chunks):
        sum_ref[c] = sum_ref[c] + own[:, c * LANES : (c + 1) * LANES]


def join_coded_kernel(rhs, keep_ref, pair_ref, *rest):
    *got, sum_ref, total_ref = rest
    size = keep_ref.shape[0]
    total, code = keep_ref[...], jnp.zeros(pair_ref.shape, F32)
    for ref in got:
        total = total + ref[:size].astype(F32)
        code = code + ref[size].astype(F32)
    sum_ref[...] = total
    total_ref[...] = pair_ref[...] + decode(code, rhs)


def message_kernel(rhs, panel_ref, pair_ref, message_ref):
    message_ref[: panel_ref.shape[0]] = panel_ref[...].astype(BF16)
    message_ref[panel_ref.shape[0]] = encode(pair_ref[...], rhs)


def code_kernel(rhs, pair_ref, code_ref):
    code_ref[...] = encode(pair_ref[...], rhs)


def pair_kernel(rhs, pair_ref, got_ref, total_ref):
    total_ref[...] = pair_ref[...] + decode(got_ref[...].astype(F32), rhs)


def gathered_product(keep_ref, pair_ref, got, direction, nugget, rhs, chunks):
    total = keep_ref[...]
    code = jnp.zeros(pair_ref.shape, F32)
    for ref in got:
        total = total + ref[:chunks].astype(F32)
        code = code + ref[chunks].astype(F32)
    applied = nugget * direction + jnp.concatenate([total[c] for c in range(chunks)], axis=1)
    return applied, pair_ref[...] + decode(code, rhs)


def middle_kernel(
    rhs, chunks, direction_ref, nugget_ref, keep_ref, pair_ref, *rest
):
    *got, message_ref, residual_ref, step_ref, gram_ref = rest
    direction = direction_ref[...]
    applied, pair = gathered_product(keep_ref, pair_ref, got, direction, nugget_ref[...], rhs, chunks)
    first_gram = second_of(pair, rhs)
    gram_ref[...] = first_gram
    step = right_divide(pair, first_gram, rhs)
    residual = direction - left_multiply(step, applied, rhs)
    residual_ref[...] = residual
    store_message(message_ref, residual, rhs)
    message_ref[chunks] = encode(sums_of([gram(residual, residual)], rhs), rhs)
    step_ref[...] = step


def last_kernel(
    rhs, chunks, direction_ref, nugget_ref, keep_ref, pair_ref, gram_ref, residual_ref, solution_ref, *rest
):
    *got, out_solution_ref, out_residual_ref = rest
    direction = direction_ref[...]
    applied, pair = gathered_product(keep_ref, pair_ref, got, direction, nugget_ref[...], rhs, chunks)
    step = right_divide(pair, gram_ref[...], rhs)
    out_solution_ref[...] = solution_ref[...] + left_multiply(step, direction, rhs)
    out_residual_ref[...] = residual_ref[...] - left_multiply(step, applied, rhs)


def call(kernel, outs, *args, far=(), scalars=(), fixed=(), scratch=(), micros=0.0):
    whole = pl.BlockSpec(memory_space=pltpu.VMEM)
    spaces = {i: pltpu.HBM for i in far} | {i: pltpu.SMEM for i in scalars}
    return pl.pallas_call(
        kernel,
        out_shape=[
            pltpu.VMEM(shape, dtype) if i in fixed else jax.ShapeDtypeStruct(shape, dtype)
            for i, (shape, dtype) in enumerate(outs)
        ],
        in_specs=[pl.BlockSpec(memory_space=spaces[i]) if i in spaces else whole for i in range(len(args))],
        out_specs=[whole] * len(outs),
        scratch_shapes=list(scratch),
        cost_estimate=pl.CostEstimate(flops=int(micros * 1e9), bytes_accessed=0, transcendentals=0),
        compiler_params=pltpu.CompilerParams(vmem_limit_bytes=32 * 1024 * 1024),
    )(*args)


def after(value, *others):
    return lax.optimization_barrier((value, *others))[0]


def shards(right_sides, nugget, left_factors, right_factors, tile_column, live_slots):
    devices = lax.axis_size("row")
    bits = devices.bit_length() - 1
    low_bits = bits - 2
    slots, rank, width = left_factors.shape
    rhs = right_sides.shape[0]
    chunks = width // LANES
    part = functools.partial

    def swap(array, offset):
        return lax.ppermute(array, "row", [(i, i ^ offset) for i in range(devices)])

    order = (0, 3, 2, 1)
    groups = []
    for k in order:
        group = [k << low_bits]
        for b in range(low_bits - 1, 1, -1):
            group = group + [o | (1 << b) for o in group]
        groups.append(group)
    m = len(groups[0])
    held_offsets = sum(groups, [])
    offsets = held_offsets + [o | 2 for o in held_offsets]
    held, late = 0, 4 * m

    def place_of(offset):
        place = ((4 - (offset >> low_bits)) & 3) * m
        for b in range(low_bits - 1, 1, -1):
            place = place + (((offset >> b) & 1) << (low_bits - 1 - b))
        return place + ((offset >> 1) & 1) * late

    assert [place_of(o) for o in offsets] == list(range(devices // 2))
    stay, go = tuple(range(late + m)), tuple(range(late + m, 2 * late))

    small = ((rhs, LANES), F32)
    panel = ((rhs, width), F32)
    row_block = ((rhs, slots * rank), F32)
    two_rows = ((rhs, 2 * slots * rank), F32)
    core_message = ((rhs, 2 * slots * rank + LANES), F32)
    factor = ((slots * rank, width), BF16)
    semaphore = pltpu.SemaphoreType.DMA

    def plain(count):
        return ((count * chunks, rhs, LANES), BF16)

    def coded(count):
        return ((count * chunks + 1, rhs, LANES), BF16)

    def kept(count):
        return ((count * chunks, rhs, LANES), F32)

    sent = [coded(m)] * 3 + ([kept(1)] * 2 + [coded(1)] * 2 if m == 1 else [kept(m)] + [plain(m)] * 3) + [kept(m)]

    def gather(message, first_terms, *early):
        if m == 1:
            far_3, far_2 = [swap(message, k << low_bits)[None] for k in order[1:3]]
            beside = swap(message[None], 2)
            far_1 = swap(message, order[3] << low_bits)[None]
            last = [
                swap(after(jnp.concatenate([far_3, far_2]), *early), 2),
                swap(beside, order[3] << low_bits),
            ]
            bases = (late, late + 1, late + 3)
            held_panels = jnp.concatenate([message[None], far_3, far_2, far_1])
        else:
            mine = [message[None]] + [swap(message, k << low_bits)[None] for k in order[1:]]
            for b in range(low_bits - 1, 1, -1):
                mine = [jnp.concatenate([g, swap(g, 1 << b)]) for g in mine]
            beside = swap(mine[0], 2)
            last = [swap(jnp.concatenate(mine[1:]), 2)]
            bases = (late, late + m)
            held_panels = jnp.concatenate(mine)
        terms, sums, turned, factors, places = first_terms(held_panels)
        last = [after(x, terms) for x in last]
        (message,) = call(
            part(add_kernel, rhs, chunks, bases), [core_message], turned, places, terms, sums, beside, *last
        )
        return message, swap(message, 1), turned, factors, places

    def reduce(sends, pair, projected, left, *early):
        sends, stays = sends[:3], sends[3:]
        if m == 1:
            got_side = swap(sends[0], 2)
            got_far = [swap(sends[i], order[i + 1] << low_bits) for i in (1, 2)]
            mine, keep, *sends, beside = stays
            got_here = [swap(sends[i - 1], order[i + 1] << low_bits) for i in (1, 2)]
            pair, send = call(part(part_kernel, rhs), [small, coded(1)], keep, pair, got_side)
            got_last = swap(send, order[1] << low_bits)
            (send,) = call(part(pass_kernel, rhs), [coded(1)], beside, *got_far)
            got_beside = swap(send, 2)
            join = part(join_coded_kernel, rhs)
            mine, pair = call(
                part(own_kernel, rhs, chunks), [kept(1), small],
                projected, left, after(mine, *early), pair, *got_here,
                micros=0.3,
            )
            mine, pair = call(join, [kept(1), small], mine, pair, got_last, micros=0.3)
            return mine, pair, [got_beside]
        got = [swap(x, k << low_bits) for x, k in zip(sends, order[1:])]
        keep, *sends, beside = stays
        got_here = [swap(x, k << low_bits) for x, k in zip(sends, order[1:])]
        turned, pair = call(part(join_coded_kernel, rhs), [kept(m), small], beside, pair, *got)
        (keep,) = call(join_kernel, [kept(m)], after(keep, *early), *got_here)
        for b in range(2, low_bits):
            (code,) = call(part(code_kernel, rhs), [((rhs, LANES), BF16)], pair)
            (pair,) = call(part(pair_kernel, rhs), [small], pair, swap(code, 1 << b))
            half = keep.shape[0] // 2
            keep, turned = [
                x[:half] + swap(x[half:].astype(BF16), 1 << b).astype(F32) for x in (keep, turned)
            ]
        (turned,) = call(part(message_kernel, rhs), [coded(1)], turned, pair)
        keep, pair = call(part(own_kernel, rhs, chunks), [kept(1), small], projected, left, keep, pair)
        return keep, pair, [swap(turned, 2)]

    def in_hbm(array):
        return pltpu.with_memory_space_constraint(array, pltpu.HBM)

    message, right_sides = call(
        part(open_kernel, rhs), [plain(1), panel], in_hbm(right_sides), far=(0,), fixed=(1,), scratch=[semaphore]
    )
    right = right_factors.reshape(slots * rank, width)
    other = swap(after(right, message), 1)
    named_shape = ((8, slots * rank), jnp.int32)
    nugget, left, here, named, near, sums = call(
        part(load_kernel, rhs, rank),
        [((1, width), F32), factor, factor, named_shape, row_block, small],
        right_sides, in_hbm(tile_column.reshape(slots)), live_slots, in_hbm(nugget[None, :]),
        in_hbm(left_factors.reshape(slots * rank, width)), in_hbm(right),
        far=(1, 3, 4, 5), scalars=(2,), fixed=(0, 1, 2), scratch=[pltpu.SMEM((slots,), jnp.int32)] + [semaphore] * 4,
    )
    other_named = swap(named, 1)

    def loading(mine):
        terms, places, turned = call(
            part(load_add_kernel, rhs, chunks, place_of, held),
            [two_rows, ((rhs, 2 * slots * rank), jnp.int32), ((width, 2 * slots * rank), BF16)],
            mine, near, named, other_named, here, other,
            fixed=(2,),
        )
        return terms, sums, turned, (here, other), places

    message, got, turned, factors, places = gather(message, loading, near)
    pair, earlier, weighted, *sends = call(
        part(first_kernel, rhs, chunks, go + stay),
        [small, two_rows, small] + sent,
        message, got, *factors, places,
    )
    mine, pair, got = reduce(sends, pair, earlier, left)
    message, residual, step, first_gram = call(
        part(middle_kernel, rhs, chunks),
        [coded(1), panel, small, small],
        right_sides, nugget, mine, pair, *got,
    )

    (solution,) = call(part(solution_kernel, rhs), [panel], step, right_sides)

    def loaded(mine):
        terms, sums = call(
            part(near_add_kernel, rhs, chunks, held),
            [two_rows, small],
            after(mine, solution), residual, right_sides, nugget, left, named, places, turned,
            micros=0.0,
        )
        return terms, sums, turned, factors, places

    message, got, *_ = gather(message, loaded)
    pair, projected, next_gram, mix, *sends = call(
        part(second_kernel, rhs, chunks, go + stay),
        [small, two_rows, small, small] + sent,
        message, got, *factors, places, first_gram, weighted, earlier,
    )
    (direction,) = call(part(direction_kernel, rhs), [panel], mix, right_sides, residual)
    mine, pair, got = reduce(sends, pair, projected, left, direction)
    return tuple(
        call(
            part(last_kernel, rhs, chunks),
            [panel, panel],
            direction, nugget, mine, pair, next_gram, residual, solution, *got,
        )
    )


def solution(mesh):
    return jax.shard_map(
        shards,
        mesh=mesh,
        in_specs=(
            P(None, ("groups", "row")),
            P(("groups", "row")),
            P(("groups", "row"), None, None),
            P(("groups", "row"), None, None),
            P(("groups", "row"), None),
            P(("groups", "row")),
        ),
        out_specs=(P(None, ("groups", "row")), P(None, ("groups", "row"))),
        check_vma=False,
    )
```

```python
import functools

import jax
import jax.numpy as jnp
from jax import lax
from jax.experimental import pallas as pl
from jax.experimental.pallas import tpu as pltpu
from jax.sharding import PartitionSpec as P

LANES = 128
F32 = jnp.float32
BF16 = jnp.bfloat16
EXACT = lax.Precision.HIGHEST
NN = (((1,), (0,)), ((), ()))
NT = (((1,), (1,)), ((), ()))


def lanes_of(block):
    return lax.broadcasted_iota(jnp.int32, block.shape, len(block.shape) - 1)


def sums_of(parts, rhs):
    rest = jnp.zeros((rhs, LANES - rhs * len(parts)), F32)
    return jnp.concatenate(parts + [rest], axis=1)


def encode(pair, rhs):
    high = pair.astype(BF16).astype(F32)
    rest = pair - high
    middle = rest.astype(BF16).astype(F32)
    low = rest - middle
    return (high + pltpu.roll(middle, 2 * rhs, 1) + pltpu.roll(low, 4 * rhs, 1)).astype(BF16)


def decode(code, rhs):
    total = code + pltpu.roll(code, LANES - 2 * rhs, 1) + pltpu.roll(code, LANES - 4 * rhs, 1)
    return jnp.where(lanes_of(total) < 2 * rhs, total, 0.0)


def second_of(pair, rhs):
    return pltpu.roll(pair, LANES - rhs, 1)


def right_divide(top, bottom, rhs):
    both = jnp.concatenate([top, bottom], axis=0)
    lane = lanes_of(both)
    both = jnp.where(lane < rhs, both, 0.0)
    one = lane[:1]
    for k in range(0, rhs, 4):
        cols = [jnp.broadcast_to(both[:, k + j : k + j + 1], both.shape) for j in range(4)]
        p = [[cols[j][k + i : k + i + 1] for j in range(4)] for i in range(4)]
        inside = (one >= k) & (one < k + 4)
        rows = [
            jnp.where(inside, jnp.where(one == k + i, -1.0, 0.0), both[k + i : k + i + 1]) for i in range(4)
        ]
        inverse = 1.0 / (p[0][0] * p[1][1] - p[0][1] * p[1][0])

        def upper(x, y):
            return (p[1][1] * x - p[0][1] * y) * inverse, (p[0][0] * y - p[1][0] * x) * inverse

        b_02, b_12 = upper(p[0][2], p[1][2])
        b_03, b_13 = upper(p[0][3], p[1][3])
        r_0, r_1 = upper(rows[0], rows[1])
        s_22 = p[2][2] - p[2][0] * b_02 - p[2][1] * b_12
        s_23 = p[2][3] - p[2][0] * b_03 - p[2][1] * b_13
        s_32 = p[3][2] - p[3][0] * b_02 - p[3][1] * b_12
        s_33 = p[3][3] - p[3][0] * b_03 - p[3][1] * b_13
        inverse_low = 1.0 / (s_22 * s_33 - s_23 * s_32)
        q_2 = rows[2] - p[2][0] * r_0 - p[2][1] * r_1
        q_3 = rows[3] - p[3][0] * r_0 - p[3][1] * r_1
        w_2 = (s_33 * q_2 - s_23 * q_3) * inverse_low
        w_3 = (s_22 * q_3 - s_32 * q_2) * inverse_low
        w_0 = r_0 - b_02 * w_2 - b_03 * w_3
        w_1 = r_1 - b_12 * w_2 - b_13 * w_3
        both = jnp.where((lane >= k) & (lane < k + 4), 0.0, both)
        both = both - cols[0] * w_0 - cols[1] * w_1 - cols[2] * w_2 - cols[3] * w_3
    return both[rhs:, :]


def left_multiply(square, block, rhs):
    return lax.dot_general(square[:, :rhs], block, NN, precision=EXACT, preferred_element_type=F32)


def gram(former, latter):
    return lax.dot_general(former, latter, NT, precision=EXACT, preferred_element_type=F32)


def rows_of(ref, chunks):
    panels, _, rhs, lanes = ref.shape
    return jnp.concatenate([ref[:, c].reshape(panels * rhs, lanes) for c in range(chunks)], axis=1)


def store_message(message_ref, block, rhs, at=0):
    for c in range(block.shape[1] // LANES):
        message_ref[at + c] = block[:, c * LANES : (c + 1) * LANES].astype(message_ref.dtype)


def far_terms(total, panels, turned_ref, places, bases, rhs, chunks):
    rows = jnp.concatenate([rows_of(ref, chunks) for ref in panels], axis=0)
    far = lax.dot_general(rows, turned_ref[...], NN, preferred_element_type=F32)
    at = 0
    for base, ref in zip(bases, panels):
        for i in range(ref.shape[0]):
            total = total + jnp.where(places == base + i, far[at : at + rhs], 0.0)
            at += rhs
    return total


def codes_of(panels_ref, chunks):
    count, held = panels_ref.shape[:2]
    code = jnp.zeros(panels_ref.shape[2:], F32)
    for i in range(count if held > chunks else 0):
        code = code + panels_ref[i, chunks].astype(F32)
    return code


def spread_terms(projected, factors, places, wanted, store, rhs, chunks):
    masked = [jnp.where(places == place, projected, 0.0).astype(BF16) for place in wanted]
    masked = jnp.concatenate(masked, axis=0)
    width = factors[0].shape[0]
    step = 2 * LANES
    for block in range(chunks // 2):
        at = slice(block * step, (block + 1) * step)
        moved = sum(
            lax.dot_general(
                masked[:, i * width : (i + 1) * width], ref[:, at], NN, preferred_element_type=F32
            )
            for i, ref in enumerate(factors)
        )
        for i in range(len(wanted)):
            for b in range(2):
                piece = moved[i * rhs : (i + 1) * rhs, b * LANES : (b + 1) * LANES]
                store(i, 2 * block + b, piece)


def open_kernel(rhs, right_side_hbm, message_ref, right_side_ref, sem):
    copy = pltpu.make_async_copy(right_side_hbm, right_side_ref, sem)
    copy.start()
    copy.wait()
    store_message(message_ref, right_side_ref[...], rhs)


def load_kernel(
    rhs, rank, own_ref, column_hbm, live_ref, nugget_hbm, left_hbm, right_hbm,
    nugget_ref, left_ref, right_ref, named_ref, near_ref, sums_ref,
    column_ref, column_sem, nugget_sem, left_sem, right_sem,
):
    copies = [
        pltpu.make_async_copy(column_hbm, column_ref, column_sem),
        pltpu.make_async_copy(nugget_hbm, nugget_ref, nugget_sem),
        pltpu.make_async_copy(left_hbm, left_ref, left_sem),
        pltpu.make_async_copy(right_hbm, right_ref, right_sem),
    ]
    for copy in copies:
        copy.start()
    own = own_ref[...]
    for copy in copies[:2]:
        copy.wait()
    slot_of = lax.broadcasted_iota(jnp.int32, (1, named_ref.shape[1]), 1) // rank
    named = jnp.full(slot_of.shape, -1, jnp.int32)
    for s in range(column_ref.shape[0]):
        named = jnp.where(slot_of == s, jnp.where(s < live_ref[0], column_ref[s], -1), named)
    named_ref[...] = jnp.broadcast_to(named, named_ref.shape)
    sums_ref[...] = sums_of([gram(own * nugget_ref[...], own), gram(own, own)], rhs)
    copies[2].wait()
    near = lax.dot_general(own.astype(BF16), left_ref[...], NT, preferred_element_type=F32)
    near_ref[...] = jnp.where(named >= 0, near, 0.0)
    copies[3].wait()


def load_add_kernel(
    rhs, chunks, place_of, base, held_ref, near_ref, named_ref, other_named_ref, right_ref, other_ref,
    part_ref, places_ref, turned_ref,
):
    named = jnp.concatenate([named_ref[...], other_named_ref[...]], axis=1)
    offset = named ^ lax.axis_index("row")
    places = jnp.where((named >= 0) & ((offset & 1) == 0), place_of(offset), -1)
    places = jnp.concatenate([places] * (rhs // places.shape[0]), axis=0)
    places_ref[...] = places
    near = near_ref[...]
    total = jnp.concatenate([near, jnp.zeros(near.shape, F32)], axis=1)
    half = other_ref.shape[0]
    turned_ref[:, half:] = other_ref[...].T
    turned_ref[:, :half] = right_ref[...].T
    part_ref[...] = far_terms(total, [held_ref], turned_ref, places, [base], rhs, chunks)


def near_add_kernel(
    rhs, chunks, base, held_ref, own_ref, right_side_ref, nugget_ref, left_ref, named_ref, places_ref,
    turned_ref, gram_ref, part_ref, sums_ref, inverse_ref,
):
    row = lax.broadcasted_iota(jnp.int32, gram_ref.shape, 0)
    inverse_ref[...] = right_divide(gram_ref[...], jnp.where(row == lanes_of(row), 1.0, 0.0), rhs)
    own = own_ref[...]
    near = lax.dot_general(own.astype(BF16), left_ref[...], NT, preferred_element_type=F32)
    near = jnp.where(named_ref[:1] >= 0, near, 0.0)
    total = jnp.concatenate([near, jnp.zeros(near.shape, F32)], axis=1)
    part_ref[...] = far_terms(total, [held_ref], turned_ref, places_ref[...], [base], rhs, chunks)
    weighted = own * nugget_ref[...]
    code = codes_of(held_ref, chunks)
    none = jnp.zeros((rhs, rhs), F32)
    sums_ref[...] = decode(code, rhs) + sums_of([none, gram(weighted, own), gram(right_side_ref[...], weighted)], rhs)


def add_kernel(
    rhs, chunks, bases, turned_ref, places_ref, part_ref, sums_ref, *rest
):
    *panels, message_ref = rest
    total = far_terms(part_ref[...], panels, turned_ref, places_ref[...], bases, rhs, chunks)
    width = total.shape[1]
    message_ref[:, :width] = total
    message_ref[:, width:] = sums_ref[...] + decode(sum(codes_of(ref, chunks) for ref in panels), rhs)


def both_cores(message_ref, got_ref):
    half = (message_ref.shape[1] - LANES) // 2
    own = message_ref[:, :half] + got_ref[:, half : 2 * half]
    other = message_ref[:, half : 2 * half] + got_ref[:, :half]
    sums = message_ref[:, 2 * half :] + got_ref[:, 2 * half :]
    return jnp.concatenate([own, other], axis=1), sums


def rounded_gram(projected):
    rounded = projected.astype(BF16)
    return lax.dot_general(rounded, rounded, NT, preferred_element_type=F32)


def send_terms(outs, projected, factors, places, wanted, pair, rhs, chunks):
    slots = [(ref, i) for ref in outs for i in range(ref.shape[0] // chunks)]

    def store(i, c, piece):
        ref, j = slots[i]
        ref[j * chunks + c] = piece.astype(ref.dtype)

    spread_terms(projected, factors, places, wanted, store, rhs, chunks)
    code = encode(pair, rhs)
    for ref in outs:
        if ref.shape[0] % chunks:
            ref[ref.shape[0] - 1] = code


def first_kernel(
    rhs, chunks, wanted, message_ref, got_ref, right_ref, other_ref, places_ref,
    pair_ref, projected_ref, sums_ref, *sends,
):
    projected, sums = both_cores(message_ref, got_ref)
    projected_ref[...] = projected
    sums_ref[...] = sums
    pair = sums + sums_of([rounded_gram(projected)], rhs)
    pair_ref[...] = pair
    send_terms(sends, projected, (right_ref, other_ref), places_ref[...], wanted, pair, rhs, chunks)


def second_kernel(
    rhs, chunks, wanted, message_ref, got_ref, right_ref, other_ref, places_ref,
    inverse_ref, weighted_ref, earlier_ref,
    pair_ref, projected_ref, next_gram_ref, mix_ref, *sends,
):
    projected, sums = both_cores(message_ref, got_ref)
    next_gram_ref[...] = sums
    mix = left_multiply(sums, inverse_ref[...], rhs)
    projected = projected + left_multiply(mix, earlier_ref[...], rhs)
    projected_ref[...] = projected
    weighted = left_multiply(mix, jnp.concatenate([sums[:, 2 * rhs : 3 * rhs], weighted_ref[:, :rhs]], axis=1), rhs)
    mixed = weighted[:, :rhs]
    curvature = sums[:, rhs : 2 * rhs] + mixed + mixed.T + gram(weighted[:, rhs:], mix[:, :rhs])
    pair = sums_of([curvature + rounded_gram(projected)], rhs)
    pair_ref[...] = pair
    send_terms(sends, projected, (right_ref, other_ref), places_ref[...], wanted, pair, rhs, chunks)
    mix_ref[...] = mix


def solution_kernel(rhs, step_ref, right_side_ref, solution_ref):
    solution_ref[...] = left_multiply(step_ref[...], right_side_ref[...], rhs)


def direction_kernel(rhs, mix_ref, right_side_ref, residual_ref, direction_ref):
    direction_ref[...] = residual_ref[...] + left_multiply(mix_ref[...], right_side_ref[...], rhs)


def join_kernel(keep_ref, *rest):
    *got, sum_ref = rest
    total = keep_ref[...]
    for ref in got:
        total = total + ref[...].astype(F32)
    sum_ref[...] = total


def pass_kernel(rhs, keep_ref, *rest):
    *got, message_ref = rest
    size = keep_ref.shape[0]
    message_ref[:size] = (keep_ref[...] + sum(ref[:size].astype(F32) for ref in got)).astype(BF16)
    message_ref[size] = encode(decode(sum(ref[size].astype(F32) for ref in got), rhs), rhs)


def part_kernel(rhs, keep_ref, pair_ref, got_ref, total_ref, *sends):
    size = sends[0].shape[0] - 1
    total = pair_ref[...] + decode(got_ref[got_ref.shape[0] - 1].astype(F32), rhs)
    total_ref[...] = total
    code = encode(total, rhs)
    for i, send in enumerate(sends):
        at = i * size
        send[:size] = (keep_ref[at : at + size] + got_ref[at : at + size].astype(F32)).astype(BF16)
        send[size] = code


def own_kernel(rhs, chunks, projected_ref, left_ref, keep_ref, *rest):
    *_, sum_ref, total_ref = rest
    join_coded_kernel(rhs, keep_ref, *rest)
    own = projected_ref[:, : left_ref.shape[0]].astype(BF16)
    own = lax.dot_general(own, left_ref[...], NN, preferred_element_type=F32)
    for c in range(chunks):
        sum_ref[c] = sum_ref[c] + own[:, c * LANES : (c + 1) * LANES]


def join_coded_kernel(rhs, keep_ref, pair_ref, *rest):
    *got, sum_ref, total_ref = rest
    size = keep_ref.shape[0]
    total, code = keep_ref[...], jnp.zeros(pair_ref.shape, F32)
    for ref in got:
        total = total + ref[:size].astype(F32)
        code = code + ref[size].astype(F32)
    sum_ref[...] = total
    total_ref[...] = pair_ref[...] + decode(code, rhs)


def message_kernel(rhs, panel_ref, pair_ref, message_ref):
    message_ref[: panel_ref.shape[0]] = panel_ref[...].astype(BF16)
    message_ref[panel_ref.shape[0]] = encode(pair_ref[...], rhs)


def code_kernel(rhs, pair_ref, code_ref):
    code_ref[...] = encode(pair_ref[...], rhs)


def pair_kernel(rhs, pair_ref, got_ref, total_ref):
    total_ref[...] = pair_ref[...] + decode(got_ref[...].astype(F32), rhs)


def gathered_product(keep_ref, pair_ref, got, direction, nugget, rhs, chunks):
    total = keep_ref[...]
    code = jnp.zeros(pair_ref.shape, F32)
    for ref in got:
        total = total + ref[:chunks].astype(F32)
        code = code + ref[chunks].astype(F32)
    applied = nugget * direction + jnp.concatenate([total[c] for c in range(chunks)], axis=1)
    return applied, pair_ref[...] + decode(code, rhs)


def middle_kernel(
    rhs, chunks, direction_ref, nugget_ref, keep_ref, pair_ref, *rest
):
    *got, message_ref, residual_ref, step_ref, gram_ref = rest
    direction = direction_ref[...]
    applied, pair = gathered_product(keep_ref, pair_ref, got, direction, nugget_ref[...], rhs, chunks)
    first_gram = second_of(pair, rhs)
    gram_ref[...] = first_gram
    step = right_divide(pair, first_gram, rhs)
    residual = direction - left_multiply(step, applied, rhs)
    residual_ref[...] = residual
    store_message(message_ref, residual, rhs)
    message_ref[chunks] = encode(sums_of([gram(residual, residual)], rhs), rhs)
    step_ref[...] = step


def last_kernel(
    rhs, chunks, direction_ref, nugget_ref, keep_ref, pair_ref, gram_ref, residual_ref, solution_ref, *rest
):
    *got, out_solution_ref, out_residual_ref = rest
    direction = direction_ref[...]
    applied, pair = gathered_product(keep_ref, pair_ref, got, direction, nugget_ref[...], rhs, chunks)
    step = right_divide(pair, gram_ref[...], rhs)
    out_solution_ref[...] = solution_ref[...] + left_multiply(step, direction, rhs)
    out_residual_ref[...] = residual_ref[...] - left_multiply(step, applied, rhs)


def call(kernel, outs, *args, far=(), scalars=(), fixed=(), scratch=(), micros=0.0):
    whole = pl.BlockSpec(memory_space=pltpu.VMEM)
    spaces = {i: pltpu.HBM for i in far} | {i: pltpu.SMEM for i in scalars}
    return pl.pallas_call(
        kernel,
        out_shape=[
            pltpu.VMEM(shape, dtype) if i in fixed else jax.ShapeDtypeStruct(shape, dtype)
            for i, (shape, dtype) in enumerate(outs)
        ],
        in_specs=[pl.BlockSpec(memory_space=spaces[i]) if i in spaces else whole for i in range(len(args))],
        out_specs=[whole] * len(outs),
        scratch_shapes=list(scratch),
        cost_estimate=pl.CostEstimate(flops=int(micros * 1e9), bytes_accessed=0, transcendentals=0),
        compiler_params=pltpu.CompilerParams(vmem_limit_bytes=32 * 1024 * 1024),
    )(*args)


def after(value, *others):
    return lax.optimization_barrier((value, *others))[0]


def shards(right_sides, nugget, left_factors, right_factors, tile_column, live_slots):
    devices = lax.axis_size("row")
    bits = devices.bit_length() - 1
    low_bits = bits - 2
    slots, rank, width = left_factors.shape
    rhs = right_sides.shape[0]
    chunks = width // LANES
    part = functools.partial

    def swap(array, offset):
        return lax.ppermute(array, "row", [(i, i ^ offset) for i in range(devices)])

    order = (0, 3, 2, 1)
    groups = []
    for k in order:
        group = [k << low_bits]
        for b in range(low_bits - 1, 1, -1):
            group = group + [o | (1 << b) for o in group]
        groups.append(group)
    m = len(groups[0])
    held_offsets = sum(groups, [])
    offsets = held_offsets + [o | 2 for o in held_offsets]
    held, late = 0, 4 * m

    def place_of(offset):
        place = ((4 - (offset >> low_bits)) & 3) * m
        for b in range(low_bits - 1, 1, -1):
            place = place + (((offset >> b) & 1) << (low_bits - 1 - b))
        return place + ((offset >> 1) & 1) * late

    assert [place_of(o) for o in offsets] == list(range(devices // 2))
    stay, go = tuple(range(late + m)), tuple(range(late + m, 2 * late))

    small = ((rhs, LANES), F32)
    panel = ((rhs, width), F32)
    row_block = ((rhs, slots * rank), F32)
    two_rows = ((rhs, 2 * slots * rank), F32)
    core_message = ((rhs, 2 * slots * rank + LANES), F32)
    factor = ((slots * rank, width), BF16)
    semaphore = pltpu.SemaphoreType.DMA

    def plain(count):
        return ((count * chunks, rhs, LANES), BF16)

    def coded(count):
        return ((count * chunks + 1, rhs, LANES), BF16)

    def kept(count):
        return ((count * chunks, rhs, LANES), F32)

    sent = [coded(m)] * 3 + ([kept(1)] * 2 + [coded(1)] * 2 if m == 1 else [kept(m)] + [plain(m)] * 3) + [kept(m)]

    def gather(message, first_terms, *early):
        if m == 1:
            far_3, far_2 = [swap(message, k << low_bits)[None] for k in order[1:3]]
            beside = swap(message[None], 2)
            far_1 = swap(message, order[3] << low_bits)[None]
            last = [
                swap(after(jnp.concatenate([far_3, far_2]), *early), 2),
                swap(beside, order[3] << low_bits),
            ]
            bases = (late, late + 1, late + 3)
            held_panels = jnp.concatenate([message[None], far_3, far_2, far_1])
        else:
            mine = [message[None]] + [swap(message, k << low_bits)[None] for k in order[1:]]
            for b in range(low_bits - 1, 1, -1):
                mine = [jnp.concatenate([g, swap(g, 1 << b)]) for g in mine]
            beside = swap(mine[0], 2)
            last = [swap(jnp.concatenate(mine[1:]), 2)]
            bases = (late, late + m)
            held_panels = jnp.concatenate(mine)
        terms, sums, turned, factors, places = first_terms(held_panels)
        last = [after(x, terms) for x in last]
        (message,) = call(
            part(add_kernel, rhs, chunks, bases), [core_message], turned, places, terms, sums, beside, *last
        )
        return message, swap(message, 1), turned, factors, places

    def reduce(sends, pair, projected, left, *early):
        sends, stays = sends[:3], sends[3:]
        if m == 1:
            got_side = swap(sends[0], 2)
            got_far = [swap(sends[i], order[i + 1] << low_bits) for i in (1, 2)]
            mine, keep, *sends, beside = stays
            got_here = [swap(sends[i - 1], order[i + 1] << low_bits) for i in (1, 2)]
            pair, send = call(part(part_kernel, rhs), [small, coded(1)], keep, pair, got_side)
            got_last = swap(send, order[1] << low_bits)
            (send,) = call(part(pass_kernel, rhs), [coded(1)], beside, *got_far)
            got_beside = swap(send, 2)
            join = part(join_coded_kernel, rhs)
            mine, pair = call(
                part(own_kernel, rhs, chunks), [kept(1), small],
                projected, left, after(mine, *early), pair, *got_here,
                micros=0.3,
            )
            mine, pair = call(join, [kept(1), small], mine, pair, got_last, micros=0.3)
            return mine, pair, [got_beside]
        got = [swap(x, k << low_bits) for x, k in zip(sends, order[1:])]
        keep, *sends, beside = stays
        got_here = [swap(x, k << low_bits) for x, k in zip(sends, order[1:])]
        turned, pair = call(part(join_coded_kernel, rhs), [kept(m), small], beside, pair, *got)
        (keep,) = call(join_kernel, [kept(m)], after(keep, *early), *got_here)
        for b in range(2, low_bits):
            (code,) = call(part(code_kernel, rhs), [((rhs, LANES), BF16)], pair)
            (pair,) = call(part(pair_kernel, rhs), [small], pair, swap(code, 1 << b))
            half = keep.shape[0] // 2
            keep, turned = [
                x[:half] + swap(x[half:].astype(BF16), 1 << b).astype(F32) for x in (keep, turned)
            ]
        (turned,) = call(part(message_kernel, rhs), [coded(1)], turned, pair)
        keep, pair = call(part(own_kernel, rhs, chunks), [kept(1), small], projected, left, keep, pair)
        return keep, pair, [swap(turned, 2)]

    def in_hbm(array):
        return pltpu.with_memory_space_constraint(array, pltpu.HBM)

    message, right_sides = call(
        part(open_kernel, rhs), [plain(1), panel], in_hbm(right_sides), far=(0,), fixed=(1,), scratch=[semaphore]
    )
    right = right_factors.reshape(slots * rank, width)
    other = swap(after(right, message), 1)
    named_shape = ((8, slots * rank), jnp.int32)
    nugget, left, here, named, near, sums = call(
        part(load_kernel, rhs, rank),
        [((1, width), F32), factor, factor, named_shape, row_block, small],
        right_sides, in_hbm(tile_column.reshape(slots)), live_slots, in_hbm(nugget[None, :]),
        in_hbm(left_factors.reshape(slots * rank, width)), in_hbm(right),
        far=(1, 3, 4, 5), scalars=(2,), fixed=(0, 1, 2), scratch=[pltpu.SMEM((slots,), jnp.int32)] + [semaphore] * 4,
    )
    other_named = swap(named, 1)

    def loading(mine):
        terms, places, turned = call(
            part(load_add_kernel, rhs, chunks, place_of, held),
            [two_rows, ((rhs, 2 * slots * rank), jnp.int32), ((width, 2 * slots * rank), BF16)],
            mine, near, named, other_named, here, other,
            fixed=(2,),
        )
        return terms, sums, turned, (here, other), places

    message, got, turned, factors, places = gather(message, loading, near)
    pair, earlier, weighted, *sends = call(
        part(first_kernel, rhs, chunks, go + stay),
        [small, two_rows, small] + sent,
        message, got, *factors, places,
    )
    mine, pair, got = reduce(sends, pair, earlier, left)
    message, residual, step, first_gram = call(
        part(middle_kernel, rhs, chunks),
        [coded(1), panel, small, small],
        right_sides, nugget, mine, pair, *got,
    )

    (solution,) = call(part(solution_kernel, rhs), [panel], step, right_sides)

    def loaded(mine):
        terms, sums, inverse = call(
            part(near_add_kernel, rhs, chunks, held),
            [two_rows, small, small],
            mine, residual, right_sides, nugget, left, named, places, turned, first_gram,
            micros=0.0,
        )
        return terms, sums, turned, (inverse,), places

    message, got, _, (inverse,), _ = gather(message, loaded)
    pair, projected, next_gram, mix, *sends = call(
        part(second_kernel, rhs, chunks, go + stay),
        [small, two_rows, small, small] + sent,
        message, got, *factors, places, inverse, weighted, earlier,
    )
    (direction,) = call(part(direction_kernel, rhs), [panel], mix, right_sides, residual)
    mine, pair, got = reduce(sends, pair, projected, left, direction, solution)
    return tuple(
        call(
            part(last_kernel, rhs, chunks),
            [panel, panel],
            direction, nugget, mine, pair, next_gram, residual, solution, *got,
        )
    )


def solution(mesh):
    return jax.shard_map(
        shards,
        mesh=mesh,
        in_specs=(
            P(None, ("groups", "row")),
            P(("groups", "row")),
            P(("groups", "row"), None, None),
            P(("groups", "row"), None, None),
            P(("groups", "row"), None),
            P(("groups", "row")),
        ),
        out_specs=(P(None, ("groups", "row")), P(None, ("groups", "row"))),
        check_vma=False,
    )
```

```python
import functools

import jax
import jax.numpy as jnp
from jax import lax
from jax.experimental import pallas as pl
from jax.experimental.pallas import tpu as pltpu
from jax.sharding import PartitionSpec as P

LANES = 128
F32 = jnp.float32
BF16 = jnp.bfloat16
EXACT = lax.Precision.HIGHEST
NN = (((1,), (0,)), ((), ()))
NT = (((1,), (1,)), ((), ()))


def lanes_of(block):
    return lax.broadcasted_iota(jnp.int32, block.shape, len(block.shape) - 1)


def sums_of(parts, rhs):
    rest = jnp.zeros((rhs, LANES - rhs * len(parts)), F32)
    return jnp.concatenate(parts + [rest], axis=1)


def encode(pair, rhs):
    high = pair.astype(BF16).astype(F32)
    rest = pair - high
    middle = rest.astype(BF16).astype(F32)
    low = rest - middle
    return (high + pltpu.roll(middle, 2 * rhs, 1) + pltpu.roll(low, 4 * rhs, 1)).astype(BF16)


def decode(code, rhs):
    total = code + pltpu.roll(code, LANES - 2 * rhs, 1) + pltpu.roll(code, LANES - 4 * rhs, 1)
    return jnp.where(lanes_of(total) < 2 * rhs, total, 0.0)


def second_of(pair, rhs):
    return pltpu.roll(pair, LANES - rhs, 1)


def right_divide(top, bottom, rhs):
    both = jnp.concatenate([top, bottom], axis=0)
    lane = lanes_of(both)
    both = jnp.where(lane < rhs, both, 0.0)
    one = lane[:1]
    for k in range(0, rhs, 4):
        cols = [jnp.broadcast_to(both[:, k + j : k + j + 1], both.shape) for j in range(4)]
        p = [[cols[j][k + i : k + i + 1] for j in range(4)] for i in range(4)]
        inside = (one >= k) & (one < k + 4)
        rows = [
            jnp.where(inside, jnp.where(one == k + i, -1.0, 0.0), both[k + i : k + i + 1]) for i in range(4)
        ]
        inverse = 1.0 / (p[0][0] * p[1][1] - p[0][1] * p[1][0])

        def upper(x, y):
            return (p[1][1] * x - p[0][1] * y) * inverse, (p[0][0] * y - p[1][0] * x) * inverse

        b_02, b_12 = upper(p[0][2], p[1][2])
        b_03, b_13 = upper(p[0][3], p[1][3])
        r_0, r_1 = upper(rows[0], rows[1])
        s_22 = p[2][2] - p[2][0] * b_02 - p[2][1] * b_12
        s_23 = p[2][3] - p[2][0] * b_03 - p[2][1] * b_13
        s_32 = p[3][2] - p[3][0] * b_02 - p[3][1] * b_12
        s_33 = p[3][3] - p[3][0] * b_03 - p[3][1] * b_13
        inverse_low = 1.0 / (s_22 * s_33 - s_23 * s_32)
        q_2 = rows[2] - p[2][0] * r_0 - p[2][1] * r_1
        q_3 = rows[3] - p[3][0] * r_0 - p[3][1] * r_1
        w_2 = (s_33 * q_2 - s_23 * q_3) * inverse_low
        w_3 = (s_22 * q_3 - s_32 * q_2) * inverse_low
        w_0 = r_0 - b_02 * w_2 - b_03 * w_3
        w_1 = r_1 - b_12 * w_2 - b_13 * w_3
        both = jnp.where((lane >= k) & (lane < k + 4), 0.0, both)
        both = both - cols[0] * w_0 - cols[1] * w_1 - cols[2] * w_2 - cols[3] * w_3
    return both[rhs:, :]


def left_multiply(square, block, rhs):
    return lax.dot_general(square[:, :rhs], block, NN, precision=EXACT, preferred_element_type=F32)


def gram(former, latter):
    return lax.dot_general(former, latter, NT, precision=EXACT, preferred_element_type=F32)


def rows_of(ref, chunks):
    panels, _, rhs, lanes = ref.shape
    return jnp.concatenate([ref[:, c].reshape(panels * rhs, lanes) for c in range(chunks)], axis=1)


def store_message(message_ref, block, rhs, at=0):
    for c in range(block.shape[1] // LANES):
        message_ref[at + c] = block[:, c * LANES : (c + 1) * LANES].astype(message_ref.dtype)


def far_terms(total, panels, turned_ref, places, bases, rhs, chunks):
    rows = jnp.concatenate([rows_of(ref, chunks) for ref in panels], axis=0)
    if rows.shape[0] * 2 == LANES:
        rows = jnp.concatenate([rows, rows], axis=0)
    far = lax.dot_general(rows, turned_ref[...], NN, preferred_element_type=F32)
    at = 0
    for base, ref in zip(bases, panels):
        for i in range(ref.shape[0]):
            total = total + jnp.where(places == base + i, far[at : at + rhs], 0.0)
            at += rhs
    return total


def codes_of(panels_ref, chunks):
    count, held = panels_ref.shape[:2]
    code = jnp.zeros(panels_ref.shape[2:], F32)
    for i in range(count if held > chunks else 0):
        code = code + panels_ref[i, chunks].astype(F32)
    return code


def spread_terms(projected, factors, places, wanted, store, rhs, chunks):
    masked = [jnp.where(places == place, projected, 0.0).astype(BF16) for place in wanted]
    masked = jnp.concatenate(masked, axis=0)
    width = factors[0].shape[0]
    step = 2 * LANES
    for block in range(chunks // 2):
        at = slice(block * step, (block + 1) * step)
        moved = sum(
            lax.dot_general(
                masked[:, i * width : (i + 1) * width], ref[:, at], NN, preferred_element_type=F32
            )
            for i, ref in enumerate(factors)
        )
        for i in range(len(wanted)):
            for b in range(2):
                piece = moved[i * rhs : (i + 1) * rhs, b * LANES : (b + 1) * LANES]
                store(i, 2 * block + b, piece)


def open_kernel(rhs, right_side_hbm, message_ref, right_side_ref, sem):
    copy = pltpu.make_async_copy(right_side_hbm, right_side_ref, sem)
    copy.start()
    copy.wait()
    store_message(message_ref, right_side_ref[...], rhs)


def load_kernel(
    rhs, rank, own_ref, column_hbm, live_ref, nugget_hbm, left_hbm, right_hbm,
    nugget_ref, left_ref, right_ref, named_ref, near_ref, sums_ref,
    column_ref, column_sem, nugget_sem, left_sem, right_sem,
):
    copies = [
        pltpu.make_async_copy(column_hbm, column_ref, column_sem),
        pltpu.make_async_copy(nugget_hbm, nugget_ref, nugget_sem),
        pltpu.make_async_copy(left_hbm, left_ref, left_sem),
        pltpu.make_async_copy(right_hbm, right_ref, right_sem),
    ]
    for copy in copies:
        copy.start()
    own = own_ref[...]
    for copy in copies[:2]:
        copy.wait()
    slot_of = lax.broadcasted_iota(jnp.int32, (1, named_ref.shape[1]), 1) // rank
    named = jnp.full(slot_of.shape, -1, jnp.int32)
    for s in range(column_ref.shape[0]):
        named = jnp.where(slot_of == s, jnp.where(s < live_ref[0], column_ref[s], -1), named)
    named_ref[...] = jnp.broadcast_to(named, named_ref.shape)
    sums_ref[...] = sums_of([gram(own * nugget_ref[...], own), gram(own, own)], rhs)
    copies[2].wait()
    near = lax.dot_general(own.astype(BF16), left_ref[...], NT, preferred_element_type=F32)
    near_ref[...] = jnp.where(named >= 0, near, 0.0)
    copies[3].wait()


def load_add_kernel(
    rhs, chunks, place_of, base, held_ref, near_ref, named_ref, other_named_ref, right_ref, other_ref,
    part_ref, places_ref, turned_ref,
):
    named = jnp.concatenate([named_ref[...], other_named_ref[...]], axis=1)
    offset = named ^ lax.axis_index("row")
    places = jnp.where((named >= 0) & ((offset & 1) == 0), place_of(offset), -1)
    places = jnp.concatenate([places] * (rhs // places.shape[0]), axis=0)
    places_ref[...] = places
    near = near_ref[...]
    total = jnp.concatenate([near, jnp.zeros(near.shape, F32)], axis=1)
    half = other_ref.shape[0]
    turned_ref[:, half:] = other_ref[...].T
    turned_ref[:, :half] = right_ref[...].T
    part_ref[...] = far_terms(total, [held_ref], turned_ref, places, [base], rhs, chunks)


def near_add_kernel(
    rhs, chunks, base, held_ref, own_ref, right_side_ref, nugget_ref, left_ref, named_ref, places_ref,
    turned_ref, gram_ref, part_ref, sums_ref, inverse_ref,
):
    row = lax.broadcasted_iota(jnp.int32, gram_ref.shape, 0)
    inverse_ref[...] = right_divide(gram_ref[...], jnp.where(row == lanes_of(row), 1.0, 0.0), rhs)
    own = own_ref[...]
    near = lax.dot_general(own.astype(BF16), left_ref[...], NT, preferred_element_type=F32)
    near = jnp.where(named_ref[:1] >= 0, near, 0.0)
    total = jnp.concatenate([near, jnp.zeros(near.shape, F32)], axis=1)
    part_ref[...] = far_terms(total, [held_ref], turned_ref, places_ref[...], [base], rhs, chunks)
    weighted = own * nugget_ref[...]
    code = codes_of(held_ref, chunks)
    none = jnp.zeros((rhs, rhs), F32)
    sums_ref[...] = decode(code, rhs) + sums_of([none, gram(weighted, own), gram(right_side_ref[...], weighted)], rhs)


def add_kernel(
    rhs, chunks, bases, turned_ref, places_ref, part_ref, sums_ref, *rest
):
    *panels, message_ref = rest
    total = far_terms(part_ref[...], panels, turned_ref, places_ref[...], bases, rhs, chunks)
    width = total.shape[1]
    message_ref[:, :width] = total
    message_ref[:, width:] = sums_ref[...] + decode(sum(codes_of(ref, chunks) for ref in panels), rhs)


def both_cores(message_ref, got_ref):
    half = (message_ref.shape[1] - LANES) // 2
    own = message_ref[:, :half] + got_ref[:, half : 2 * half]
    other = message_ref[:, half : 2 * half] + got_ref[:, :half]
    sums = message_ref[:, 2 * half :] + got_ref[:, 2 * half :]
    return jnp.concatenate([own, other], axis=1), sums


def rounded_gram(projected):
    rounded = projected.astype(BF16)
    return lax.dot_general(rounded, rounded, NT, preferred_element_type=F32)


def send_terms(outs, projected, factors, places, wanted, pair, rhs, chunks):
    slots = [(ref, i) for ref in outs for i in range(ref.shape[0] // chunks)]

    def store(i, c, piece):
        ref, j = slots[i]
        ref[j * chunks + c] = piece.astype(ref.dtype)

    spread_terms(projected, factors, places, wanted, store, rhs, chunks)
    code = encode(pair, rhs)
    for ref in outs:
        if ref.shape[0] % chunks:
            ref[ref.shape[0] - 1] = code


def first_kernel(
    rhs, chunks, wanted, message_ref, got_ref, right_ref, other_ref, places_ref,
    pair_ref, projected_ref, sums_ref, *sends,
):
    projected, sums = both_cores(message_ref, got_ref)
    projected_ref[...] = projected
    sums_ref[...] = sums
    pair = sums + sums_of([rounded_gram(projected)], rhs)
    pair_ref[...] = pair
    send_terms(sends, projected, (right_ref, other_ref), places_ref[...], wanted, pair, rhs, chunks)


def second_kernel(
    rhs, chunks, wanted, message_ref, got_ref, right_ref, other_ref, places_ref,
    inverse_ref, weighted_ref, earlier_ref,
    pair_ref, projected_ref, next_gram_ref, mix_ref, *sends,
):
    projected, sums = both_cores(message_ref, got_ref)
    next_gram_ref[...] = sums
    mix = left_multiply(sums, inverse_ref[...], rhs)
    projected = projected + left_multiply(mix, earlier_ref[...], rhs)
    projected_ref[...] = projected
    weighted = left_multiply(mix, jnp.concatenate([sums[:, 2 * rhs : 3 * rhs], weighted_ref[:, :rhs]], axis=1), rhs)
    mixed = weighted[:, :rhs]
    curvature = sums[:, rhs : 2 * rhs] + mixed + mixed.T + gram(weighted[:, rhs:], mix[:, :rhs])
    pair = sums_of([curvature + rounded_gram(projected)], rhs)
    pair_ref[...] = pair
    send_terms(sends, projected, (right_ref, other_ref), places_ref[...], wanted, pair, rhs, chunks)
    mix_ref[...] = mix


def solution_kernel(rhs, step_ref, right_side_ref, solution_ref):
    solution_ref[...] = left_multiply(step_ref[...], right_side_ref[...], rhs)


def direction_kernel(rhs, mix_ref, right_side_ref, residual_ref, direction_ref):
    direction_ref[...] = residual_ref[...] + left_multiply(mix_ref[...], right_side_ref[...], rhs)


def join_kernel(keep_ref, *rest):
    *got, sum_ref = rest
    total = keep_ref[...]
    for ref in got:
        total = total + ref[...].astype(F32)
    sum_ref[...] = total


def pass_kernel(rhs, keep_ref, *rest):
    *got, message_ref = rest
    size = keep_ref.shape[0]
    message_ref[:size] = (keep_ref[...] + sum(ref[:size].astype(F32) for ref in got)).astype(BF16)
    message_ref[size] = encode(decode(sum(ref[size].astype(F32) for ref in got), rhs), rhs)


def part_kernel(rhs, keep_ref, pair_ref, got_ref, total_ref, *sends):
    size = sends[0].shape[0] - 1
    total = pair_ref[...] + decode(got_ref[got_ref.shape[0] - 1].astype(F32), rhs)
    total_ref[...] = total
    code = encode(total, rhs)
    for i, send in enumerate(sends):
        at = i * size
        send[:size] = (keep_ref[at : at + size] + got_ref[at : at + size].astype(F32)).astype(BF16)
        send[size] = code


def own_kernel(rhs, chunks, projected_ref, left_ref, keep_ref, *rest):
    *_, sum_ref, total_ref = rest
    join_coded_kernel(rhs, keep_ref, *rest)
    own = projected_ref[:, : left_ref.shape[0]].astype(BF16)
    own = lax.dot_general(own, left_ref[...], NN, preferred_element_type=F32)
    for c in range(chunks):
        sum_ref[c] = sum_ref[c] + own[:, c * LANES : (c + 1) * LANES]


def join_coded_kernel(rhs, keep_ref, pair_ref, *rest):
    *got, sum_ref, total_ref = rest
    size = keep_ref.shape[0]
    total, code = keep_ref[...], jnp.zeros(pair_ref.shape, F32)
    for ref in got:
        total = total + ref[:size].astype(F32)
        code = code + ref[size].astype(F32)
    sum_ref[...] = total
    total_ref[...] = pair_ref[...] + decode(code, rhs)


def message_kernel(rhs, panel_ref, pair_ref, message_ref):
    message_ref[: panel_ref.shape[0]] = panel_ref[...].astype(BF16)
    message_ref[panel_ref.shape[0]] = encode(pair_ref[...], rhs)


def code_kernel(rhs, pair_ref, code_ref):
    code_ref[...] = encode(pair_ref[...], rhs)


def pair_kernel(rhs, pair_ref, got_ref, total_ref):
    total_ref[...] = pair_ref[...] + decode(got_ref[...].astype(F32), rhs)


def gathered_product(keep_ref, pair_ref, got, direction, nugget, rhs, chunks):
    total = keep_ref[...]
    code = jnp.zeros(pair_ref.shape, F32)
    for ref in got:
        total = total + ref[:chunks].astype(F32)
        code = code + ref[chunks].astype(F32)
    applied = nugget * direction + jnp.concatenate([total[c] for c in range(chunks)], axis=1)
    return applied, pair_ref[...] + decode(code, rhs)


def middle_kernel(
    rhs, chunks, direction_ref, nugget_ref, keep_ref, pair_ref, *rest
):
    *got, message_ref, residual_ref, step_ref, gram_ref = rest
    direction = direction_ref[...]
    applied, pair = gathered_product(keep_ref, pair_ref, got, direction, nugget_ref[...], rhs, chunks)
    first_gram = second_of(pair, rhs)
    gram_ref[...] = first_gram
    step = right_divide(pair, first_gram, rhs)
    residual = direction - left_multiply(step, applied, rhs)
    residual_ref[...] = residual
    store_message(message_ref, residual, rhs)
    message_ref[chunks] = encode(sums_of([gram(residual, residual)], rhs), rhs)
    step_ref[...] = step


def last_kernel(
    rhs, chunks, direction_ref, nugget_ref, keep_ref, pair_ref, gram_ref, residual_ref, solution_ref, *rest
):
    *got, out_solution_ref, out_residual_ref = rest
    direction = direction_ref[...]
    applied, pair = gathered_product(keep_ref, pair_ref, got, direction, nugget_ref[...], rhs, chunks)
    step = right_divide(pair, gram_ref[...], rhs)
    out_solution_ref[...] = solution_ref[...] + left_multiply(step, direction, rhs)
    out_residual_ref[...] = residual_ref[...] - left_multiply(step, applied, rhs)


def call(kernel, outs, *args, far=(), scalars=(), fixed=(), scratch=(), micros=0.0):
    whole = pl.BlockSpec(memory_space=pltpu.VMEM)
    spaces = {i: pltpu.HBM for i in far} | {i: pltpu.SMEM for i in scalars}
    return pl.pallas_call(
        kernel,
        out_shape=[
            pltpu.VMEM(shape, dtype) if i in fixed else jax.ShapeDtypeStruct(shape, dtype)
            for i, (shape, dtype) in enumerate(outs)
        ],
        in_specs=[pl.BlockSpec(memory_space=spaces[i]) if i in spaces else whole for i in range(len(args))],
        out_specs=[whole] * len(outs),
        scratch_shapes=list(scratch),
        cost_estimate=pl.CostEstimate(flops=int(micros * 1e9), bytes_accessed=0, transcendentals=0),
        compiler_params=pltpu.CompilerParams(vmem_limit_bytes=32 * 1024 * 1024),
    )(*args)


def after(value, *others):
    return lax.optimization_barrier((value, *others))[0]


def shards(right_sides, nugget, left_factors, right_factors, tile_column, live_slots):
    devices = lax.axis_size("row")
    bits = devices.bit_length() - 1
    low_bits = bits - 2
    slots, rank, width = left_factors.shape
    rhs = right_sides.shape[0]
    chunks = width // LANES
    part = functools.partial

    def swap(array, offset):
        return lax.ppermute(array, "row", [(i, i ^ offset) for i in range(devices)])

    order = (0, 3, 2, 1)
    groups = []
    for k in order:
        group = [k << low_bits]
        for b in range(low_bits - 1, 1, -1):
            group = group + [o | (1 << b) for o in group]
        groups.append(group)
    m = len(groups[0])
    held_offsets = sum(groups, [])
    offsets = held_offsets + [o | 2 for o in held_offsets]
    held, late = 0, 4 * m

    def place_of(offset):
        place = ((4 - (offset >> low_bits)) & 3) * m
        for b in range(low_bits - 1, 1, -1):
            place = place + (((offset >> b) & 1) << (low_bits - 1 - b))
        return place + ((offset >> 1) & 1) * late

    assert [place_of(o) for o in offsets] == list(range(devices // 2))
    stay, go = tuple(range(late + m)), tuple(range(late + m, 2 * late))

    small = ((rhs, LANES), F32)
    panel = ((rhs, width), F32)
    row_block = ((rhs, slots * rank), F32)
    two_rows = ((rhs, 2 * slots * rank), F32)
    core_message = ((rhs, 2 * slots * rank + LANES), F32)
    factor = ((slots * rank, width), BF16)
    semaphore = pltpu.SemaphoreType.DMA

    def plain(count):
        return ((count * chunks, rhs, LANES), BF16)

    def coded(count):
        return ((count * chunks + 1, rhs, LANES), BF16)

    def kept(count):
        return ((count * chunks, rhs, LANES), F32)

    sent = [coded(m)] * 3 + ([kept(1)] * 2 + [coded(1)] * 2 if m == 1 else [kept(m)] + [plain(m)] * 3) + [kept(m)]

    def gather(message, first_terms, *early):
        if m == 1:
            far_3, far_2 = [swap(message, k << low_bits)[None] for k in order[1:3]]
            beside = swap(message[None], 2)
            far_1 = swap(message, order[3] << low_bits)[None]
            last = [
                swap(after(jnp.concatenate([far_3, far_2]), *early), 2),
                swap(beside, order[3] << low_bits),
            ]
            bases = (late, late + 1, late + 3)
            held_panels = jnp.concatenate([message[None], far_3, far_2, far_1])
        else:
            mine = [message[None]] + [swap(message, k << low_bits)[None] for k in order[1:]]
            for b in range(low_bits - 1, 1, -1):
                mine = [jnp.concatenate([g, swap(g, 1 << b)]) for g in mine]
            beside = swap(mine[0], 2)
            last = [swap(jnp.concatenate(mine[1:]), 2)]
            bases = (late, late + m)
            held_panels = jnp.concatenate(mine)
        terms, sums, turned, factors, places = first_terms(held_panels)
        last = [after(x, terms) for x in last]
        (message,) = call(
            part(add_kernel, rhs, chunks, bases), [core_message], turned, places, terms, sums, beside, *last
        )
        return message, swap(message, 1), turned, factors, places

    def reduce(sends, pair, projected, left, *early):
        sends, stays = sends[:3], sends[3:]
        if m == 1:
            got_side = swap(sends[0], 2)
            got_far = [swap(sends[i], order[i + 1] << low_bits) for i in (1, 2)]
            mine, keep, *sends, beside = stays
            got_here = [swap(sends[i - 1], order[i + 1] << low_bits) for i in (1, 2)]
            pair, send = call(part(part_kernel, rhs), [small, coded(1)], keep, pair, got_side)
            got_last = swap(send, order[1] << low_bits)
            (send,) = call(part(pass_kernel, rhs), [coded(1)], beside, *got_far)
            got_beside = swap(send, 2)
            join = part(join_coded_kernel, rhs)
            mine, pair = call(
                part(own_kernel, rhs, chunks), [kept(1), small],
                projected, left, after(mine, *early), pair, *got_here,
                micros=0.3,
            )
            mine, pair = call(join, [kept(1), small], mine, pair, got_last, micros=0.3)
            return mine, pair, [got_beside]
        got = [swap(x, k << low_bits) for x, k in zip(sends, order[1:])]
        keep, *sends, beside = stays
        got_here = [swap(x, k << low_bits) for x, k in zip(sends, order[1:])]
        turned, pair = call(part(join_coded_kernel, rhs), [kept(m), small], beside, pair, *got)
        (keep,) = call(join_kernel, [kept(m)], after(keep, *early), *got_here)
        for b in range(2, low_bits):
            (code,) = call(part(code_kernel, rhs), [((rhs, LANES), BF16)], pair)
            (pair,) = call(part(pair_kernel, rhs), [small], pair, swap(code, 1 << b))
            half = keep.shape[0] // 2
            keep, turned = [
                x[:half] + swap(x[half:].astype(BF16), 1 << b).astype(F32) for x in (keep, turned)
            ]
        (turned,) = call(part(message_kernel, rhs), [coded(1)], turned, pair)
        keep, pair = call(part(own_kernel, rhs, chunks), [kept(1), small], projected, left, keep, pair)
        return keep, pair, [swap(turned, 2)]

    def in_hbm(array):
        return pltpu.with_memory_space_constraint(array, pltpu.HBM)

    message, right_sides = call(
        part(open_kernel, rhs), [plain(1), panel], in_hbm(right_sides), far=(0,), fixed=(1,), scratch=[semaphore]
    )
    right = right_factors.reshape(slots * rank, width)
    other = swap(after(right, message), 1)
    named_shape = ((8, slots * rank), jnp.int32)
    nugget, left, here, named, near, sums = call(
        part(load_kernel, rhs, rank),
        [((1, width), F32), factor, factor, named_shape, row_block, small],
        right_sides, in_hbm(tile_column.reshape(slots)), live_slots, in_hbm(nugget[None, :]),
        in_hbm(left_factors.reshape(slots * rank, width)), in_hbm(right),
        far=(1, 3, 4, 5), scalars=(2,), fixed=(0, 1, 2), scratch=[pltpu.SMEM((slots,), jnp.int32)] + [semaphore] * 4,
    )
    other_named = swap(named, 1)

    def loading(mine):
        terms, places, turned = call(
            part(load_add_kernel, rhs, chunks, place_of, held),
            [two_rows, ((rhs, 2 * slots * rank), jnp.int32), ((width, 2 * slots * rank), BF16)],
            mine, near, named, other_named, here, other,
            fixed=(2,),
        )
        return terms, sums, turned, (here, other), places

    message, got, turned, factors, places = gather(message, loading, near)
    pair, earlier, weighted, *sends = call(
        part(first_kernel, rhs, chunks, go + stay),
        [small, two_rows, small] + sent,
        message, got, *factors, places,
    )
    mine, pair, got = reduce(sends, pair, earlier, left)
    message, residual, step, first_gram = call(
        part(middle_kernel, rhs, chunks),
        [coded(1), panel, small, small],
        right_sides, nugget, mine, pair, *got,
    )

    (solution,) = call(part(solution_kernel, rhs), [panel], step, right_sides)

    def loaded(mine):
        terms, sums, inverse = call(
            part(near_add_kernel, rhs, chunks, held),
            [two_rows, small, small],
            mine, residual, right_sides, nugget, left, named, places, turned, first_gram,
            micros=0.0,
        )
        return terms, sums, turned, (inverse,), places

    message, got, _, (inverse,), _ = gather(message, loaded)
    pair, projected, next_gram, mix, *sends = call(
        part(second_kernel, rhs, chunks, go + stay),
        [small, two_rows, small, small] + sent,
        message, got, *factors, places, inverse, weighted, earlier,
    )
    (direction,) = call(part(direction_kernel, rhs), [panel], mix, right_sides, residual)
    mine, pair, got = reduce(sends, pair, projected, left, direction, solution)
    return tuple(
        call(
            part(last_kernel, rhs, chunks),
            [panel, panel],
            direction, nugget, mine, pair, next_gram, residual, solution, *got,
        )
    )


def solution(mesh):
    return jax.shard_map(
        shards,
        mesh=mesh,
        in_specs=(
            P(None, ("groups", "row")),
            P(("groups", "row")),
            P(("groups", "row"), None, None),
            P(("groups", "row"), None, None),
            P(("groups", "row"), None),
            P(("groups", "row")),
        ),
        out_specs=(P(None, ("groups", "row")), P(None, ("groups", "row"))),
        check_vma=False,
    )
```

```python
import functools

import jax
import jax.numpy as jnp
from jax import lax
from jax.experimental import pallas as pl
from jax.experimental.pallas import tpu as pltpu
from jax.sharding import PartitionSpec as P

LANES = 128
F32 = jnp.float32
BF16 = jnp.bfloat16
EXACT = lax.Precision.HIGHEST
NN = (((1,), (0,)), ((), ()))
NT = (((1,), (1,)), ((), ()))


def lanes_of(block):
    return lax.broadcasted_iota(jnp.int32, block.shape, len(block.shape) - 1)


def sums_of(parts, rhs):
    rest = jnp.zeros((rhs, LANES - rhs * len(parts)), F32)
    return jnp.concatenate(parts + [rest], axis=1)


def encode(pair, rhs):
    high = pair.astype(BF16).astype(F32)
    rest = pair - high
    middle = rest.astype(BF16).astype(F32)
    low = rest - middle
    return (high + pltpu.roll(middle, 2 * rhs, 1) + pltpu.roll(low, 4 * rhs, 1)).astype(BF16)


def decode(code, rhs):
    total = code + pltpu.roll(code, LANES - 2 * rhs, 1) + pltpu.roll(code, LANES - 4 * rhs, 1)
    return jnp.where(lanes_of(total) < 2 * rhs, total, 0.0)


def second_of(pair, rhs):
    return pltpu.roll(pair, LANES - rhs, 1)


def right_divide(top, bottom, rhs):
    both = jnp.concatenate([top, bottom], axis=0)
    lane = lanes_of(both)
    both = jnp.where(lane < rhs, both, 0.0)
    one = lane[:1]
    for k in range(0, rhs, 4):
        cols = [jnp.broadcast_to(both[:, k + j : k + j + 1], both.shape) for j in range(4)]
        p = [[cols[j][k + i : k + i + 1] for j in range(4)] for i in range(4)]
        inside = (one >= k) & (one < k + 4)
        rows = [
            jnp.where(inside, jnp.where(one == k + i, -1.0, 0.0), both[k + i : k + i + 1]) for i in range(4)
        ]
        inverse = 1.0 / (p[0][0] * p[1][1] - p[0][1] * p[1][0])

        def upper(x, y):
            return (p[1][1] * x - p[0][1] * y) * inverse, (p[0][0] * y - p[1][0] * x) * inverse

        b_02, b_12 = upper(p[0][2], p[1][2])
        b_03, b_13 = upper(p[0][3], p[1][3])
        r_0, r_1 = upper(rows[0], rows[1])
        s_22 = p[2][2] - p[2][0] * b_02 - p[2][1] * b_12
        s_23 = p[2][3] - p[2][0] * b_03 - p[2][1] * b_13
        s_32 = p[3][2] - p[3][0] * b_02 - p[3][1] * b_12
        s_33 = p[3][3] - p[3][0] * b_03 - p[3][1] * b_13
        inverse_low = 1.0 / (s_22 * s_33 - s_23 * s_32)
        q_2 = rows[2] - p[2][0] * r_0 - p[2][1] * r_1
        q_3 = rows[3] - p[3][0] * r_0 - p[3][1] * r_1
        w_2 = (s_33 * q_2 - s_23 * q_3) * inverse_low
        w_3 = (s_22 * q_3 - s_32 * q_2) * inverse_low
        w_0 = r_0 - b_02 * w_2 - b_03 * w_3
        w_1 = r_1 - b_12 * w_2 - b_13 * w_3
        both = jnp.where((lane >= k) & (lane < k + 4), 0.0, both)
        both = both - cols[0] * w_0 - cols[1] * w_1 - cols[2] * w_2 - cols[3] * w_3
    return both[rhs:, :]


def left_multiply(square, block, rhs):
    return lax.dot_general(square[:, :rhs], block, NN, precision=EXACT, preferred_element_type=F32)


def gram(former, latter):
    return lax.dot_general(former, latter, NT, precision=EXACT, preferred_element_type=F32)


def split_gram(block, rhs):
    high = block.astype(BF16)
    low = (block - high.astype(F32)).astype(BF16)
    both = jnp.concatenate([high, low], axis=0)
    total = lax.dot_general(both, both, NT, preferred_element_type=F32)
    return total[:rhs, :rhs] + total[:rhs, rhs:] + total[rhs:, :rhs]


def rows_of(ref, chunks):
    panels, _, rhs, lanes = ref.shape
    return jnp.concatenate([ref[:, c].reshape(panels * rhs, lanes) for c in range(chunks)], axis=1)


def store_message(message_ref, block, rhs, at=0):
    for c in range(block.shape[1] // LANES):
        message_ref[at + c] = block[:, c * LANES : (c + 1) * LANES].astype(message_ref.dtype)


def far_terms(total, panels, turned_ref, places, bases, rhs, chunks):
    rows = jnp.concatenate([rows_of(ref, chunks) for ref in panels], axis=0)
    if rows.shape[0] * 2 == LANES:
        rows = jnp.concatenate([rows, rows], axis=0)
    far = lax.dot_general(rows, turned_ref[...], NN, preferred_element_type=F32)
    at = 0
    for base, ref in zip(bases, panels):
        for i in range(ref.shape[0]):
            total = total + jnp.where(places == base + i, far[at : at + rhs], 0.0)
            at += rhs
    return total


def codes_of(panels_ref, chunks):
    count, held = panels_ref.shape[:2]
    code = jnp.zeros(panels_ref.shape[2:], F32)
    for i in range(count if held > chunks else 0):
        code = code + panels_ref[i, chunks].astype(F32)
    return code


def spread_terms(projected, factors, places, wanted, store, rhs, chunks):
    masked = [jnp.where(places == place, projected, 0.0).astype(BF16) for place in wanted]
    masked = jnp.concatenate(masked, axis=0)
    width = factors[0].shape[0]
    step = 2 * LANES
    for block in range(chunks // 2):
        at = slice(block * step, (block + 1) * step)
        moved = sum(
            lax.dot_general(
                masked[:, i * width : (i + 1) * width], ref[:, at], NN, preferred_element_type=F32
            )
            for i, ref in enumerate(factors)
        )
        for i in range(len(wanted)):
            for b in range(2):
                piece = moved[i * rhs : (i + 1) * rhs, b * LANES : (b + 1) * LANES]
                store(i, 2 * block + b, piece)


def open_kernel(rhs, right_side_hbm, message_ref, right_side_ref, sem):
    copy = pltpu.make_async_copy(right_side_hbm, right_side_ref, sem)
    copy.start()
    copy.wait()
    store_message(message_ref, right_side_ref[...], rhs)


def load_kernel(
    rhs, rank, own_ref, column_hbm, live_ref, nugget_hbm, left_hbm, right_hbm,
    nugget_ref, left_ref, right_ref, named_ref, near_ref, sums_ref,
    column_ref, column_sem, nugget_sem, left_sem, right_sem,
):
    copies = [
        pltpu.make_async_copy(column_hbm, column_ref, column_sem),
        pltpu.make_async_copy(nugget_hbm, nugget_ref, nugget_sem),
        pltpu.make_async_copy(left_hbm, left_ref, left_sem),
        pltpu.make_async_copy(right_hbm, right_ref, right_sem),
    ]
    for copy in copies:
        copy.start()
    own = own_ref[...]
    for copy in copies[:2]:
        copy.wait()
    slot_of = lax.broadcasted_iota(jnp.int32, (1, named_ref.shape[1]), 1) // rank
    named = jnp.full(slot_of.shape, -1, jnp.int32)
    for s in range(column_ref.shape[0]):
        named = jnp.where(slot_of == s, jnp.where(s < live_ref[0], column_ref[s], -1), named)
    named_ref[...] = jnp.broadcast_to(named, named_ref.shape)
    sums_ref[...] = sums_of([gram(own * nugget_ref[...], own), gram(own, own)], rhs)
    copies[2].wait()
    near = lax.dot_general(own.astype(BF16), left_ref[...], NT, preferred_element_type=F32)
    near_ref[...] = jnp.where(named >= 0, near, 0.0)
    copies[3].wait()


def load_add_kernel(
    rhs, chunks, place_of, base, held_ref, near_ref, named_ref, other_named_ref, right_ref, other_ref,
    part_ref, places_ref, turned_ref,
):
    named = jnp.concatenate([named_ref[...], other_named_ref[...]], axis=1)
    offset = named ^ lax.axis_index("row")
    places = jnp.where((named >= 0) & ((offset & 1) == 0), place_of(offset), -1)
    places = jnp.concatenate([places] * (rhs // places.shape[0]), axis=0)
    places_ref[...] = places
    near = near_ref[...]
    total = jnp.concatenate([near, jnp.zeros(near.shape, F32)], axis=1)
    half = other_ref.shape[0]
    turned_ref[:, half:] = other_ref[...].T
    turned_ref[:, :half] = right_ref[...].T
    part_ref[...] = far_terms(total, [held_ref], turned_ref, places, [base], rhs, chunks)


def near_add_kernel(
    rhs, chunks, base, held_ref, own_ref, right_side_ref, nugget_ref, left_ref, named_ref, places_ref,
    turned_ref, gram_ref, part_ref, sums_ref, inverse_ref,
):
    row = lax.broadcasted_iota(jnp.int32, gram_ref.shape, 0)
    inverse_ref[...] = right_divide(gram_ref[...], jnp.where(row == lanes_of(row), 1.0, 0.0), rhs)
    own = own_ref[...]
    near = lax.dot_general(own.astype(BF16), left_ref[...], NT, preferred_element_type=F32)
    near = jnp.where(named_ref[:1] >= 0, near, 0.0)
    total = jnp.concatenate([near, jnp.zeros(near.shape, F32)], axis=1)
    part_ref[...] = far_terms(total, [held_ref], turned_ref, places_ref[...], [base], rhs, chunks)
    weighted = own * nugget_ref[...]
    code = codes_of(held_ref, chunks)
    none = jnp.zeros((rhs, rhs), F32)
    sums_ref[...] = decode(code, rhs) + sums_of([none, gram(weighted, own), gram(right_side_ref[...], weighted)], rhs)


def add_kernel(
    rhs, chunks, bases, turned_ref, places_ref, part_ref, sums_ref, *rest
):
    *panels, message_ref = rest
    total = far_terms(part_ref[...], panels, turned_ref, places_ref[...], bases, rhs, chunks)
    width = total.shape[1]
    message_ref[:, :width] = total
    message_ref[:, width:] = sums_ref[...] + decode(sum(codes_of(ref, chunks) for ref in panels), rhs)


def both_cores(message_ref, got_ref):
    half = (message_ref.shape[1] - LANES) // 2
    own = message_ref[:, :half] + got_ref[:, half : 2 * half]
    other = message_ref[:, half : 2 * half] + got_ref[:, :half]
    sums = message_ref[:, 2 * half :] + got_ref[:, 2 * half :]
    return jnp.concatenate([own, other], axis=1), sums


def rounded_gram(projected):
    rounded = projected.astype(BF16)
    return lax.dot_general(rounded, rounded, NT, preferred_element_type=F32)


def send_terms(outs, projected, factors, places, wanted, pair, rhs, chunks):
    slots = [(ref, i) for ref in outs for i in range(ref.shape[0] // chunks)]

    def store(i, c, piece):
        ref, j = slots[i]
        ref[j * chunks + c] = piece.astype(ref.dtype)

    spread_terms(projected, factors, places, wanted, store, rhs, chunks)
    code = encode(pair, rhs)
    for ref in outs:
        if ref.shape[0] % chunks:
            ref[ref.shape[0] - 1] = code


def first_kernel(
    rhs, chunks, wanted, message_ref, got_ref, right_ref, other_ref, places_ref,
    pair_ref, projected_ref, sums_ref, *sends,
):
    projected, sums = both_cores(message_ref, got_ref)
    projected_ref[...] = projected
    sums_ref[...] = sums
    pair = sums + sums_of([rounded_gram(projected)], rhs)
    pair_ref[...] = pair
    send_terms(sends, projected, (right_ref, other_ref), places_ref[...], wanted, pair, rhs, chunks)


def second_kernel(
    rhs, chunks, wanted, message_ref, got_ref, right_ref, other_ref, places_ref,
    inverse_ref, weighted_ref, earlier_ref,
    pair_ref, projected_ref, next_gram_ref, mix_ref, *sends,
):
    projected, sums = both_cores(message_ref, got_ref)
    next_gram_ref[...] = sums
    mix = left_multiply(sums, inverse_ref[...], rhs)
    projected = projected + left_multiply(mix, earlier_ref[...], rhs)
    projected_ref[...] = projected
    weighted = left_multiply(mix, jnp.concatenate([sums[:, 2 * rhs : 3 * rhs], weighted_ref[:, :rhs]], axis=1), rhs)
    mixed = weighted[:, :rhs]
    curvature = sums[:, rhs : 2 * rhs] + mixed + mixed.T + gram(weighted[:, rhs:], mix[:, :rhs])
    pair = sums_of([curvature + rounded_gram(projected)], rhs)
    pair_ref[...] = pair
    send_terms(sends, projected, (right_ref, other_ref), places_ref[...], wanted, pair, rhs, chunks)
    mix_ref[...] = mix


def solution_kernel(rhs, step_ref, right_side_ref, solution_ref):
    solution_ref[...] = left_multiply(step_ref[...], right_side_ref[...], rhs)


def direction_kernel(rhs, mix_ref, right_side_ref, residual_ref, direction_ref):
    direction_ref[...] = residual_ref[...] + left_multiply(mix_ref[...], right_side_ref[...], rhs)


def join_kernel(keep_ref, *rest):
    *got, sum_ref = rest
    total = keep_ref[...]
    for ref in got:
        total = total + ref[...].astype(F32)
    sum_ref[...] = total


def pass_kernel(rhs, keep_ref, *rest):
    *got, message_ref = rest
    size = keep_ref.shape[0]
    message_ref[:size] = (keep_ref[...] + sum(ref[:size].astype(F32) for ref in got)).astype(BF16)
    message_ref[size] = encode(decode(sum(ref[size].astype(F32) for ref in got), rhs), rhs)


def part_kernel(rhs, keep_ref, pair_ref, got_ref, total_ref, *sends):
    size = sends[0].shape[0] - 1
    total = pair_ref[...] + decode(got_ref[got_ref.shape[0] - 1].astype(F32), rhs)
    total_ref[...] = total
    code = encode(total, rhs)
    for i, send in enumerate(sends):
        at = i * size
        send[:size] = (keep_ref[at : at + size] + got_ref[at : at + size].astype(F32)).astype(BF16)
        send[size] = code


def own_kernel(rhs, chunks, projected_ref, left_ref, keep_ref, *rest):
    *_, sum_ref, total_ref = rest
    join_coded_kernel(rhs, keep_ref, *rest)
    own = projected_ref[:, : left_ref.shape[0]].astype(BF16)
    own = lax.dot_general(own, left_ref[...], NN, preferred_element_type=F32)
    for c in range(chunks):
        sum_ref[c] = sum_ref[c] + own[:, c * LANES : (c + 1) * LANES]


def join_coded_kernel(rhs, keep_ref, pair_ref, *rest):
    *got, sum_ref, total_ref = rest
    size = keep_ref.shape[0]
    total, code = keep_ref[...], jnp.zeros(pair_ref.shape, F32)
    for ref in got:
        total = total + ref[:size].astype(F32)
        code = code + ref[size].astype(F32)
    sum_ref[...] = total
    total_ref[...] = pair_ref[...] + decode(code, rhs)


def message_kernel(rhs, panel_ref, pair_ref, message_ref):
    message_ref[: panel_ref.shape[0]] = panel_ref[...].astype(BF16)
    message_ref[panel_ref.shape[0]] = encode(pair_ref[...], rhs)


def code_kernel(rhs, pair_ref, code_ref):
    code_ref[...] = encode(pair_ref[...], rhs)


def pair_kernel(rhs, pair_ref, got_ref, total_ref):
    total_ref[...] = pair_ref[...] + decode(got_ref[...].astype(F32), rhs)


def gathered_product(keep_ref, pair_ref, got, direction, nugget, rhs, chunks):
    total = keep_ref[...]
    code = jnp.zeros(pair_ref.shape, F32)
    for ref in got:
        total = total + ref[:chunks].astype(F32)
        code = code + ref[chunks].astype(F32)
    applied = nugget * direction + jnp.concatenate([total[c] for c in range(chunks)], axis=1)
    return applied, pair_ref[...] + decode(code, rhs)


def middle_kernel(
    rhs, chunks, direction_ref, nugget_ref, keep_ref, pair_ref, *rest
):
    *got, message_ref, residual_ref, step_ref, gram_ref = rest
    direction = direction_ref[...]
    applied, pair = gathered_product(keep_ref, pair_ref, got, direction, nugget_ref[...], rhs, chunks)
    first_gram = second_of(pair, rhs)
    gram_ref[...] = first_gram
    step = right_divide(pair, first_gram, rhs)
    residual = direction - left_multiply(step, applied, rhs)
    residual_ref[...] = residual
    store_message(message_ref, residual, rhs)
    message_ref[chunks] = encode(sums_of([split_gram(residual, rhs)], rhs), rhs)
    step_ref[...] = step


def last_kernel(
    rhs, chunks, direction_ref, nugget_ref, keep_ref, pair_ref, gram_ref, residual_ref, solution_ref, *rest
):
    *got, out_solution_ref, out_residual_ref = rest
    direction = direction_ref[...]
    applied, pair = gathered_product(keep_ref, pair_ref, got, direction, nugget_ref[...], rhs, chunks)
    step = right_divide(pair, gram_ref[...], rhs)
    out_solution_ref[...] = solution_ref[...] + left_multiply(step, direction, rhs)
    out_residual_ref[...] = residual_ref[...] - left_multiply(step, applied, rhs)


def call(kernel, outs, *args, far=(), scalars=(), fixed=(), scratch=(), micros=0.0):
    whole = pl.BlockSpec(memory_space=pltpu.VMEM)
    spaces = {i: pltpu.HBM for i in far} | {i: pltpu.SMEM for i in scalars}
    return pl.pallas_call(
        kernel,
        out_shape=[
            pltpu.VMEM(shape, dtype) if i in fixed else jax.ShapeDtypeStruct(shape, dtype)
            for i, (shape, dtype) in enumerate(outs)
        ],
        in_specs=[pl.BlockSpec(memory_space=spaces[i]) if i in spaces else whole for i in range(len(args))],
        out_specs=[whole] * len(outs),
        scratch_shapes=list(scratch),
        cost_estimate=pl.CostEstimate(flops=int(micros * 1e9), bytes_accessed=0, transcendentals=0),
        compiler_params=pltpu.CompilerParams(vmem_limit_bytes=32 * 1024 * 1024),
    )(*args)


def after(value, *others):
    return lax.optimization_barrier((value, *others))[0]


def shards(right_sides, nugget, left_factors, right_factors, tile_column, live_slots):
    devices = lax.axis_size("row")
    bits = devices.bit_length() - 1
    low_bits = bits - 2
    slots, rank, width = left_factors.shape
    rhs = right_sides.shape[0]
    chunks = width // LANES
    part = functools.partial

    def swap(array, offset):
        return lax.ppermute(array, "row", [(i, i ^ offset) for i in range(devices)])

    order = (0, 3, 2, 1)
    groups = []
    for k in order:
        group = [k << low_bits]
        for b in range(low_bits - 1, 1, -1):
            group = group + [o | (1 << b) for o in group]
        groups.append(group)
    m = len(groups[0])
    held_offsets = sum(groups, [])
    offsets = held_offsets + [o | 2 for o in held_offsets]
    held, late = 0, 4 * m

    def place_of(offset):
        place = ((4 - (offset >> low_bits)) & 3) * m
        for b in range(low_bits - 1, 1, -1):
            place = place + (((offset >> b) & 1) << (low_bits - 1 - b))
        return place + ((offset >> 1) & 1) * late

    assert [place_of(o) for o in offsets] == list(range(devices // 2))
    stay, go = tuple(range(late + m)), tuple(range(late + m, 2 * late))

    small = ((rhs, LANES), F32)
    panel = ((rhs, width), F32)
    row_block = ((rhs, slots * rank), F32)
    two_rows = ((rhs, 2 * slots * rank), F32)
    core_message = ((rhs, 2 * slots * rank + LANES), F32)
    factor = ((slots * rank, width), BF16)
    semaphore = pltpu.SemaphoreType.DMA

    def plain(count):
        return ((count * chunks, rhs, LANES), BF16)

    def coded(count):
        return ((count * chunks + 1, rhs, LANES), BF16)

    def kept(count):
        return ((count * chunks, rhs, LANES), F32)

    sent = [coded(m)] * 3 + ([kept(1)] * 2 + [coded(1)] * 2 if m == 1 else [kept(m)] + [plain(m)] * 3) + [kept(m)]

    def gather(message, first_terms, *early):
        if m == 1:
            far_3, far_2 = [swap(message, k << low_bits)[None] for k in order[1:3]]
            beside = swap(message[None], 2)
            far_1 = swap(message, order[3] << low_bits)[None]
            last = [
                swap(after(jnp.concatenate([far_3, far_2]), *early), 2),
                swap(beside, order[3] << low_bits),
            ]
            bases = (late, late + 1, late + 3)
            held_panels = jnp.concatenate([message[None], far_3, far_2, far_1])
        else:
            mine = [message[None]] + [swap(message, k << low_bits)[None] for k in order[1:]]
            for b in range(low_bits - 1, 1, -1):
                mine = [jnp.concatenate([g, swap(g, 1 << b)]) for g in mine]
            beside = swap(mine[0], 2)
            last = [swap(jnp.concatenate(mine[1:]), 2)]
            bases = (late, late + m)
            held_panels = jnp.concatenate(mine)
        terms, sums, turned, factors, places = first_terms(held_panels)
        last = [after(x, terms) for x in last]
        (message,) = call(
            part(add_kernel, rhs, chunks, bases), [core_message], turned, places, terms, sums, beside, *last
        )
        return message, swap(message, 1), turned, factors, places

    def reduce(sends, pair, projected, left, *early):
        sends, stays = sends[:3], sends[3:]
        if m == 1:
            got_side = swap(sends[0], 2)
            got_far = [swap(sends[i], order[i + 1] << low_bits) for i in (1, 2)]
            mine, keep, *sends, beside = stays
            got_here = [swap(sends[i - 1], order[i + 1] << low_bits) for i in (1, 2)]
            pair, send = call(part(part_kernel, rhs), [small, coded(1)], keep, pair, got_side)
            got_last = swap(send, order[1] << low_bits)
            (send,) = call(part(pass_kernel, rhs), [coded(1)], beside, *got_far)
            got_beside = swap(send, 2)
            join = part(join_coded_kernel, rhs)
            mine, pair = call(
                part(own_kernel, rhs, chunks), [kept(1), small],
                projected, left, after(mine, *early), pair, *got_here,
                micros=0.3,
            )
            mine, pair = call(join, [kept(1), small], mine, pair, got_last, micros=0.3)
            return mine, pair, [got_beside]
        got = [swap(x, k << low_bits) for x, k in zip(sends, order[1:])]
        keep, *sends, beside = stays
        got_here = [swap(x, k << low_bits) for x, k in zip(sends, order[1:])]
        turned, pair = call(part(join_coded_kernel, rhs), [kept(m), small], beside, pair, *got)
        (keep,) = call(join_kernel, [kept(m)], after(keep, *early), *got_here)
        for b in range(2, low_bits):
            (code,) = call(part(code_kernel, rhs), [((rhs, LANES), BF16)], pair)
            (pair,) = call(part(pair_kernel, rhs), [small], pair, swap(code, 1 << b))
            half = keep.shape[0] // 2
            keep, turned = [
                x[:half] + swap(x[half:].astype(BF16), 1 << b).astype(F32) for x in (keep, turned)
            ]
        (turned,) = call(part(message_kernel, rhs), [coded(1)], turned, pair)
        keep, pair = call(part(own_kernel, rhs, chunks), [kept(1), small], projected, left, keep, pair)
        return keep, pair, [swap(turned, 2)]

    def in_hbm(array):
        return pltpu.with_memory_space_constraint(array, pltpu.HBM)

    message, right_sides = call(
        part(open_kernel, rhs), [plain(1), panel], in_hbm(right_sides), far=(0,), fixed=(1,), scratch=[semaphore]
    )
    right = right_factors.reshape(slots * rank, width)
    other = swap(after(right, message), 1)
    named_shape = ((8, slots * rank), jnp.int32)
    nugget, left, here, named, near, sums = call(
        part(load_kernel, rhs, rank),
        [((1, width), F32), factor, factor, named_shape, row_block, small],
        right_sides, in_hbm(tile_column.reshape(slots)), live_slots, in_hbm(nugget[None, :]),
        in_hbm(left_factors.reshape(slots * rank, width)), in_hbm(right),
        far=(1, 3, 4, 5), scalars=(2,), fixed=(0, 1, 2), scratch=[pltpu.SMEM((slots,), jnp.int32)] + [semaphore] * 4,
    )
    other_named = swap(named, 1)

    def loading(mine):
        terms, places, turned = call(
            part(load_add_kernel, rhs, chunks, place_of, held),
            [two_rows, ((rhs, 2 * slots * rank), jnp.int32), ((width, 2 * slots * rank), BF16)],
            mine, near, named, other_named, here, other,
            fixed=(2,),
        )
        return terms, sums, turned, (here, other), places

    message, got, turned, factors, places = gather(message, loading, near)
    pair, earlier, weighted, *sends = call(
        part(first_kernel, rhs, chunks, go + stay),
        [small, two_rows, small] + sent,
        message, got, *factors, places,
    )
    mine, pair, got = reduce(sends, pair, earlier, left)
    message, residual, step, first_gram = call(
        part(middle_kernel, rhs, chunks),
        [coded(1), panel, small, small],
        right_sides, nugget, mine, pair, *got,
    )

    (solution,) = call(part(solution_kernel, rhs), [panel], step, right_sides)

    def loaded(mine):
        terms, sums, inverse = call(
            part(near_add_kernel, rhs, chunks, held),
            [two_rows, small, small],
            mine, residual, right_sides, nugget, left, named, places, turned, first_gram,
            micros=0.0,
        )
        return terms, sums, turned, (inverse,), places

    message, got, _, (inverse,), _ = gather(message, loaded)
    pair, projected, next_gram, mix, *sends = call(
        part(second_kernel, rhs, chunks, go + stay),
        [small, two_rows, small, small] + sent,
        message, got, *factors, places, inverse, weighted, earlier,
    )
    (direction,) = call(part(direction_kernel, rhs), [panel], mix, right_sides, residual)
    mine, pair, got = reduce(sends, pair, projected, left, direction, solution)
    return tuple(
        call(
            part(last_kernel, rhs, chunks),
            [panel, panel],
            direction, nugget, mine, pair, next_gram, residual, solution, *got,
        )
    )


def solution(mesh):
    return jax.shard_map(
        shards,
        mesh=mesh,
        in_specs=(
            P(None, ("groups", "row")),
            P(("groups", "row")),
            P(("groups", "row"), None, None),
            P(("groups", "row"), None, None),
            P(("groups", "row"), None),
            P(("groups", "row")),
        ),
        out_specs=(P(None, ("groups", "row")), P(None, ("groups", "row"))),
        check_vma=False,
    )
```

```python
import functools

import jax
import jax.numpy as jnp
from jax import lax
from jax.experimental import pallas as pl
from jax.experimental.pallas import tpu as pltpu
from jax.sharding import PartitionSpec as P

LANES = 128
F32 = jnp.float32
BF16 = jnp.bfloat16
EXACT = lax.Precision.HIGHEST
NN = (((1,), (0,)), ((), ()))
NT = (((1,), (1,)), ((), ()))


def lanes_of(block):
    return lax.broadcasted_iota(jnp.int32, block.shape, len(block.shape) - 1)


def sums_of(parts, rhs):
    rest = jnp.zeros((rhs, LANES - rhs * len(parts)), F32)
    return jnp.concatenate(parts + [rest], axis=1)


def encode(pair, rhs):
    high = pair.astype(BF16).astype(F32)
    rest = pair - high
    middle = rest.astype(BF16).astype(F32)
    low = rest - middle
    return (high + pltpu.roll(middle, 2 * rhs, 1) + pltpu.roll(low, 4 * rhs, 1)).astype(BF16)


def decode(code, rhs):
    total = code + pltpu.roll(code, LANES - 2 * rhs, 1) + pltpu.roll(code, LANES - 4 * rhs, 1)
    return jnp.where(lanes_of(total) < 2 * rhs, total, 0.0)


def second_of(pair, rhs):
    return pltpu.roll(pair, LANES - rhs, 1)


def right_divide(top, bottom, rhs):
    both = jnp.concatenate([top, bottom], axis=0)
    lane = lanes_of(both)
    both = jnp.where(lane < rhs, both, 0.0)
    one = lane[:1]
    for k in range(0, rhs, 4):
        cols = [jnp.broadcast_to(both[:, k + j : k + j + 1], both.shape) for j in range(4)]
        p = [[cols[j][k + i : k + i + 1] for j in range(4)] for i in range(4)]
        inside = (one >= k) & (one < k + 4)
        rows = [
            jnp.where(inside, jnp.where(one == k + i, -1.0, 0.0), both[k + i : k + i + 1]) for i in range(4)
        ]
        inverse = 1.0 / (p[0][0] * p[1][1] - p[0][1] * p[1][0])

        def upper(x, y):
            return (p[1][1] * x - p[0][1] * y) * inverse, (p[0][0] * y - p[1][0] * x) * inverse

        b_02, b_12 = upper(p[0][2], p[1][2])
        b_03, b_13 = upper(p[0][3], p[1][3])
        r_0, r_1 = upper(rows[0], rows[1])
        s_22 = p[2][2] - p[2][0] * b_02 - p[2][1] * b_12
        s_23 = p[2][3] - p[2][0] * b_03 - p[2][1] * b_13
        s_32 = p[3][2] - p[3][0] * b_02 - p[3][1] * b_12
        s_33 = p[3][3] - p[3][0] * b_03 - p[3][1] * b_13
        inverse_low = 1.0 / (s_22 * s_33 - s_23 * s_32)
        q_2 = rows[2] - p[2][0] * r_0 - p[2][1] * r_1
        q_3 = rows[3] - p[3][0] * r_0 - p[3][1] * r_1
        w_2 = (s_33 * q_2 - s_23 * q_3) * inverse_low
        w_3 = (s_22 * q_3 - s_32 * q_2) * inverse_low
        w_0 = r_0 - b_02 * w_2 - b_03 * w_3
        w_1 = r_1 - b_12 * w_2 - b_13 * w_3
        both = jnp.where((lane >= k) & (lane < k + 4), 0.0, both)
        both = both - cols[0] * w_0 - cols[1] * w_1 - cols[2] * w_2 - cols[3] * w_3
    return both[rhs:, :]


def left_multiply(square, block, rhs):
    return lax.dot_general(square[:, :rhs], block, NN, precision=EXACT, preferred_element_type=F32)


def gram(former, latter):
    return lax.dot_general(former, latter, NT, precision=EXACT, preferred_element_type=F32)


def split_gram(block, rhs):
    high = block.astype(BF16)
    low = (block - high.astype(F32)).astype(BF16)
    both = jnp.concatenate([high, low], axis=0)
    total = lax.dot_general(both, both, NT, preferred_element_type=F32)
    return total[:rhs, :rhs] + total[:rhs, rhs:] + total[rhs:, :rhs]


def rows_of(ref, chunks):
    panels, _, rhs, lanes = ref.shape
    return jnp.concatenate([ref[:, c].reshape(panels * rhs, lanes) for c in range(chunks)], axis=1)


def store_message(message_ref, block, rhs, at=0):
    for c in range(block.shape[1] // LANES):
        message_ref[at + c] = block[:, c * LANES : (c + 1) * LANES].astype(message_ref.dtype)


def far_terms(total, panels, turned_ref, places, bases, rhs, chunks):
    rows = jnp.concatenate([rows_of(ref, chunks) for ref in panels], axis=0)
    if rows.shape[0] * 2 == LANES:
        rows = jnp.concatenate([rows, rows], axis=0)
    far = lax.dot_general(rows, turned_ref[...], NN, preferred_element_type=F32)
    at = 0
    for base, ref in zip(bases, panels):
        for i in range(ref.shape[0]):
            total = total + jnp.where(places == base + i, far[at : at + rhs], 0.0)
            at += rhs
    return total


def codes_of(panels_ref, chunks):
    count, held = panels_ref.shape[:2]
    code = jnp.zeros(panels_ref.shape[2:], F32)
    for i in range(count if held > chunks else 0):
        code = code + panels_ref[i, chunks].astype(F32)
    return code


def spread_terms(projected, factors, places, wanted, store, rhs, chunks):
    masked = [jnp.where(places == place, projected, 0.0).astype(BF16) for place in wanted]
    masked = jnp.concatenate(masked, axis=0)
    width = factors[0].shape[0]
    step = 2 * LANES
    for block in range(chunks // 2):
        at = slice(block * step, (block + 1) * step)
        moved = sum(
            lax.dot_general(
                masked[:, i * width : (i + 1) * width], ref[:, at], NN, preferred_element_type=F32
            )
            for i, ref in enumerate(factors)
        )
        for i in range(len(wanted)):
            for b in range(2):
                piece = moved[i * rhs : (i + 1) * rhs, b * LANES : (b + 1) * LANES]
                store(i, 2 * block + b, piece)


def open_kernel(rhs, right_side_hbm, message_ref, right_side_ref, sem):
    copy = pltpu.make_async_copy(right_side_hbm, right_side_ref, sem)
    copy.start()
    copy.wait()
    store_message(message_ref, right_side_ref[...], rhs)


def load_kernel(
    rhs, rank, own_ref, column_hbm, live_ref, nugget_hbm, left_hbm, right_hbm,
    nugget_ref, left_ref, right_ref, named_ref, near_ref, sums_ref,
    column_ref, column_sem, nugget_sem, left_sem, right_sem,
):
    copies = [
        pltpu.make_async_copy(column_hbm, column_ref, column_sem),
        pltpu.make_async_copy(nugget_hbm, nugget_ref, nugget_sem),
        pltpu.make_async_copy(left_hbm, left_ref, left_sem),
        pltpu.make_async_copy(right_hbm, right_ref, right_sem),
    ]
    for copy in copies:
        copy.start()
    own = own_ref[...]
    for copy in copies[:2]:
        copy.wait()
    slot_of = lax.broadcasted_iota(jnp.int32, (1, named_ref.shape[1]), 1) // rank
    named = jnp.full(slot_of.shape, -1, jnp.int32)
    for s in range(column_ref.shape[0]):
        named = jnp.where(slot_of == s, jnp.where(s < live_ref[0], column_ref[s], -1), named)
    named_ref[...] = jnp.broadcast_to(named, named_ref.shape)
    sums_ref[...] = sums_of([gram(own * nugget_ref[...], own), gram(own, own)], rhs)
    copies[2].wait()
    near = lax.dot_general(own.astype(BF16), left_ref[...], NT, preferred_element_type=F32)
    near_ref[...] = jnp.where(named >= 0, near, 0.0)
    copies[3].wait()


def load_add_kernel(
    rhs, chunks, place_of, base, held_ref, near_ref, named_ref, other_named_ref, right_ref, other_ref,
    part_ref, places_ref, turned_ref,
):
    named = jnp.concatenate([named_ref[...], other_named_ref[...]], axis=1)
    offset = named ^ lax.axis_index("row")
    places = jnp.where((named >= 0) & ((offset & 1) == 0), place_of(offset), -1)
    places = jnp.concatenate([places] * (rhs // places.shape[0]), axis=0)
    places_ref[...] = places
    near = near_ref[...]
    total = jnp.concatenate([near, jnp.zeros(near.shape, F32)], axis=1)
    half = other_ref.shape[0]
    turned_ref[:, half:] = other_ref[...].T
    turned_ref[:, :half] = right_ref[...].T
    part_ref[...] = far_terms(total, [held_ref], turned_ref, places, [base], rhs, chunks)


def near_add_kernel(
    rhs, chunks, base, held_ref, own_ref, right_side_ref, nugget_ref, left_ref, named_ref, places_ref,
    turned_ref, gram_ref, part_ref, sums_ref, inverse_ref,
):
    row = lax.broadcasted_iota(jnp.int32, gram_ref.shape, 0)
    inverse_ref[...] = right_divide(gram_ref[...], jnp.where(row == lanes_of(row), 1.0, 0.0), rhs)
    own = own_ref[...]
    near = lax.dot_general(own.astype(BF16), left_ref[...], NT, preferred_element_type=F32)
    near = jnp.where(named_ref[:1] >= 0, near, 0.0)
    total = jnp.concatenate([near, jnp.zeros(near.shape, F32)], axis=1)
    part_ref[...] = far_terms(total, [held_ref], turned_ref, places_ref[...], [base], rhs, chunks)
    weighted = own * nugget_ref[...]
    code = codes_of(held_ref, chunks)
    none = jnp.zeros((rhs, rhs), F32)
    sums_ref[...] = decode(code, rhs) + sums_of([none, gram(weighted, own), gram(right_side_ref[...], weighted)], rhs)


def add_kernel(
    rhs, chunks, bases, turned_ref, places_ref, part_ref, sums_ref, *rest
):
    *panels, message_ref = rest
    total = far_terms(part_ref[...], panels, turned_ref, places_ref[...], bases, rhs, chunks)
    width = total.shape[1]
    message_ref[:, :width] = total
    message_ref[:, width:] = sums_ref[...] + decode(sum(codes_of(ref, chunks) for ref in panels), rhs)


def both_cores(message_ref, got_ref):
    half = (message_ref.shape[1] - LANES) // 2
    own = message_ref[:, :half] + got_ref[:, half : 2 * half]
    other = message_ref[:, half : 2 * half] + got_ref[:, :half]
    sums = message_ref[:, 2 * half :] + got_ref[:, 2 * half :]
    return jnp.concatenate([own, other], axis=1), sums


def rounded_gram(projected):
    rounded = projected.astype(BF16)
    return lax.dot_general(rounded, rounded, NT, preferred_element_type=F32)


def send_terms(outs, projected, factors, places, wanted, pair, rhs, chunks):
    slots = [(ref, i) for ref in outs for i in range(ref.shape[0] // chunks)]

    def store(i, c, piece):
        ref, j = slots[i]
        ref[j * chunks + c] = piece.astype(ref.dtype)

    spread_terms(projected, factors, places, wanted, store, rhs, chunks)
    code = encode(pair, rhs)
    for ref in outs:
        if ref.shape[0] % chunks:
            ref[ref.shape[0] - 1] = code


def first_kernel(
    rhs, chunks, wanted, message_ref, got_ref, right_ref, other_ref, places_ref,
    pair_ref, projected_ref, sums_ref, *sends,
):
    projected, sums = both_cores(message_ref, got_ref)
    projected_ref[...] = projected
    sums_ref[...] = sums
    pair = sums + sums_of([rounded_gram(projected)], rhs)
    pair_ref[...] = pair
    send_terms(sends, projected, (right_ref, other_ref), places_ref[...], wanted, pair, rhs, chunks)


def second_kernel(
    rhs, chunks, wanted, message_ref, got_ref, right_ref, other_ref, places_ref,
    inverse_ref, weighted_ref, earlier_ref,
    pair_ref, projected_ref, next_gram_ref, mix_ref, *sends,
):
    projected, sums = both_cores(message_ref, got_ref)
    next_gram_ref[...] = sums
    mix = left_multiply(sums, inverse_ref[...], rhs)
    projected = projected + left_multiply(mix, earlier_ref[...], rhs)
    projected_ref[...] = projected
    weighted = left_multiply(mix, jnp.concatenate([sums[:, 2 * rhs : 3 * rhs], weighted_ref[:, :rhs]], axis=1), rhs)
    mixed = weighted[:, :rhs]
    curvature = sums[:, rhs : 2 * rhs] + mixed + mixed.T + gram(weighted[:, rhs:], mix[:, :rhs])
    pair = sums_of([curvature + rounded_gram(projected)], rhs)
    pair_ref[...] = pair
    send_terms(sends, projected, (right_ref, other_ref), places_ref[...], wanted, pair, rhs, chunks)
    mix_ref[...] = mix


def solution_kernel(rhs, step_ref, right_side_ref, solution_ref):
    solution_ref[...] = left_multiply(step_ref[...], right_side_ref[...], rhs)


def direction_kernel(rhs, mix_ref, right_side_ref, residual_ref, direction_ref):
    direction_ref[...] = residual_ref[...] + left_multiply(mix_ref[...], right_side_ref[...], rhs)


def join_kernel(keep_ref, *rest):
    *got, sum_ref = rest
    total = keep_ref[...]
    for ref in got:
        total = total + ref[...].astype(F32)
    sum_ref[...] = total


def pass_kernel(rhs, keep_ref, *rest):
    *got, message_ref = rest
    size = keep_ref.shape[0]
    message_ref[:size] = (keep_ref[...] + sum(ref[:size].astype(F32) for ref in got)).astype(BF16)
    message_ref[size] = encode(decode(sum(ref[size].astype(F32) for ref in got), rhs), rhs)


def part_kernel(rhs, keep_ref, pair_ref, got_ref, total_ref, *sends):
    size = sends[0].shape[0] - 1
    total = pair_ref[...] + decode(got_ref[got_ref.shape[0] - 1].astype(F32), rhs)
    total_ref[...] = total
    code = encode(total, rhs)
    for i, send in enumerate(sends):
        at = i * size
        send[:size] = (keep_ref[at : at + size] + got_ref[at : at + size].astype(F32)).astype(BF16)
        send[size] = code


def own_kernel(rhs, chunks, projected_ref, left_ref, keep_ref, *rest):
    *_, sum_ref, total_ref = rest
    join_coded_kernel(rhs, keep_ref, *rest)
    own = projected_ref[:, : left_ref.shape[0]].astype(BF16)
    own = lax.dot_general(own, left_ref[...], NN, preferred_element_type=F32)
    for c in range(chunks):
        sum_ref[c] = sum_ref[c] + own[:, c * LANES : (c + 1) * LANES]


def join_coded_kernel(rhs, keep_ref, pair_ref, *rest):
    *got, sum_ref, total_ref = rest
    size = keep_ref.shape[0]
    total, code = keep_ref[...], jnp.zeros(pair_ref.shape, F32)
    for ref in got:
        total = total + ref[:size].astype(F32)
        code = code + ref[size].astype(F32)
    sum_ref[...] = total
    total_ref[...] = pair_ref[...] + decode(code, rhs)


def message_kernel(rhs, panel_ref, pair_ref, message_ref):
    message_ref[: panel_ref.shape[0]] = panel_ref[...].astype(BF16)
    message_ref[panel_ref.shape[0]] = encode(pair_ref[...], rhs)


def code_kernel(rhs, pair_ref, code_ref):
    code_ref[...] = encode(pair_ref[...], rhs)


def pair_kernel(rhs, pair_ref, got_ref, total_ref):
    total_ref[...] = pair_ref[...] + decode(got_ref[...].astype(F32), rhs)


def gathered_product(keep_ref, pair_ref, got, direction, nugget, rhs, chunks):
    total = keep_ref[...]
    code = jnp.zeros(pair_ref.shape, F32)
    for ref in got:
        total = total + ref[:chunks].astype(F32)
        code = code + ref[chunks].astype(F32)
    applied = nugget * direction + jnp.concatenate([total[c] for c in range(chunks)], axis=1)
    return applied, pair_ref[...] + decode(code, rhs)


def middle_kernel(
    rhs, chunks, direction_ref, nugget_ref, keep_ref, pair_ref, *rest
):
    *got, message_ref, residual_ref, step_ref, gram_ref = rest
    direction = direction_ref[...]
    applied, pair = gathered_product(keep_ref, pair_ref, got, direction, nugget_ref[...], rhs, chunks)
    first_gram = second_of(pair, rhs)
    gram_ref[...] = first_gram
    step = right_divide(pair, first_gram, rhs)
    residual = direction - left_multiply(step, applied, rhs)
    residual_ref[...] = residual
    store_message(message_ref, residual, rhs)
    message_ref[chunks] = encode(sums_of([split_gram(residual, rhs)], rhs), rhs)
    step_ref[...] = step


def last_kernel(
    rhs, chunks, direction_ref, nugget_ref, keep_ref, pair_ref, gram_ref, residual_ref, solution_ref, *rest
):
    *got, out_solution_ref, out_residual_ref = rest
    direction = direction_ref[...]
    applied, pair = gathered_product(keep_ref, pair_ref, got, direction, nugget_ref[...], rhs, chunks)
    step = right_divide(pair, gram_ref[...], rhs)
    width = direction.shape[1]
    update = left_multiply(step, jnp.concatenate([direction, applied], axis=1), rhs)
    out_solution_ref[...] = solution_ref[...] + update[:, :width]
    out_residual_ref[...] = residual_ref[...] - update[:, width:]


def call(kernel, outs, *args, far=(), scalars=(), fixed=(), scratch=(), micros=0.0):
    whole = pl.BlockSpec(memory_space=pltpu.VMEM)
    spaces = {i: pltpu.HBM for i in far} | {i: pltpu.SMEM for i in scalars}
    return pl.pallas_call(
        kernel,
        out_shape=[
            pltpu.VMEM(shape, dtype) if i in fixed else jax.ShapeDtypeStruct(shape, dtype)
            for i, (shape, dtype) in enumerate(outs)
        ],
        in_specs=[pl.BlockSpec(memory_space=spaces[i]) if i in spaces else whole for i in range(len(args))],
        out_specs=[whole] * len(outs),
        scratch_shapes=list(scratch),
        cost_estimate=pl.CostEstimate(flops=int(micros * 1e9), bytes_accessed=0, transcendentals=0),
        compiler_params=pltpu.CompilerParams(vmem_limit_bytes=32 * 1024 * 1024),
    )(*args)


def after(value, *others):
    return lax.optimization_barrier((value, *others))[0]


def shards(right_sides, nugget, left_factors, right_factors, tile_column, live_slots):
    devices = lax.axis_size("row")
    bits = devices.bit_length() - 1
    low_bits = bits - 2
    slots, rank, width = left_factors.shape
    rhs = right_sides.shape[0]
    chunks = width // LANES
    part = functools.partial

    def swap(array, offset):
        return lax.ppermute(array, "row", [(i, i ^ offset) for i in range(devices)])

    order = (0, 3, 2, 1)
    groups = []
    for k in order:
        group = [k << low_bits]
        for b in range(low_bits - 1, 1, -1):
            group = group + [o | (1 << b) for o in group]
        groups.append(group)
    m = len(groups[0])
    held_offsets = sum(groups, [])
    offsets = held_offsets + [o | 2 for o in held_offsets]
    held, late = 0, 4 * m

    def place_of(offset):
        place = ((4 - (offset >> low_bits)) & 3) * m
        for b in range(low_bits - 1, 1, -1):
            place = place + (((offset >> b) & 1) << (low_bits - 1 - b))
        return place + ((offset >> 1) & 1) * late

    assert [place_of(o) for o in offsets] == list(range(devices // 2))
    stay, go = tuple(range(late + m)), tuple(range(late + m, 2 * late))

    small = ((rhs, LANES), F32)
    panel = ((rhs, width), F32)
    row_block = ((rhs, slots * rank), F32)
    two_rows = ((rhs, 2 * slots * rank), F32)
    core_message = ((rhs, 2 * slots * rank + LANES), F32)
    factor = ((slots * rank, width), BF16)
    semaphore = pltpu.SemaphoreType.DMA

    def plain(count):
        return ((count * chunks, rhs, LANES), BF16)

    def coded(count):
        return ((count * chunks + 1, rhs, LANES), BF16)

    def kept(count):
        return ((count * chunks, rhs, LANES), F32)

    sent = [coded(m)] * 3 + ([kept(1)] * 2 + [coded(1)] * 2 if m == 1 else [kept(m)] + [plain(m)] * 3) + [kept(m)]

    def gather(message, first_terms, *early):
        if m == 1:
            far_3, far_2 = [swap(message, k << low_bits)[None] for k in order[1:3]]
            beside = swap(message[None], 2)
            far_1 = swap(message, order[3] << low_bits)[None]
            last = [
                swap(after(jnp.concatenate([far_3, far_2]), *early), 2),
                swap(beside, order[3] << low_bits),
            ]
            bases = (late, late + 1, late + 3)
            held_panels = jnp.concatenate([message[None], far_3, far_2, far_1])
        else:
            mine = [message[None]] + [swap(message, k << low_bits)[None] for k in order[1:]]
            for b in range(low_bits - 1, 1, -1):
                mine = [jnp.concatenate([g, swap(g, 1 << b)]) for g in mine]
            beside = swap(mine[0], 2)
            last = [swap(jnp.concatenate(mine[1:]), 2)]
            bases = (late, late + m)
            held_panels = jnp.concatenate(mine)
        terms, sums, turned, factors, places = first_terms(held_panels)
        last = [after(x, terms) for x in last]
        (message,) = call(
            part(add_kernel, rhs, chunks, bases), [core_message], turned, places, terms, sums, beside, *last
        )
        return message, swap(message, 1), turned, factors, places

    def reduce(sends, pair, projected, left, *early):
        sends, stays = sends[:3], sends[3:]
        if m == 1:
            got_side = swap(sends[0], 2)
            got_far = [swap(sends[i], order[i + 1] << low_bits) for i in (1, 2)]
            mine, keep, *sends, beside = stays
            got_here = [swap(sends[i - 1], order[i + 1] << low_bits) for i in (1, 2)]
            pair, send = call(part(part_kernel, rhs), [small, coded(1)], keep, pair, got_side)
            got_last = swap(send, order[1] << low_bits)
            (send,) = call(part(pass_kernel, rhs), [coded(1)], beside, *got_far)
            got_beside = swap(send, 2)
            join = part(join_coded_kernel, rhs)
            mine, pair = call(
                part(own_kernel, rhs, chunks), [kept(1), small],
                projected, left, after(mine, *early), pair, *got_here,
                micros=0.3,
            )
            mine, pair = call(join, [kept(1), small], mine, pair, got_last, micros=0.3)
            return mine, pair, [got_beside]
        got = [swap(x, k << low_bits) for x, k in zip(sends, order[1:])]
        keep, *sends, beside = stays
        got_here = [swap(x, k << low_bits) for x, k in zip(sends, order[1:])]
        turned, pair = call(part(join_coded_kernel, rhs), [kept(m), small], beside, pair, *got)
        (keep,) = call(join_kernel, [kept(m)], after(keep, *early), *got_here)
        for b in range(2, low_bits):
            (code,) = call(part(code_kernel, rhs), [((rhs, LANES), BF16)], pair)
            (pair,) = call(part(pair_kernel, rhs), [small], pair, swap(code, 1 << b))
            half = keep.shape[0] // 2
            keep, turned = [
                x[:half] + swap(x[half:].astype(BF16), 1 << b).astype(F32) for x in (keep, turned)
            ]
        (turned,) = call(part(message_kernel, rhs), [coded(1)], turned, pair)
        keep, pair = call(part(own_kernel, rhs, chunks), [kept(1), small], projected, left, keep, pair)
        return keep, pair, [swap(turned, 2)]

    def in_hbm(array):
        return pltpu.with_memory_space_constraint(array, pltpu.HBM)

    message, right_sides = call(
        part(open_kernel, rhs), [plain(1), panel], in_hbm(right_sides), far=(0,), fixed=(1,), scratch=[semaphore]
    )
    right = right_factors.reshape(slots * rank, width)
    other = swap(after(right, message), 1)
    named_shape = ((8, slots * rank), jnp.int32)
    nugget, left, here, named, near, sums = call(
        part(load_kernel, rhs, rank),
        [((1, width), F32), factor, factor, named_shape, row_block, small],
        right_sides, in_hbm(tile_column.reshape(slots)), live_slots, in_hbm(nugget[None, :]),
        in_hbm(left_factors.reshape(slots * rank, width)), in_hbm(right),
        far=(1, 3, 4, 5), scalars=(2,), fixed=(0, 1, 2), scratch=[pltpu.SMEM((slots,), jnp.int32)] + [semaphore] * 4,
    )
    other_named = swap(named, 1)

    def loading(mine):
        terms, places, turned = call(
            part(load_add_kernel, rhs, chunks, place_of, held),
            [two_rows, ((rhs, 2 * slots * rank), jnp.int32), ((width, 2 * slots * rank), BF16)],
            mine, near, named, other_named, here, other,
            fixed=(2,),
        )
        return terms, sums, turned, (here, other), places

    message, got, turned, factors, places = gather(message, loading, near)
    pair, earlier, weighted, *sends = call(
        part(first_kernel, rhs, chunks, go + stay),
        [small, two_rows, small] + sent,
        message, got, *factors, places,
    )
    mine, pair, got = reduce(sends, pair, earlier, left)
    message, residual, step, first_gram = call(
        part(middle_kernel, rhs, chunks),
        [coded(1), panel, small, small],
        right_sides, nugget, mine, pair, *got,
    )

    (solution,) = call(part(solution_kernel, rhs), [panel], step, right_sides)

    def loaded(mine):
        terms, sums, inverse = call(
            part(near_add_kernel, rhs, chunks, held),
            [two_rows, small, small],
            mine, residual, right_sides, nugget, left, named, places, turned, first_gram,
            micros=0.0,
        )
        return terms, sums, turned, (inverse,), places

    message, got, _, (inverse,), _ = gather(message, loaded)
    pair, projected, next_gram, mix, *sends = call(
        part(second_kernel, rhs, chunks, go + stay),
        [small, two_rows, small, small] + sent,
        message, got, *factors, places, inverse, weighted, earlier,
    )
    (direction,) = call(part(direction_kernel, rhs), [panel], mix, right_sides, residual)
    mine, pair, got = reduce(sends, pair, projected, left, direction, solution)
    return tuple(
        call(
            part(last_kernel, rhs, chunks),
            [panel, panel],
            direction, nugget, mine, pair, next_gram, residual, solution, *got,
        )
    )


def solution(mesh):
    return jax.shard_map(
        shards,
        mesh=mesh,
        in_specs=(
            P(None, ("groups", "row")),
            P(("groups", "row")),
            P(("groups", "row"), None, None),
            P(("groups", "row"), None, None),
            P(("groups", "row"), None),
            P(("groups", "row")),
        ),
        out_specs=(P(None, ("groups", "row")), P(None, ("groups", "row"))),
        check_vma=False,
    )
```
